32 devices in a mesh: dp: 8 (over z, y), ctx: 4 (over x, core).
Axes of the slice: x: 2, y: 2, z: 4, core: 2. Of those that a mesh axis runs over, the one named last changes fastest.
Arguments:
- state_input: bfloat16 [8192, 4096], P(('dp', 'ctx')), may hold values from -6 to 6
- gate_values: bfloat16 [8192, 4096], P(('dp', 'ctx')), may hold values from -6 to 6
- input_matrix: bfloat16 [8192, 512], P(('dp', 'ctx')), may hold values from -1.2 to 1.2
- readout_matrix: bfloat16 [8192, 512], P(('dp', 'ctx')), may hold values from -1.1953125 to 1.1953125
- step_unbiased: float32 [8192, 64], P(('dp', 'ctx')), may hold values from -3 to 1280
- step_bias: float32 [64], replicated, may hold values from -1 to 0.5
- decay_rate_log: float32 [64], replicated
- skip_coefficients: float32 [64], replicated, may hold values from 3 to 10
- norm_gain: float32 [4096], replicated, may hold values from 0.1 to 8
- adapter_down: bfloat16 [64, 4096], replicated, may hold values from -0.09375 to 0.09375
- adapter_up: bfloat16 [64, 2048], replicated, may hold values from -0.75 to 0.75
- projection_weight: bfloat16 [2048, 4096], P(('dp', 'ctx')), may hold values from -0.09375 to 0.09375
- output_cotangent: bfloat16 [8192, 2048], P(('dp', 'ctx')), may hold values from -30 to 30
Outputs:
- input_gradient: bfloat16 [8192, 4096], P(('dp', 'ctx'))
- adapter_down_gradient: float32 [64, 4096], P(None, ('dp', 'ctx'))
- adapter_up_gradient: float32 [64, 2048], P(None, ('dp', 'ctx'))
The draws below stay inside these ranges and needn't reach their ends.
All inputs are finite; a program needn't handle non-finite values.
Results may differ from the reference program's by a relative error of at most 0.009.
Values may be sent and summed in bfloat16 or wider, within the bound.
No kernel may reach another device: no remote copies, remote signals or barrier semaphores. Data moves between devices by JAX's collectives and lax.ppermute only.
A program may use at most 192 MiB of HBM per device.

```python
import math
import jax
import jax.numpy as jnp
from jax import lax

H = 64
P_SIZE = 64
N = 128
G = 4
OUTPUT_FEATURES = 2048
ADAPTER_RANK = 64
Q = 256
INNER_CHANNELS = 4096
SEQUENCE_LENGTH = 1024
TOTAL_ROWS = 8192
N_DP = 8


def spike_mask(key):
    spike_picks = jax.random.randint(jax.random.fold_in(key, 101), (N_DP, 2), 0, SEQUENCE_LENGTH)
    location_list = jnp.arange(SEQUENCE_LENGTH, dtype=jnp.int32)
    spike_hits = jnp.any(location_list[None, :, None] == spike_picks[:, None, :], axis=2)
    return spike_hits.reshape(N_DP * SEQUENCE_LENGTH)


def draw_step_unbiased(key, part):
    spike_hits = spike_mask(key)
    frozen_values = jnp.clip(0.8 * jax.random.normal(jax.random.fold_in(key, 1), (TOTAL_ROWS, H), jnp.float32), -3.0, 3.0)
    return jnp.where(spike_hits[:, None], jnp.float32(1.25 * SEQUENCE_LENGTH), frozen_values)


def draw_input_matrix(key, part):
    spike_hits = spike_mask(key)
    raw_values = jnp.clip(0.3 * jax.random.normal(jax.random.fold_in(key, 2), (TOTAL_ROWS, G * N), jnp.float32), -1.1875, 1.1875)
    clip_factor = jnp.where(spike_hits, jnp.float32(1.0 / (1.25 * SEQUENCE_LENGTH)), jnp.float32(1.0))
    return (raw_values * clip_factor[:, None]).astype(jnp.bfloat16)


def draw_decay_rate_log(key, part):
    head_ranks = jax.random.permutation(jax.random.fold_in(key, 3), H)
    rank_share = head_ranks.astype(jnp.float32) / H
    rate_pick = jax.random.uniform(jax.random.fold_in(key, 4), (H,), jnp.float32)
    slow_rates = jnp.exp(math.log(0.18) + rate_pick * (math.log(0.55) - math.log(0.18))) / SEQUENCE_LENGTH
    middle = jnp.exp(math.log(1.0 / 256) + rate_pick * (math.log(1.0 / 64) - math.log(1.0 / 256)))
    fast_rates = 1.0 / 45 + rate_pick * (1.0 / 22 - 1.0 / 45)
    head_rates = jnp.where(rank_share < 0.5, slow_rates, jnp.where(rank_share < 0.75, middle, fast_rates))
    return jnp.log(head_rates).astype(jnp.float32)


def draw_norm_gain(key, part):
    column_ramp = 0.5 + 1.5 * jnp.arange(INNER_CHANNELS, dtype=jnp.float32) / INNER_CHANNELS
    spread = jnp.exp(jax.random.uniform(jax.random.fold_in(key, 5), (INNER_CHANNELS,), jnp.float32, math.log(0.3), math.log(3.0)))
    return (column_ramp * spread).astype(jnp.float32)


def draw_output_cotangent(key, part):
    column_ramp = 0.5 + 1.5 * jnp.arange(OUTPUT_FEATURES, dtype=jnp.float32) / OUTPUT_FEATURES
    column_scale = column_ramp * jnp.exp(jax.random.uniform(jax.random.fold_in(key, 6), (OUTPUT_FEATURES,), jnp.float32, math.log(0.4), math.log(2.5)))
    body_values = jnp.clip(jax.random.normal(jax.random.fold_in(key, 8), (TOTAL_ROWS, OUTPUT_FEATURES), jnp.float32), -4.0, 4.0)
    return (body_values * column_scale[None, :]).astype(jnp.bfloat16)


def block_scale(own_key, dims, cuts, smallest, top_value):
    def one(dim, shards_of):
        draws = jax.random.uniform(jax.random.fold_in(jax.random.fold_in(own_key, 6), dim), (shards_of,), jnp.float32, smallest / len(cuts), top_value / len(cuts))
        return jnp.repeat(jnp.exp(draws), dims[dim] // shards_of).reshape((-1,) + (1,) * (len(dims) - dim - 1))

    level = one(*cuts[0])
    for cut in cuts[1:]:
        level = level * one(*cut)
    return level


def noise(own_key, dims, deviation, most, cuts=(), held_as=jnp.bfloat16):
    factor_of = block_scale(own_key, dims, cuts, -0.22, 0.18) if cuts else 1.0
    array = jax.random.normal(own_key, dims, jnp.float32) * deviation * factor_of
    return jnp.minimum(jnp.maximum(array, -most), most).astype(held_as)


def setup_inputs(seed: int = 0) -> dict:
    key_list = jax.random.split(jax.random.key(seed), 14)
    return {
        "state_input": noise(key_list[0], (TOTAL_ROWS, INNER_CHANNELS), 1.0, 6.0, ((0, 32),)),
        "gate_values": noise(key_list[1], (TOTAL_ROWS, INNER_CHANNELS), 1.0, 6.0, ((0, 32),)),
        "input_matrix": draw_input_matrix(jax.random.fold_in(key_list[13], 71), 0),
        "readout_matrix": noise(key_list[3], (TOTAL_ROWS, G * N), 0.3, 1.1953125, ((0, 32),)),
        "step_unbiased": draw_step_unbiased(jax.random.fold_in(key_list[13], 71), 0),
        "step_bias": jnp.clip(jax.random.uniform(key_list[5], (H,), jnp.float32, -1.0, 0.5), -1.0, 0.5),
        "decay_rate_log": draw_decay_rate_log(jax.random.fold_in(key_list[13], 71), 0),
        "skip_coefficients": jnp.clip(jnp.exp(jax.random.uniform(key_list[7], (H,), jnp.float32, math.log(3.0), math.log(10.0))), 3.0, 10.0),
        "norm_gain": draw_norm_gain(jax.random.fold_in(key_list[13], 71), 0),
        "adapter_down": noise(key_list[9], (ADAPTER_RANK, INNER_CHANNELS), INNER_CHANNELS ** -0.5, 0.09375),
        "adapter_up": noise(key_list[10], (ADAPTER_RANK, OUTPUT_FEATURES), ADAPTER_RANK ** -0.5, 0.75),
        "projection_weight": noise(key_list[11], (OUTPUT_FEATURES, INNER_CHANNELS), INNER_CHANNELS ** -0.5, 0.09375, ((0, 32),)),
        "output_cotangent": draw_output_cotangent(jax.random.fold_in(key_list[13], 71), 0),
    }


EPS_NORM = 1e-05
CLIP_EPSILON = 1e-06
ADAPTER_SCALE = 2.0

def heads_of(grouped):
    lead = grouped.shape[:-2]
    spread = jnp.broadcast_to(grouped[..., :, None, :], lead + (G, H // G, grouped.shape[-1]))
    return spread.reshape(lead + (H, grouped.shape[-1]))

def block_pieces(cum_decay, block_b, block_c):
    b_float = block_b.astype(jnp.float32)
    c_float = block_c.astype(jnp.float32)
    inner_prod = jnp.einsum('ign,jgn->gij', c_float, b_float)
    inner_prod = jnp.broadcast_to(inner_prod[:, None], (G, H // G, Q, Q)).reshape(H, Q, Q)
    cum_heads = cum_decay.T
    gap_logs = cum_heads[:, :, None] - cum_heads[:, None, :]
    causal = lax.broadcasted_iota(jnp.int32, (Q, Q), 0) >= lax.broadcasted_iota(jnp.int32, (Q, Q), 1)
    weights = jnp.where(causal[None], jnp.exp(jnp.where(causal[None], gap_logs, 0.0)), 0.0)
    scores = (inner_prod * weights).astype(jnp.bfloat16)
    block_total = cum_decay[-1]
    b_weighted = (jnp.exp(block_total[None, :] - cum_decay)[:, :, None] * heads_of(b_float)).astype(jnp.bfloat16)
    return (scores, b_weighted)

def forward_block(run_state, block_item):
    xdt_block, block_b, block_c, cum_decay = block_item
    scores, b_weighted = block_pieces(cum_decay, block_b, block_c)
    xdt_float = xdt_block.astype(jnp.float32)
    intra_part = jnp.einsum('hij,jhp->ihp', scores.astype(jnp.float32), xdt_float)
    incoming_bf = run_state.astype(jnp.bfloat16).astype(jnp.float32)
    c_heads = heads_of(block_c.astype(jnp.float32))
    inter_part = jnp.exp(cum_decay)[:, :, None] * jnp.einsum('ihn,hnp->ihp', c_heads, incoming_bf)
    block_state = jnp.einsum('jhn,jhp->hnp', b_weighted.astype(jnp.float32), xdt_float)
    next_state = jnp.exp(cum_decay[-1])[:, None, None] * run_state + block_state
    return (next_state, intra_part + inter_part)

def backward_block(grad_state, block_item):
    grad_block, block_b, block_c, cum_decay = block_item
    scores, b_weighted = block_pieces(cum_decay, block_b, block_c)
    grad_float = grad_block.astype(jnp.float32)
    intra_back = jnp.einsum('hij,ihp->jhp', scores.astype(jnp.float32), grad_float)
    outgoing_bf = grad_state.astype(jnp.bfloat16).astype(jnp.float32)
    cross_part = jnp.einsum('jhn,hnp->jhp', b_weighted.astype(jnp.float32), outgoing_bf)
    c_heads = heads_of(block_c.astype(jnp.float32))
    c_weighted = (jnp.exp(cum_decay)[:, :, None] * c_heads).astype(jnp.bfloat16)
    block_grad = jnp.einsum('ihn,ihp->hnp', c_weighted.astype(jnp.float32), grad_float)
    next_grad = jnp.exp(cum_decay[-1])[:, None, None] * grad_state + block_grad
    return (next_grad, intra_back + cross_part)

def reference(state_input, gate_values, input_matrix, readout_matrix, step_unbiased, step_bias, decay_rate_log, skip_coefficients, norm_gain, adapter_down, adapter_up, projection_weight, output_cotangent):
    block_count = SEQUENCE_LENGTH // Q
    group_width = INNER_CHANNELS // G
    weight_groups = norm_gain.reshape(G, group_width)

    def one_sequence(seq_item):
        seq_x, seq_z, seq_b, seq_c, seq_dt, sequence_gradient = seq_item
        step_size = jax.nn.softplus(seq_dt + step_bias[None, :])
        cum_decay = jnp.cumsum((-jnp.exp(decay_rate_log)[None, :] * step_size).reshape(block_count, Q, H), axis=1)
        x_heads = seq_x.astype(jnp.float32).reshape(SEQUENCE_LENGTH, H, P_SIZE)
        xdt_all = (x_heads * step_size[:, :, None]).astype(jnp.bfloat16).reshape(block_count, Q, H, P_SIZE)
        b_blocks = seq_b.reshape(block_count, Q, G, N)
        c_blocks = seq_c.reshape(block_count, Q, G, N)
        zero_state = jnp.zeros((H, N, P_SIZE), jnp.float32)
        last_state, ssd_parts = lax.scan(forward_block, zero_state, (xdt_all, b_blocks, c_blocks, cum_decay))
        ssd_out = ssd_parts.reshape(SEQUENCE_LENGTH, H, P_SIZE) + skip_coefficients[None, :, None] * x_heads
        silu_z = jax.nn.silu(seq_z.astype(jnp.float32))
        gated = (ssd_out.reshape(SEQUENCE_LENGTH, INNER_CHANNELS) * silu_z).reshape(SEQUENCE_LENGTH, G, group_width)
        rstd = lax.rsqrt(lax.optimization_barrier(jnp.mean(gated * gated, axis=-1, keepdims=True)) + EPS_NORM)
        normalized = (gated * rstd * weight_groups).reshape(SEQUENCE_LENGTH, INNER_CHANNELS).astype(jnp.bfloat16)
        down_product = lax.dot_general(normalized, adapter_down, (((1,), (1,)), ((), ())), preferred_element_type=jnp.float32).astype(jnp.bfloat16)
        upper_gradient = lax.dot_general(sequence_gradient, adapter_up, (((1,), (1,)), ((), ())), preferred_element_type=jnp.float32).astype(jnp.bfloat16)
        down_portion = ADAPTER_SCALE * lax.dot_general(upper_gradient, normalized, (((0,), (0,)), ((), ())), preferred_element_type=jnp.float32)
        up_portion = ADAPTER_SCALE * lax.dot_general(down_product, sequence_gradient, (((0,), (0,)), ((), ())), preferred_element_type=jnp.float32)
        normed_gradient = jnp.dot(sequence_gradient, projection_weight, preferred_element_type=jnp.float32) + ADAPTER_SCALE * jnp.dot(upper_gradient, adapter_down, preferred_element_type=jnp.float32)
        weighted_grad = normed_gradient.reshape(SEQUENCE_LENGTH, G, group_width) * weight_groups
        d_gated = rstd * weighted_grad - gated * (rstd * rstd * rstd) * lax.optimization_barrier(jnp.mean(gated * weighted_grad, axis=-1, keepdims=True))
        d_ssd = d_gated.reshape(SEQUENCE_LENGTH, INNER_CHANNELS) * silu_z
        d_ssd_bf = d_ssd.reshape(block_count, Q, H, P_SIZE).astype(jnp.bfloat16)
        first_grad, back_parts = lax.scan(backward_block, zero_state, (d_ssd_bf, b_blocks, c_blocks, cum_decay), reverse=True)
        grad_heads = step_size[:, :, None] * back_parts.reshape(SEQUENCE_LENGTH, H, P_SIZE) + skip_coefficients[None, :, None] * d_ssd.reshape(SEQUENCE_LENGTH, H, P_SIZE)
        return (grad_heads.reshape(SEQUENCE_LENGTH, INNER_CHANNELS).astype(jnp.bfloat16), down_portion, up_portion)
    stacked = (state_input.reshape(N_DP, SEQUENCE_LENGTH, INNER_CHANNELS), gate_values.reshape(N_DP, SEQUENCE_LENGTH, INNER_CHANNELS), input_matrix.reshape(N_DP, SEQUENCE_LENGTH, G * N), readout_matrix.reshape(N_DP, SEQUENCE_LENGTH, G * N), step_unbiased.reshape(N_DP, SEQUENCE_LENGTH, H), output_cotangent.reshape(N_DP, SEQUENCE_LENGTH, OUTPUT_FEATURES))
    gradient_sequence, parts_a, parts_b = lax.map(one_sequence, stacked)
    down_total = lax.optimization_barrier(jnp.sum(parts_a, axis=0))
    up_total = lax.optimization_barrier(jnp.sum(parts_b, axis=0))
    adapter_down_gradient = down_total / jnp.maximum(1.0, jnp.sqrt(jnp.mean(down_total * down_total) + CLIP_EPSILON))
    adapter_up_gradient = up_total / jnp.maximum(1.0, jnp.sqrt(jnp.mean(up_total * up_total) + CLIP_EPSILON))
    return (gradient_sequence.reshape(TOTAL_ROWS, INNER_CHANNELS), adapter_down_gradient, adapter_up_gradient)
```

```python
import functools

import jax
import jax.numpy as jnp
from jax import lax
from jax.experimental import pallas as pl
from jax.experimental.pallas import tpu as pltpu
from jax.sharding import Mesh
from jax.sharding import PartitionSpec as P

P_SIZE = 64
N = 128
G = 4
Q = 256
EPS_NORM = 1e-05
CLIP_EPSILON = 1e-06
ADAPTER_SCALE = 2.0
WAVES = 2
VMEM_BYTES = 44 * 1024 * 1024

F32 = jnp.float32
BF16 = jnp.bfloat16
AXES = ("dp", "x", "core")


def dot(a, b, dims=((1,), (0,))):
    return lax.dot_general(a, b, (dims, ((), ())), preferred_element_type=F32)


def spread(values, pattern):
    high = values.astype(BF16)
    rest = values - high.astype(F32)
    mid = rest.astype(BF16)
    low = (rest - mid.astype(F32)).astype(BF16)
    return dot(high, pattern) + dot(mid, pattern) + dot(low, pattern)


def pair_rows(pair):
    lane = lax.broadcasted_iota(jnp.int32, pair.shape, 1)
    zero = jnp.zeros_like(pair)
    return jnp.concatenate(
        [jnp.where(lane < P_SIZE, pair, zero), jnp.where(lane >= P_SIZE, pair, zero)], axis=0
    )


def whole(shape):
    return pl.BlockSpec(shape, lambda *_: (0,) * len(shape))


def params(*semantics):
    return pltpu.CompilerParams(
        dimension_semantics=semantics or None, vmem_limit_bytes=VMEM_BYTES
    )


def local_kernel(
    first, heads, x_ref, b_ref, c_ref, step_ref, cum_ref, cum_t_ref, skip_ref, pattern_ref,
    scores_ref, ssd_ref, state_ref, total_ref, step_wide_ref, cum_wide_ref, weight_ref, decay_ref,
):
    block = pl.program_id(0)
    own = slice(first, first + heads)
    pattern = pattern_ref[...]
    step = step_ref[:, own]
    cum = cum_ref[:, own]
    last = cum[Q - 1 : Q, :]
    step_wide = spread(step, pattern)
    cum_wide = spread(jnp.exp(cum), pattern)
    weight = spread(step * jnp.exp(last - cum), pattern)
    step_wide_ref[...] = step_wide
    cum_wide_ref[...] = cum_wide
    weight_ref[...] = weight
    decay = cum_wide[Q - 1 : Q, :]
    decay_ref[...] = jnp.broadcast_to(decay, decay_ref.shape)
    x = x_ref[...].astype(F32)
    xdt = (x * step_wide).astype(BF16)
    state = dot(b_ref[...], (x * weight).astype(BF16), ((0,), (0,)))
    state_ref[...] = state

    @pl.when(block == 0)
    def _():
        total_ref[...] = state

    @pl.when(block > 0)
    def _():
        total_ref[...] = total_ref[...] * decay + state

    inner = dot(b_ref[...], c_ref[...], ((1,), (1,)))
    causal = lax.broadcasted_iota(jnp.int32, (Q, Q), 1) >= lax.broadcasted_iota(
        jnp.int32, (Q, Q), 0
    )
    masked = jnp.where(causal, inner, 0.0)
    for pair in range(heads // 2):
        parts = []
        for head in (2 * pair, 2 * pair + 1):
            gap = cum_t_ref[0, first + head : first + head + 1, :] - cum[:, head : head + 1]
            part = (masked * jnp.exp(jnp.where(causal, gap, 0.0))).astype(BF16)
            scores_ref[:, head * Q : (head + 1) * Q] = part
            parts.append(part)
        lanes = slice(pair * 2 * P_SIZE, (pair + 1) * 2 * P_SIZE)
        intra = dot(jnp.concatenate(parts, axis=0), pair_rows(xdt[:, lanes]), ((0,), (0,)))
        ssd_ref[:, lanes] = intra + skip_ref[:, lanes] * x_ref[:, lanes].astype(F32)


def local_part(group, heads, x, b, c, step, cum, cum_t, skip, pattern):
    rows = x.shape[0]
    blocks = rows // Q
    width = heads * P_SIZE
    row_block = pl.BlockSpec((Q, width), lambda i: (i, 0))
    return pl.pallas_call(
        functools.partial(local_kernel, group * heads, heads),
        grid=(blocks,),
        in_specs=[
            pl.BlockSpec((Q, width), lambda i: (i, group)),
            pl.BlockSpec((Q, N), lambda i: (i, group)),
            pl.BlockSpec((Q, N), lambda i: (i, group)),
            pl.BlockSpec((Q, step.shape[1]), lambda i: (i, 0)),
            pl.BlockSpec((Q, step.shape[1]), lambda i: (i, 0)),
            pl.BlockSpec((1,) + cum_t.shape[1:], lambda i: (i, 0, 0)),
            pl.BlockSpec((1, width), lambda i: (0, group)),
            whole(pattern.shape),
        ],
        out_specs=[
            pl.BlockSpec((Q, heads * Q), lambda i: (i, 0)),
            row_block,
            pl.BlockSpec((N, width), lambda i: (i, 0)),
            pl.BlockSpec((N, width), lambda i: (0, 0)),
            row_block,
            row_block,
            row_block,
            pl.BlockSpec((8, width), lambda i: (i, 0)),
        ],
        out_shape=[
            jax.ShapeDtypeStruct((rows, heads * Q), BF16),
            jax.ShapeDtypeStruct((rows, width), F32),
            jax.ShapeDtypeStruct((blocks * N, width), F32),
            jax.ShapeDtypeStruct((N, width), F32),
            jax.ShapeDtypeStruct((rows, width), F32),
            jax.ShapeDtypeStruct((rows, width), F32),
            jax.ShapeDtypeStruct((rows, width), F32),
            jax.ShapeDtypeStruct((blocks * 8, width), F32),
        ],
        compiler_params=params("arbitrary"),
        cost_estimate=pl.CostEstimate(
            flops=rows * width * Q * 4, bytes_accessed=rows * width * 24, transcendentals=0
        ),
        name="local_part",
    )(x, b, c, step, cum, cum_t, skip, pattern)


def norm_kernel(
    blocks, c_ref, incoming_ref, state_ref, decay_ref, cum_wide_ref, ssd_ref, z_ref, gain_ref,
    down_ref, up_ref, hat_ref, slope_ref, product_ref, sum_ref,
):
    gain = gain_ref[...]
    run = incoming_ref[...].astype(F32)
    total = None
    for block in range(blocks):
        rows = slice(block * Q, (block + 1) * Q)
        inter = dot(c_ref[rows, :], run.astype(BF16))
        ssd = ssd_ref[rows, :] + cum_wide_ref[rows, :] * inter
        z = z_ref[rows, :].astype(F32)
        silu = z / (1.0 + jnp.exp(-z))
        gated = ssd * silu
        rstd = lax.rsqrt(jnp.mean(gated * gated, axis=1, keepdims=True) + EPS_NORM)
        hat = gated * rstd
        normed = (hat * gain).astype(BF16)
        hat_ref[rows, :] = hat.astype(hat_ref.dtype)
        slope_ref[rows, :] = rstd * silu
        product_ref[rows, :] = dot(normed, down_ref[...], ((1,), (1,)))
        part = dot(up_ref[rows, :], normed, ((0,), (0,)))
        total = part if total is None else total + part
        if block + 1 < blocks:
            states = slice(block * N, (block + 1) * N)
            run = run * decay_ref[block * 8 : block * 8 + 1, :] + state_ref[states, :]
    sum_ref[...] = total


def norm_part(group, c, incoming, state, decay, cum_wide, ssd, z, gain, down, up_twice):
    rows, width = ssd.shape
    rank = down.shape[0]
    blocks = rows // Q
    return pl.pallas_call(
        functools.partial(norm_kernel, blocks),
        grid=(1,),
        in_specs=[
            pl.BlockSpec((rows, N), lambda i: (0, group)),
            whole(incoming.shape),
            whole(state.shape),
            whole(decay.shape),
            whole(cum_wide.shape),
            whole(ssd.shape),
            pl.BlockSpec((rows, width), lambda i: (0, group)),
            pl.BlockSpec((1, width), lambda i: (0, group)),
            pl.BlockSpec((rank, width), lambda i: (0, group)),
            whole(up_twice.shape),
        ],
        out_specs=[
            whole((rows, width)), whole((rows, width)), whole((rows, rank)), whole((rank, width)),
        ],
        out_shape=[
            jax.ShapeDtypeStruct((rows, width), F32),
            jax.ShapeDtypeStruct((rows, width), F32),
            jax.ShapeDtypeStruct((rows, rank), F32),
            jax.ShapeDtypeStruct((rank, width), F32),
        ],
        compiler_params=params("arbitrary"),
        cost_estimate=pl.CostEstimate(
            flops=rows * width * 512, bytes_accessed=rows * width * 20, transcendentals=0
        ),
        name="norm_part",
    )(c, incoming, state, decay, cum_wide, ssd, z, gain, down, up_twice)


def grad_kernel(
    blocks, segments, place_ref, cot_ref, up_ref, down_ref, gain_ref, hat_ref, slope_ref,
    cum_wide_ref, decay_ref, c_ref, *rest,
):
    count = len({segment[0] for segment in segments})
    pieces, rest = rest[:count], rest[count:]
    grad_ref, block_grad_ref, total_ref, weights, sems = rest
    copies = []
    for index, (piece, start, size, slot, offset, column) in enumerate(segments):
        target = pl.multiple_of(place_ref[slot] + offset, 16)
        copy = pltpu.make_async_copy(
            pieces[piece].at[pl.ds(start, size)],
            weights.at[pl.ds(target, size), pl.ds(column, pieces[piece].shape[1])],
            sems.at[index],
        )
        copy.start()
        copies.append(copy)
    for copy in copies:
        copy.wait()
    gain = gain_ref[...]
    later = None
    for block in reversed(range(blocks)):
        rows = slice(block * Q, (block + 1) * Q)
        product = dot(cot_ref[rows, :], weights[...]) + dot(up_ref[rows, :], down_ref[...])
        weighted = product * gain
        hat = hat_ref[rows, :]
        mean = jnp.mean(hat * weighted, axis=1, keepdims=True)
        grad = slope_ref[rows, :] * (weighted - hat * mean)
        grad_ref[rows, :] = grad
        fresh = dot(c_ref[rows, :], (cum_wide_ref[rows, :] * grad).astype(BF16), ((0,), (0,)))
        block_grad_ref[block * N : (block + 1) * N, :] = fresh
        later = (
            fresh
            if later is None
            else later * decay_ref[block * 8 : block * 8 + 1, :] + fresh
        )
    total_ref[...] = later.astype(BF16)


def grad_part(group, place, cot, up_twice, down, gain, hat, slope, cum_wide, decay, c, pieces, segments):
    rows, width = hat.shape
    rank = down.shape[0]
    blocks = rows // Q
    depth = cot.shape[1]
    return pl.pallas_call(
        functools.partial(grad_kernel, blocks, segments),
        grid=(1,),
        in_specs=[
            pl.BlockSpec(memory_space=pltpu.SMEM),
            whole(cot.shape),
            whole(up_twice.shape),
            pl.BlockSpec((rank, width), lambda i: (0, group)),
            pl.BlockSpec((1, width), lambda i: (0, group)),
            whole(hat.shape),
            whole(slope.shape),
            whole(cum_wide.shape),
            whole(decay.shape),
            pl.BlockSpec((rows, N), lambda i: (0, group)),
        ]
        + [pl.BlockSpec(memory_space=pl.ANY)] * len(pieces),
        out_specs=[whole((rows, width)), whole((blocks * N, width)), whole((N, width))],
        out_shape=[
            jax.ShapeDtypeStruct((rows, width), F32),
            jax.ShapeDtypeStruct((blocks * N, width), F32),
            jax.ShapeDtypeStruct((N, width), BF16),
        ],
        scratch_shapes=[
            pltpu.VMEM((depth, width), BF16),
            pltpu.SemaphoreType.DMA((len(segments),)),
        ],
        compiler_params=params("arbitrary"),
        cost_estimate=pl.CostEstimate(
            flops=2 * rows * width * depth, bytes_accessed=depth * width * 2 + rows * width * 20,
            transcendentals=0,
        ),
        name="grad_part",
    )(place, cot, up_twice, down, gain, hat, slope, cum_wide, decay, c, *pieces)


def back_kernel(heads, scores_ref, grad_ref, step_wide_ref, skip_ref, out_ref):
    for pair in range(heads // 2):
        lanes = slice(pair * 2 * P_SIZE, (pair + 1) * 2 * P_SIZE)
        grad = grad_ref[:, lanes]
        back = dot(
            scores_ref[:, 2 * pair * Q : 2 * (pair + 1) * Q], pair_rows(grad.astype(BF16))
        )
        out_ref[:, lanes] = step_wide_ref[:, lanes] * back + skip_ref[:, lanes] * grad


def back_part(group, heads, scores, grad, step_wide, skip):
    rows, width = grad.shape
    row_block = pl.BlockSpec((Q, width), lambda i: (i, 0))
    return pl.pallas_call(
        functools.partial(back_kernel, heads),
        grid=(rows // Q,),
        in_specs=[
            pl.BlockSpec((Q, heads * Q), lambda i: (i, 0)),
            row_block,
            row_block,
            pl.BlockSpec((1, width), lambda i: (0, group)),
        ],
        out_specs=row_block,
        out_shape=jax.ShapeDtypeStruct((rows, width), F32),
        compiler_params=params("arbitrary"),
        cost_estimate=pl.CostEstimate(
            flops=rows * width * Q * 2, bytes_accessed=rows * width * 20, transcendentals=0
        ),
        name="back_part",
    )(scores, grad, step_wide, skip)


def cross_kernel(blocks, b_ref, outgoing_ref, block_grad_ref, decay_ref, weight_ref, base_ref, out_ref):
    run = outgoing_ref[...].astype(F32)
    for block in reversed(range(blocks)):
        rows = slice(block * Q, (block + 1) * Q)
        cross = dot(b_ref[rows, :], run.astype(BF16))
        out_ref[rows, :] = (base_ref[rows, :] + weight_ref[rows, :] * cross).astype(out_ref.dtype)
        if block > 0:
            states = slice(block * N, (block + 1) * N)
            run = run * decay_ref[block * 8 : block * 8 + 1, :] + block_grad_ref[states, :]


def cross_part(group, b, outgoing, block_grad, decay, weight, base):
    rows, width = base.shape
    blocks = rows // Q
    return pl.pallas_call(
        functools.partial(cross_kernel, blocks),
        grid=(1,),
        in_specs=[
            pl.BlockSpec((rows, N), lambda i: (0, group)),
            whole(outgoing.shape),
            whole(block_grad.shape),
            whole(decay.shape),
            whole(weight.shape),
            whole(base.shape),
        ],
        out_specs=whole((rows, width)),
        out_shape=jax.ShapeDtypeStruct((rows, width), BF16),
        compiler_params=params("arbitrary"),
        cost_estimate=pl.CostEstimate(
            flops=rows * width * N * 2, bytes_accessed=rows * width * 12, transcendentals=0
        ),
        name="cross_part",
    )(b, outgoing, block_grad, decay, weight, base)


def ring_order(count):
    return list(range(0, count, 2)) + list(range(count - 1 - count % 2, 0, -2))


def rotations(count):
    return [[(i, (i + k) % count) for i in range(count)] for k in range(count)]


class Gather:
    def __init__(self):
        self.ring = lax.axis_size("dp")
        self.across = lax.axis_size("x")
        order = ring_order(self.ring)
        self.ahead = [(order[i], order[(i + 1) % self.ring]) for i in range(self.ring)]
        self.back = [(b, a) for a, b in self.ahead]
        self.turns = rotations(self.across)
        self.offsets = [0]
        for distance in range(1, (self.ring - 1) // 2 + 1):
            self.offsets += [-distance, distance]
        if self.ring % 2 == 0:
            self.offsets.append(self.ring // 2)
        seat = [0] * self.ring
        for position, member in enumerate(order):
            seat[member] = position
        table = jnp.asarray(order, jnp.int32)
        mine = jnp.asarray(seat, jnp.int32)[lax.axis_index("dp")]
        x = lax.axis_index("x")
        chips = []
        for offset in self.offsets:
            member = table[(mine + offset) % self.ring]
            chips += [member * self.across + (x - k) % self.across for k in range(self.across)]
        self.chips = jnp.stack(chips).astype(jnp.int32)

    def chain(self, own, spans):
        pieces = [(own, [(0 * self.across + s, o, r) for s, o, r in spans])]
        ahead = back = own
        for index in range(1, (self.ring - 1) // 2 + 1):
            ahead = lax.ppermute(ahead, "dp", self.ahead)
            back = lax.ppermute(back, "dp", self.back)
            for place, piece in ((2 * index - 1, ahead), (2 * index, back)):
                pieces.append((piece, [(place * self.across + s, o, r) for s, o, r in spans]))
        if self.ring % 2 == 0:
            half = own.shape[0] // 2
            place = len(self.offsets) - 1
            front, rear, seen = [], [], 0
            for s, o, r in spans:
                slot = place * self.across + s
                if seen + r <= half:
                    front.append((slot, o, r))
                elif seen >= half:
                    rear.append((slot, o, r))
                else:
                    front.append((slot, o, half - seen))
                    rear.append((slot, o + half - seen, r - half + seen))
                seen += r
            pieces.append((lax.ppermute(ahead[:half], "dp", self.ahead), front))
            pieces.append((lax.ppermute(back[half:], "dp", self.back), rear))
        return pieces

    def across_first(self, own):
        rows = own.shape[0]
        parts = [own] + [lax.ppermute(own, "x", turn) for turn in self.turns[1:]]
        spans = [(k, 0, rows) for k in range(self.across)]
        return self.chain(jnp.concatenate(parts, axis=0), spans)

    def across_last(self, own):
        pieces = self.chain(own, [(0, 0, own.shape[0])])
        batches = [pieces[:3], pieces[3:5], pieces[5:]]
        result = list(pieces)
        for batch in batches:
            if not batch:
                continue
            joined = jnp.concatenate([piece for piece, _ in batch], axis=0)
            spans = [span for _, listed in batch for span in listed]
            for k, turn in enumerate(self.turns[1:], 1):
                moved = lax.ppermute(joined, "x", turn)
                result.append((moved, [(slot + k, o, r) for slot, o, r in spans]))
        return result


def layout(parts):
    arrays, segments = [], []
    for pieces, column in parts:
        for array, spans in pieces:
            start = 0
            for slot, offset, rows in spans:
                segments.append((len(arrays), start, rows, slot, offset, column))
                start += rows
            arrays.append(array)
    return arrays, tuple(segments)


def summed_blocks(sum_a, sum_b):
    ring, across = lax.axis_size("dp"), lax.axis_size("x")
    rank = sum_a.shape[0]
    chips = ring * across
    wide_a, wide_b = sum_a.shape[1] // chips, sum_b.shape[1] // chips

    def by_block(value, width):
        return value.reshape(rank, chips, width).transpose(1, 0, 2)

    blocks = jnp.concatenate([by_block(sum_a, wide_a), by_block(sum_b, wide_b)], axis=2)
    blocks = blocks.reshape(ring, across, rank, wide_a + wide_b)
    x, place = lax.axis_index("x"), lax.axis_index("dp")

    def column(index):
        return lax.dynamic_index_in_dim(blocks, index, 1, False)

    total = column(x)
    for k, turn in enumerate(rotations(across)[1:], 1):
        sent = column((x + k) % across).astype(BF16)
        total = total + lax.ppermute(sent, "x", turn).astype(F32)
    distance = ring // 2
    while distance:
        upper = (place // distance) % 2
        kept = lax.dynamic_slice_in_dim(total, upper * distance, distance, 0)
        sent = lax.dynamic_slice_in_dim(total, (1 - upper) * distance, distance, 0)
        pairs = [(i, i ^ distance) for i in range(ring)]
        total = kept + lax.ppermute(sent.astype(BF16), "dp", pairs).astype(F32)
        distance //= 2
    return total[0, :, :wide_a], total[0, :, wide_a:]


def on_device(
    state_input, gate_values, input_matrix, readout_matrix, step_unbiased, step_bias,
    decay_rate_log, skip_coefficients, norm_gain, adapter_down, adapter_up, projection_weight,
    output_cotangent,
):
    ring, across = lax.axis_size("dp"), lax.axis_size("x")
    core = lax.axis_index("core")
    swap = [(0, 1), (1, 0)]
    near_rows = state_input.shape[0]
    groups = G // 2
    heads = step_bias.shape[0] // G
    width = heads * P_SIZE

    def half(value, which, axis=-1):
        size = value.shape[axis] // 2
        return lax.dynamic_slice_in_dim(value, which * size, size, axis)

    def in_order(near, far, axis=0):
        return jnp.concatenate(
            [jnp.where(core == 0, near, far), jnp.where(core == 0, far, near)], axis=axis
        )

    def both_cores(value):
        far = lax.ppermute(half(value, 1 - core), "core", swap)
        return in_order(half(value, core), far)

    gather = Gather()
    shard = both_cores(projection_weight)
    chip_rows = shard.shape[0]
    place = gather.chips * chip_rows
    plans = []
    if WAVES == 1:
        first = gather.across_first(shard[:, :width])
        second = gather.across_last(shard[:, width:])
        plans = [layout([(first, 0)]), layout([(second, 0)])]
    else:
        for group in range(groups):
            part = shard[:, group * width : (group + 1) * width]
            cut = width // 2
            plans.append(
                layout(
                    [(gather.across_first(part[:, :cut]), 0), (gather.across_last(part[:, cut:]), cut)]
                )
            )

    step_raw = both_cores(step_unbiased)
    rows = step_raw.shape[0]
    blocks = rows // Q
    x = both_cores(state_input)
    b = both_cores(input_matrix)
    c = both_cores(readout_matrix)
    z = both_cores(gate_values)
    cot = in_order(output_cotangent, lax.ppermute(output_cotangent, "core", swap))
    step = jax.nn.softplus(step_raw + half(step_bias, core)[None, :])
    log_decay = -jnp.exp(half(decay_rate_log, core))[None, :] * step
    cum_blocks = jnp.cumsum(log_decay.reshape(blocks, Q, -1), axis=1)
    cum = cum_blocks.reshape(rows, -1)
    cum_t = jnp.swapaxes(cum_blocks, 1, 2)
    skip = jnp.repeat(half(skip_coefficients, core), P_SIZE)[None, :]
    gain = half(norm_gain, core)[None, :]
    down = half(adapter_down, core)
    pattern = jnp.repeat(jnp.eye(heads, dtype=BF16), P_SIZE, axis=1)

    up_twice = (
        ADAPTER_SCALE * dot(cot, adapter_up, ((1,), (1,))).astype(BF16)
    ).astype(BF16)

    local = [
        local_part(group, heads, x, b, c, step, cum, cum_t, skip, pattern)
        for group in range(groups)
    ]
    forward = [(i, i + 1) for i in range(across - 1)]
    backward = [(i + 1, i) for i in range(across - 1)]

    def carried(fresh, decay, perm):
        chip_decay = None
        sent = fresh.astype(BF16)
        for lap in range(across - 1):
            arrived = lax.ppermute(sent, "x", perm)
            if lap + 2 < across:
                if chip_decay is None:
                    chip_decay = jnp.prod(decay.reshape(blocks, 8, -1)[:, :1], axis=0)
                sent = (arrived.astype(F32) * chip_decay + fresh.astype(F32)).astype(BF16)
        return arrived

    normed = []
    for group in range(groups):
        scores, ssd, state, total, step_wide, cum_wide, weight, decay = local[group]
        incoming = carried(total, decay, forward)
        normed.append(
            norm_part(group, c, incoming, state, decay, cum_wide, ssd, z, gain, down, up_twice)
        )

    product = functools.reduce(jnp.add, [part[2] for part in normed])
    arrived = lax.ppermute(half(product, 1 - core, 0), "core", swap)
    down_product = (half(product, core, 0) + arrived).astype(BF16)
    sum_a = jnp.concatenate([part[3] for part in normed], axis=1)
    part_b = ADAPTER_SCALE * dot(down_product, output_cotangent, ((0,), (0,)))
    far_b = lax.ppermute(half(part_b, 1 - core).astype(BF16), "core", swap)
    sum_b = half(part_b, core) + far_b.astype(F32)
    block_a, block_b = summed_blocks(sum_a, sum_b)
    squares = lax.psum(jnp.stack([jnp.sum(block_a * block_a), jnp.sum(block_b * block_b)]), AXES)
    devices = ring * across * 2
    entries = jnp.asarray([block_a.size * devices, block_b.size * devices], F32)
    scale = 1.0 / jnp.maximum(1.0, jnp.sqrt(squares / entries + CLIP_EPSILON))
    chips = ring * across
    homes = [
        ((chip * 2 + number), number * chips + chip) for chip in range(chips) for number in range(2)
    ]
    joined = jnp.concatenate([block_a * scale[0], block_b * scale[1]], axis=1)
    joined = lax.ppermute(joined, AXES, homes)
    gradient_a = joined[:, : block_a.shape[1]]
    gradient_b = joined[:, block_a.shape[1] :]

    near, far = [], []
    for group in range(groups):
        scores, ssd, state, total, step_wide, cum_wide, weight, decay = local[group]
        hat, slope = normed[group][:2]
        pieces, segments = plans[group]
        grad, block_grad, grad_total = grad_part(
            group, place, cot, up_twice, down, gain, hat, slope, cum_wide, decay, c, pieces, segments
        )
        outgoing = carried(grad_total, decay, backward)
        base = back_part(group, heads, scores, grad, step_wide, skip)
        result = cross_part(group, b, outgoing, block_grad, decay, weight, base)
        far.append(lax.ppermute(half(result, 1 - core, 0), "core", swap))
        near.append(half(result, core, 0))
    input_gradient = in_order(
        jnp.concatenate(near, axis=1), jnp.concatenate(far, axis=1), axis=1
    )
    return input_gradient, gradient_a, gradient_b


def solution(mesh):
    ring, ctx = mesh.shape["dp"], mesh.shape["ctx"]
    split = Mesh(mesh.devices.reshape(ring, ctx // 2, 2), AXES)
    rows = P(AXES, None)
    placed = (rows,) * 5 + (P(),) * 6 + (rows,) * 2
    return jax.shard_map(
        on_device,
        mesh=split,
        in_specs=placed,
        out_specs=(rows, P(None, AXES), P(None, AXES)),
        check_vma=False,
    )
```

```python
import functools

import jax
import jax.numpy as jnp
import numpy as np
from jax import lax
from jax.experimental import pallas as pl
from jax.experimental.pallas import tpu as pltpu
from jax.sharding import Mesh
from jax.sharding import PartitionSpec as P

P_SIZE = 64
N = 128
G = 4
Q = 256
EPS_NORM = 1e-05
CLIP_EPSILON = 1e-06
ADAPTER_SCALE = 2.0
VMEM_BYTES = 24 * 1024 * 1024

F32 = jnp.float32
BF16 = jnp.bfloat16
AXES = ("dp", "x", "core")


def dot(a, b, dims=((1,), (0,))):
    return lax.dot_general(a, b, (dims, ((), ())), preferred_element_type=F32)


def spread(values, pattern):
    high = values.astype(BF16).astype(F32)
    rest = values - high
    mid = rest.astype(BF16).astype(F32)
    return dot(jnp.concatenate([high, mid, rest - mid], axis=1).astype(BF16), pattern)


def spread_pattern(heads):
    return np.tile(np.repeat(np.eye(heads), P_SIZE, axis=1), (3, 1)).astype(BF16)


def of_core(ref, rows, core, first, heads):
    half = ref.shape[1] // 2
    return jnp.where(
        core == 0, ref[rows, first : first + heads], ref[rows, half + first : half + first + heads]
    )


def pair_rows(pair):
    lane = lax.broadcasted_iota(jnp.int32, pair.shape, 1)
    zero = jnp.zeros_like(pair)
    return jnp.concatenate(
        [jnp.where(lane < P_SIZE, pair, zero), jnp.where(lane >= P_SIZE, pair, zero)], axis=0
    )


def whole(shape):
    return pl.BlockSpec(shape, lambda *_: (0,) * len(shape))


def cost(flops, slowdown):
    return pl.CostEstimate(flops=flops * slowdown, bytes_accessed=0, transcendentals=0)


def params(*semantics):
    return pltpu.CompilerParams(
        dimension_semantics=semantics or None, vmem_limit_bytes=VMEM_BYTES
    )


def step_kernel(blocks, core_ref, near_ref, far_ref, bias_ref, rate_ref, step_ref, cum_ref, cum_t_ref):
    lower = lax.broadcasted_iota(jnp.int32, (Q, Q), 0) >= lax.broadcasted_iota(
        jnp.int32, (Q, Q), 1
    )
    for block in range(blocks):
        rows = slice(block * Q, (block + 1) * Q)
        local = slice(block % (blocks // 2) * Q, (block % (blocks // 2) + 1) * Q)
        raw = jnp.where(
            core_ref[0] == block // (blocks // 2), near_ref[local, :], far_ref[local, :]
        )
        raw = raw + bias_ref[...]
        step = jnp.maximum(raw, 0.0) + jnp.log1p(jnp.exp(-jnp.abs(raw)))
        cum = lax.dot_general(
            lower.astype(F32),
            -jnp.exp(rate_ref[...]) * step,
            (((1,), (0,)), ((), ())),
            precision=lax.Precision.HIGHEST,
            preferred_element_type=F32,
        )
        step_ref[rows, :] = step
        cum_ref[rows, :] = cum
        cum_t_ref[block] = cum.T


def step_part(core, near, far, bias, rate):
    rows, heads = 2 * near.shape[0], near.shape[1]
    spec = pltpu.PrefetchScalarGridSpec(
        num_scalar_prefetch=1,
        grid=(1,),
        in_specs=[whole(near.shape), whole(far.shape), whole(bias.shape), whole(rate.shape)],
        out_specs=[whole((rows, heads)), whole((rows, heads)), whole((rows // Q, heads, Q))],
    )
    return pl.pallas_call(
        functools.partial(step_kernel, rows // Q),
        grid_spec=spec,
        out_shape=[
            jax.ShapeDtypeStruct((rows, heads), F32),
            jax.ShapeDtypeStruct((rows, heads), F32),
            jax.ShapeDtypeStruct((rows // Q, heads, Q), F32),
        ],
        compiler_params=params("arbitrary"),
        cost_estimate=cost(rows * heads * Q, 200),
        name="step_part",
    )(core, near, far, bias, rate)


def local_kernel(
    first, heads, core_ref, near_ref, far_ref, b_ref, c_ref, step_ref, cum_ref, cum_t_ref, skip_ref,
    pattern_ref, scores_ref, ssd_ref, state_ref, total_ref, x_ref,
):
    block = pl.program_id(0)
    core = core_ref[0]
    x_ref[...] = jnp.where(
        block // (pl.num_programs(0) // 2) == core, near_ref[...], far_ref[...]
    )
    pattern = pattern_ref[...]
    step = of_core(step_ref, slice(None), core, first, heads)
    cum = of_core(cum_ref, slice(None), core, first, heads)
    start = pl.multiple_of(core * (cum_t_ref.shape[1] // 2) + first, 8)
    cum_t = cum_t_ref[0, pl.ds(start, heads), :]
    last = cum[Q - 1 : Q, :]
    step_wide = spread(step, pattern)
    weight = spread(step * jnp.exp(last - cum), pattern)
    decay = spread(jnp.broadcast_to(jnp.exp(last), (8, heads)), pattern)[:1, :]
    x = x_ref[...].astype(F32)
    xdt = (x * step_wide).astype(BF16)
    state = dot(b_ref[...], (x * weight).astype(BF16), ((0,), (0,)))
    state_ref[...] = state

    @pl.when(block == 0)
    def _():
        total_ref[...] = state

    @pl.when(block > 0)
    def _():
        total_ref[...] = total_ref[...] * decay + state

    inner = dot(b_ref[...], c_ref[...], ((1,), (1,)))
    causal = lax.broadcasted_iota(jnp.int32, (Q, Q), 1) >= lax.broadcasted_iota(
        jnp.int32, (Q, Q), 0
    )
    masked = jnp.where(causal, inner, 0.0)
    for pair in range(heads // 2):
        parts = []
        for head in (2 * pair, 2 * pair + 1):
            gap = cum_t[head : head + 1, :] - cum[:, head : head + 1]
            part = (masked * jnp.exp(jnp.where(causal, gap, 0.0))).astype(BF16)
            scores_ref[:, head * Q : (head + 1) * Q] = part
            parts.append(part)
        lanes = slice(pair * 2 * P_SIZE, (pair + 1) * 2 * P_SIZE)
        intra = dot(jnp.concatenate(parts, axis=0), pair_rows(xdt[:, lanes]), ((0,), (0,)))
        ssd_ref[:, lanes] = intra + skip_ref[:, lanes] * x_ref[:, lanes].astype(F32)


def local_part(group, groups, heads, core, near, far, b, c, step, cum, cum_t, skip, pattern):
    rows = 2 * near.shape[0]
    blocks = rows // Q
    width = heads * P_SIZE
    row_block = pl.BlockSpec((Q, width), lambda i, s: (i, 0))
    spec = pltpu.PrefetchScalarGridSpec(
        num_scalar_prefetch=1,
        grid=(blocks,),
        in_specs=[
            pl.BlockSpec((Q, width), lambda i, s: (i % (blocks // 2), s[0] * groups + group)),
            pl.BlockSpec((Q, width), lambda i, s: (i % (blocks // 2), group)),
            pl.BlockSpec((Q, N), lambda i, s: (i, group)),
            pl.BlockSpec((Q, N), lambda i, s: (i, group)),
            pl.BlockSpec((Q, step.shape[1]), lambda i, s: (i, 0)),
            pl.BlockSpec((Q, step.shape[1]), lambda i, s: (i, 0)),
            pl.BlockSpec((1,) + cum_t.shape[1:], lambda i, s: (i, 0, 0)),
            pl.BlockSpec((1, width), lambda i, s: (0, s[0] * groups + group)),
            whole(pattern.shape),
        ],
        out_specs=[
            pl.BlockSpec((Q, heads * Q), lambda i, s: (i, 0)),
            row_block,
            pl.BlockSpec((N, width), lambda i, s: (i, 0)),
            pl.BlockSpec((N, width), lambda i, s: (0, 0)),
        ],
        scratch_shapes=[pltpu.VMEM((Q, width), BF16)],
    )
    return pl.pallas_call(
        functools.partial(local_kernel, group * heads, heads),
        grid_spec=spec,
        out_shape=[
            jax.ShapeDtypeStruct((rows, heads * Q), BF16),
            jax.ShapeDtypeStruct((rows, width), F32),
            jax.ShapeDtypeStruct((blocks * N, width), F32),
            jax.ShapeDtypeStruct((N, width), F32),
        ],
        compiler_params=params("arbitrary"),
        cost_estimate=cost(rows * width * Q * 4, 18),
        name="local_part",
    )(core, near, far, b, c, step, cum, cum_t, skip, pattern)


def norm_kernel(
    blocks, first, heads, core_ref, c_ref, incoming_ref, state_ref, cum_ref, pattern_ref, ssd_ref, near_ref,
    far_ref, gain_ref, down_ref, up_ref, hat_ref, slope_ref, product_ref, sum_ref,
):
    gain = gain_ref[...]
    run = incoming_ref[...].astype(F32)
    total = None
    for block in range(blocks):
        rows = slice(block * Q, (block + 1) * Q)
        inter = dot(c_ref[rows, :], run.astype(BF16))
        growth = spread(jnp.exp(of_core(cum_ref, rows, core_ref[0], first, heads)), pattern_ref[...])
        ssd = ssd_ref[rows, :] + growth * inter
        local = slice(block % (blocks // 2) * Q, (block % (blocks // 2) + 1) * Q)
        z = jnp.where(
            core_ref[0] == block // (blocks // 2), near_ref[local, :], far_ref[local, :]
        ).astype(F32)
        silu = z / (1.0 + jnp.exp(-z))
        gated = ssd * silu
        rstd = lax.rsqrt(jnp.mean(gated * gated, axis=1, keepdims=True) + EPS_NORM)
        hat = gated * rstd
        normed = (hat * gain).astype(BF16)
        hat_ref[rows, :] = hat.astype(hat_ref.dtype)
        slope_ref[rows, :] = rstd * silu
        product_ref[rows, :] = dot(normed, down_ref[...], ((1,), (1,)))
        part = dot(up_ref[rows, :], normed, ((0,), (0,)))
        total = part if total is None else total + part
        if block + 1 < blocks:
            states = slice(block * N, (block + 1) * N)
            run = run * growth[Q - 1 :, :] + state_ref[states, :]
    sum_ref[...] = total


def norm_part(
    group, groups, heads, core, c, incoming, state, cum, pattern, ssd, near, far, gain, down, up_twice
):
    rows, width = ssd.shape
    rank = down.shape[0]
    blocks = rows // Q
    spec = pltpu.PrefetchScalarGridSpec(
        num_scalar_prefetch=1,
        grid=(1,),
        in_specs=[
            pl.BlockSpec((rows, N), lambda i, s: (0, group)),
            whole(incoming.shape),
            whole(state.shape),
            whole(cum.shape),
            whole(pattern.shape),
            whole(ssd.shape),
            pl.BlockSpec((rows // 2, width), lambda i, s: (0, s[0] * groups + group)),
            pl.BlockSpec((rows // 2, width), lambda i, s: (0, group)),
            pl.BlockSpec((1, width), lambda i, s: (0, s[0] * groups + group)),
            pl.BlockSpec((rank, width), lambda i, s: (0, s[0] * groups + group)),
            whole(up_twice.shape),
        ],
        out_specs=[
            whole((rows, width)), whole((rows, width)), whole((rows, rank)), whole((rank, width)),
        ],
    )
    return pl.pallas_call(
        functools.partial(norm_kernel, blocks, group * heads, heads),
        grid_spec=spec,
        out_shape=[
            jax.ShapeDtypeStruct((rows, width), BF16),
            jax.ShapeDtypeStruct((rows, width), F32),
            jax.ShapeDtypeStruct((rows, rank), F32),
            jax.ShapeDtypeStruct((rank, width), F32),
        ],
        compiler_params=params("arbitrary"),
        cost_estimate=cost(rows * width * 512, 14),
        name="norm_part",
    )(core, c, incoming, state, cum, pattern, ssd, near, far, gain, down, up_twice)


def product_kernel(count, started, core_ref, near_ref, far_ref, *rest):
    pieces, out_ref = rest[started : started + count], rest[-1]
    weights = joined(pieces)
    half = near_ref.shape[0]
    for part in range(2):
        rows = slice(part * half, (part + 1) * half)
        cot = jnp.where(core_ref[0] == part, near_ref[...], far_ref[...])
        product = dot(cot, weights)
        out_ref[rows, :] = product + rest[0][rows, :] if started else product


def joined(pieces):
    return jnp.concatenate([piece[...] for piece in pieces], axis=0)


def product_part(core, near, far, earlier, pieces, width):
    rows = 2 * near.shape[0]
    held = [] if earlier is None else [earlier]
    spec = pltpu.PrefetchScalarGridSpec(
        num_scalar_prefetch=1,
        grid=(1,),
        in_specs=[whole(near.shape), whole(far.shape)]
        + [whole(array.shape) for array in held]
        + [whole(piece.shape) for piece in pieces],
        out_specs=whole((rows, width)),
    )
    return pl.pallas_call(
        functools.partial(product_kernel, len(pieces), len(held)),
        grid_spec=spec,
        out_shape=jax.ShapeDtypeStruct((rows, width), F32),
        compiler_params=params("arbitrary"),
        cost_estimate=cost(2 * rows * width * near.shape[1], 3),
        name="product_part",
    )(core, near, far, *held, *pieces)


def grad_kernel(
    blocks, first, heads, core_ref, near_ref, far_ref, earlier_ref, up_ref, down_ref, gain_ref, hat_ref,
    slope_ref, cum_ref, pattern_ref, c_ref, *rest,
):
    pieces, (grad_ref, block_grad_ref, total_ref) = rest[:-3], rest[-3:]
    weights = joined(pieces)
    gain = gain_ref[...]
    later = None
    for block in reversed(range(blocks)):
        rows = slice(block * Q, (block + 1) * Q)
        local = slice(block % (blocks // 2) * Q, (block % (blocks // 2) + 1) * Q)
        cot = jnp.where(
            core_ref[0] == block // (blocks // 2), near_ref[local, :], far_ref[local, :]
        )
        product = dot(cot, weights) + dot(up_ref[rows, :], down_ref[...]) + earlier_ref[rows, :]
        weighted = product * gain
        hat = hat_ref[rows, :].astype(F32)
        mean = jnp.mean(hat * weighted, axis=1, keepdims=True)
        grad = slope_ref[rows, :] * (weighted - hat * mean)
        grad_ref[rows, :] = grad
        growth = spread(jnp.exp(of_core(cum_ref, rows, core_ref[0], first, heads)), pattern_ref[...])
        fresh = dot(c_ref[rows, :], (growth * grad).astype(BF16), ((0,), (0,)))
        block_grad_ref[block * N : (block + 1) * N, :] = fresh
        later = (
            fresh
            if later is None
            else later * growth[Q - 1 :, :] + fresh
        )
    total_ref[...] = later.astype(BF16)


def grad_part(
    group, groups, heads, core, near, far, earlier, up_twice, down, gain, hat, slope, cum, pattern, c, pieces
):
    rows, width = hat.shape
    rank = down.shape[0]
    blocks = rows // Q
    spec = pltpu.PrefetchScalarGridSpec(
        num_scalar_prefetch=1,
        grid=(1,),
        in_specs=[
            whole(near.shape),
            whole(far.shape),
            whole(earlier.shape),
            whole(up_twice.shape),
            pl.BlockSpec((rank, width), lambda i, s: (0, s[0] * groups + group)),
            pl.BlockSpec((1, width), lambda i, s: (0, s[0] * groups + group)),
            whole(hat.shape),
            whole(slope.shape),
            whole(cum.shape),
            whole(pattern.shape),
            pl.BlockSpec((rows, N), lambda i, s: (0, group)),
        ]
        + [whole(piece.shape) for piece in pieces],
        out_specs=[whole((rows, width)), whole((blocks * N, width)), whole((N, width))],
    )
    return pl.pallas_call(
        functools.partial(grad_kernel, blocks, group * heads, heads),
        grid_spec=spec,
        out_shape=[
            jax.ShapeDtypeStruct((rows, width), F32),
            jax.ShapeDtypeStruct((blocks * N, width), F32),
            jax.ShapeDtypeStruct((N, width), BF16),
        ],
        compiler_params=params("arbitrary"),
        cost_estimate=cost(2 * rows * width * near.shape[1], 7),
        name="grad_part",
    )(
        core, near, far, earlier, up_twice, down, gain, hat, slope, cum, pattern, c,
        *pieces,
    )


def back_kernel(first, heads, core_ref, scores_ref, grad_ref, step_ref, pattern_ref, skip_ref, out_ref):
    step = of_core(step_ref, slice(None), core_ref[0], first, heads)
    out_ref[...] = spread(step, pattern_ref[...])
    for pair in range(heads // 2):
        lanes = slice(pair * 2 * P_SIZE, (pair + 1) * 2 * P_SIZE)
        grad = grad_ref[:, lanes]
        back = dot(
            scores_ref[:, 2 * pair * Q : 2 * (pair + 1) * Q], pair_rows(grad.astype(BF16))
        )
        out_ref[:, lanes] = out_ref[:, lanes] * back + skip_ref[:, lanes] * grad


def back_part(group, groups, heads, core, scores, grad, step, pattern, skip):
    rows, width = grad.shape
    row_block = pl.BlockSpec((Q, width), lambda i, s: (i, 0))
    spec = pltpu.PrefetchScalarGridSpec(
        num_scalar_prefetch=1,
        grid=(rows // Q,),
        in_specs=[
            pl.BlockSpec((Q, heads * Q), lambda i, s: (i, 0)),
            row_block,
            pl.BlockSpec((Q, step.shape[1]), lambda i, s: (i, 0)),
            whole(pattern.shape),
            pl.BlockSpec((1, width), lambda i, s: (0, s[0] * groups + group)),
        ],
        out_specs=row_block,
    )
    return pl.pallas_call(
        functools.partial(back_kernel, group * heads, heads),
        grid_spec=spec,
        out_shape=jax.ShapeDtypeStruct((rows, width), F32),
        compiler_params=params("arbitrary"),
        cost_estimate=cost(rows * width * Q * 2, 8),
        name="back_part",
    )(core, scores, grad, step, pattern, skip)


def cross_kernel(
    blocks, first, heads, core_ref, b_ref, outgoing_ref, block_grad_ref, step_ref, cum_ref, pattern_ref,
    base_ref, near_ref, far_ref,
):
    run = outgoing_ref[...].astype(F32)
    for block in reversed(range(blocks)):
        rows = slice(block * Q, (block + 1) * Q)
        local = slice(block % (blocks // 2) * Q, (block % (blocks // 2) + 1) * Q)
        cross = dot(b_ref[rows, :], run.astype(BF16))
        cum = of_core(cum_ref, rows, core_ref[0], first, heads)
        last = cum[Q - 1 :, :]
        step = of_core(step_ref, rows, core_ref[0], first, heads)
        weight = spread(step * jnp.exp(last - cum), pattern_ref[...])
        value = (base_ref[rows, :] + weight * cross).astype(near_ref.dtype)
        own = core_ref[0] == block // (blocks // 2)

        @pl.when(own)
        def _():
            near_ref[local, :] = value

        @pl.when(jnp.logical_not(own))
        def _():
            far_ref[local, :] = value

        if block > 0:
            states = slice(block * N, (block + 1) * N)
            decay = spread(jnp.broadcast_to(jnp.exp(last), (8, heads)), pattern_ref[...])[:1, :]
            run = run * decay + block_grad_ref[states, :]


def cross_part(group, heads, core, b, outgoing, block_grad, step, cum, pattern, base):
    rows, width = base.shape
    blocks = rows // Q
    spec = pltpu.PrefetchScalarGridSpec(
        num_scalar_prefetch=1,
        grid=(1,),
        in_specs=[
            pl.BlockSpec((rows, N), lambda i, s: (0, group)),
            whole(outgoing.shape),
            whole(block_grad.shape),
            whole(step.shape),
            whole(cum.shape),
            whole(pattern.shape),
            whole(base.shape),
        ],
        out_specs=[whole((rows // 2, width))] * 2,
    )
    return pl.pallas_call(
        functools.partial(cross_kernel, blocks, group * heads, heads),
        grid_spec=spec,
        out_shape=[jax.ShapeDtypeStruct((rows // 2, width), BF16)] * 2,
        compiler_params=params("arbitrary"),
        cost_estimate=cost(rows * width * N * 2, 6),
        name="cross_part",
    )(core, b, outgoing, block_grad, step, cum, pattern, base)


def ring_order(count):
    return list(range(0, count, 2)) + list(range(count - 1 - count % 2, 0, -2))


def rotations(count):
    return [[(i, (i + k) % count) for i in range(count)] for k in range(count)]


def chip_order():
    ring, across = lax.axis_size("dp"), lax.axis_size("x")
    offsets = [0]
    for distance in range(1, (ring - 1) // 2 + 1):
        offsets += [-distance, distance]
    if ring % 2 == 0:
        offsets.append(ring // 2)
    me, x = lax.axis_index("dp"), lax.axis_index("x")
    seat = jnp.where(me % 2 == 0, me // 2, ring - (me + 1) // 2)

    def member(place):
        return jnp.where(place < (ring + 1) // 2, 2 * place, 2 * (ring - place) - 1)

    return [
        [member((seat + offset + ring) % ring) * across + (x - k + across) % across for k in range(across)]
        for offset in offsets
    ]


def ring_perms():
    ring = lax.axis_size("dp")
    order = ring_order(ring)
    ahead = [(order[i], order[(i + 1) % ring]) for i in range(ring)]
    return ahead, [(b, a) for a, b in ahead]


class Gather:
    def __init__(self, shards):
        self.ring = lax.axis_size("dp")
        self.turns = rotations(lax.axis_size("x"))[1:]
        self.perms = ring_perms()
        self.shards = shards
        self.late = (shards[1], shards[1])
        self.early = None
        self.pieces = {}
        self.steps = self.ring // 2 + 2

    def onward(self, arrays, distance):
        if 2 * distance == self.ring:
            half = arrays[0].shape[0] // 2
            arrays = (arrays[0][:half], arrays[1][half:])
        return tuple(lax.ppermute(array, "dp", perm) for array, perm in zip(arrays, self.perms))

    def crossing(self, arrays):
        return [tuple(lax.ppermute(array, "x", turn) for turn in self.turns) for array in arrays]

    def step(self, index, beside):
        early = late = None
        if 2 * index <= self.ring:
            late = self.onward(self.late, index)
        if index == 1:
            crossed = self.crossing(self.shards)
        else:
            early = self.onward(self.early, index - 1)
            crossed = self.crossing(self.late)
        values = beside()
        early, late, crossed, values = lax.optimization_barrier((early, late, crossed, values))
        if index == 1:
            first = jnp.concatenate([self.shards[0], *crossed[0]], axis=0)
            self.early = (first, first)
            self.pieces[0] = [[first], [self.shards[1], *crossed[1]]]
        else:
            distance = index - 1
            if 2 * distance < self.ring:
                for side in range(2):
                    self.pieces[2 * distance - 1 + side] = [
                        [early[side]], [self.late[side], *crossed[side]]
                    ]
            else:
                halves = zip(*[(array, *met) for array, met in zip(self.late, crossed)])
                self.pieces[2 * distance - 1] = [
                    list(early), [array for pair in halves for array in pair]
                ]
            self.early = early
        self.late = late
        return values


def pack_kernel(ring, across, place_ref, first_ref, second_ref, own_ref, far_ref, mine_ref, *sent_refs):
    sums = (first_ref[...], second_ref[...])
    wide = sums[0].shape[1]
    other = own_ref[...] + far_ref[...].astype(F32)
    width_a = 2 * wide // (ring * across)
    width_b = other.shape[1] // (ring * across)
    for member in range(ring):
        blocks = []
        for x in range(across):
            chip = member * across + x
            start = chip * width_a % wide
            part = sums[chip * width_a // wide][:, start : start + width_a]
            blocks.append((part, other[:, chip * width_b : (chip + 1) * width_b]))
        for turn in range(across):
            target = (place_ref[1] + turn) % across
            chosen = blocks[0]
            for x in range(1, across):
                chosen = [jnp.where(target == x, new, old) for new, old in zip(blocks[x], chosen)]
            out = mine_ref if turn == 0 else sent_refs[turn - 1]
            out[member, :, :width_a] = chosen[0].astype(out.dtype)
            out[member, :, width_a:] = chosen[1].astype(out.dtype)


def split_kernel(ring, across, place_ref, mine_ref, *refs):
    arrived, (kept_ref, *sent_refs) = refs[: across - 1], refs[across - 1 :]
    for turn in range(ring):
        member = (place_ref[0] + turn) % ring
        total = mine_ref[member]
        for ref in arrived:
            total = total + ref[member].astype(F32)
        out = kept_ref if turn == 0 else sent_refs[turn - 1]
        out[...] = total.astype(out.dtype)


def total_kernel(width_a, kept_ref, *refs):
    arrived, (total_ref, square_ref) = refs[:-2], refs[-2:]
    total = kept_ref[...]
    for ref in arrived:
        total = total + ref[...].astype(F32)
    total_ref[...] = total
    squares = total * total
    lane = lax.broadcasted_iota(jnp.int32, squares.shape, 1)
    first = jnp.sum(jnp.where(lane < width_a, squares, 0.0))
    second = jnp.sum(jnp.where(lane >= width_a, squares, 0.0))
    column = lax.broadcasted_iota(jnp.int32, square_ref.shape, 1)
    square_ref[...] = jnp.where(column == 0, first, jnp.where(column == 1, second, 0.0))


def small_call(kernel, scalars, arrays, outs, name):
    spec = pltpu.PrefetchScalarGridSpec(
        num_scalar_prefetch=len(scalars),
        grid=(1,),
        in_specs=[whole(array.shape) for array in arrays],
        out_specs=[whole(out.shape) for out in outs],
    )
    return pl.pallas_call(
        kernel,
        grid_spec=spec,
        out_shape=outs,
        compiler_params=params("arbitrary"),
        cost_estimate=cost(10**9, 1),
        name=name,
    )(*scalars, *arrays)


class Sums:
    def __init__(self, sums_a, own_b, far_b):
        self.ring, self.across = lax.axis_size("dp"), lax.axis_size("x")
        self.place = jnp.stack([lax.axis_index("dp"), lax.axis_index("x")]).astype(jnp.int32)
        rank = own_b.shape[0]
        count = self.ring * self.across
        self.width_a = 2 * sums_a[0].shape[1] // count
        self.shape = (rank, self.width_a + own_b.shape[1] // count)
        wide = (self.ring,) + self.shape
        self.mine, *self.sent = small_call(
            functools.partial(pack_kernel, self.ring, self.across),
            [self.place],
            [*sums_a, own_b, far_b],
            [jax.ShapeDtypeStruct(wide, F32)]
            + [jax.ShapeDtypeStruct(wide, BF16)] * (self.across - 1),
            "pack_sums",
        )

    def over_x(self):
        turns = rotations(self.across)[1:]
        arrived = [lax.ppermute(value, "x", turn) for value, turn in zip(self.sent, turns)]
        self.mine, *self.sent = small_call(
            functools.partial(split_kernel, self.ring, self.across),
            [self.place],
            [self.mine, *arrived],
            [jax.ShapeDtypeStruct(self.shape, F32)]
            + [jax.ShapeDtypeStruct(self.shape, BF16)] * (self.ring - 1),
            "split_sums",
        )

    def over_dp(self):
        turns = rotations(self.ring)[1:]
        arrived = [lax.ppermute(value, "dp", turn) for value, turn in zip(self.sent, turns)]
        return small_call(
            functools.partial(total_kernel, self.width_a),
            [],
            [self.mine, *arrived],
            [jax.ShapeDtypeStruct(self.shape, F32), jax.ShapeDtypeStruct((8, 128), F32)],
            "total_sums",
        )


def everywhere(value):
    for axis in ("core", "x", "dp"):
        distance = 1
        while distance < lax.axis_size(axis):
            pairs = [(i, i ^ distance) for i in range(lax.axis_size(axis))]
            value = value + lax.ppermute(value, axis, pairs)
            distance *= 2
    return value


def on_device(
    state_input, gate_values, input_matrix, readout_matrix, step_unbiased, step_bias,
    decay_rate_log, skip_coefficients, norm_gain, adapter_down, adapter_up, projection_weight,
    output_cotangent,
):
    ring, across = lax.axis_size("dp"), lax.axis_size("x")
    core = lax.axis_index("core")
    swap = [(0, 1), (1, 0)]
    near_rows = state_input.shape[0]
    groups = G // 2
    heads = step_bias.shape[0] // G
    width = heads * P_SIZE

    def half(value, which, axis=-1):
        size = value.shape[axis] // 2
        return lax.dynamic_slice_in_dim(value, which * size, size, axis)

    def in_order(near, far, axis=0):
        return jnp.concatenate(
            [jnp.where(core == 0, near, far), jnp.where(core == 0, far, near)], axis=axis
        )

    def both_cores(value):
        far = lax.ppermute(half(value, 1 - core), "core", swap)
        return in_order(half(value, core), far)

    def swapped(value):
        return lax.ppermute(value, "core", swap)

    x_far = swapped(half(state_input, 1 - core))
    raw_far = swapped(step_unbiased)
    shard = both_cores(projection_weight)
    shards = [shard[:, group * width : (group + 1) * width] for group in range(groups)]
    (shards, state_input, gate_values, input_matrix, readout_matrix, step_unbiased, output_cotangent) = (
        lax.optimization_barrier(
            (shards, state_input, gate_values, input_matrix, readout_matrix, step_unbiased, output_cotangent)
        )
    )
    which = core.astype(jnp.int32)[None]
    chips = chip_order()
    chip_rows = shard.shape[0]
    slots = list(range(len(chips)))
    stages = [slots[:3], slots[3:5], slots[5:]] if len(slots) > 5 else [slots[:1], slots[1:]]
    rows = 2 * near_rows
    blocks = rows // Q
    gather = Gather(shards)
    forward = [(i, i + 1) for i in range(across - 1)]
    backward = [(i + 1, i) for i in range(across - 1)]

    def columns(stage):
        return jnp.concatenate(
            [
                lax.dynamic_slice_in_dim(output_cotangent, chip * chip_rows, chip_rows, 1)
                for offset in stage
                for chip in chips[offset]
            ],
            axis=1,
        )

    def staged(index, group):
        return [piece for slot in stages[index] for piece in gather.pieces[slot][group]]

    def carried(fresh, cum, group, perm):
        sent = fresh.astype(BF16)
        for lap in range(across - 1):
            arrived = lax.ppermute(sent, "x", perm)
            if lap + 2 < across:
                total = jnp.sum(cum.reshape(blocks, Q, -1)[:, Q - 1], axis=0)
                decay = jnp.exp(half(total, core)[group * heads : (group + 1) * heads])
                decay = jnp.repeat(decay, P_SIZE)[None, :]
                sent = (arrived.astype(F32) * decay + fresh.astype(F32)).astype(BF16)
        return arrived

    skip = jnp.repeat(skip_coefficients, P_SIZE)[None, :]
    gain = norm_gain[None, :]
    pattern = spread_pattern(heads)

    def inside(group, x_far, b, c, step, cum, cum_t):
        return local_part(
            group, groups, heads, which, state_input, x_far, b, c, step, cum, cum_t, skip, pattern
        )

    def prepare():
        step, cum, cum_t = step_part(
            which, step_unbiased, raw_far, step_bias[None, :], decay_rate_log[None, :]
        )
        b = both_cores(input_matrix)
        c = both_cores(readout_matrix)
        return step, cum, cum_t, b, c, inside(0, x_far, b, c, step, cum, cum_t)

    step, cum, cum_t, b, c, local_first = gather.step(1, prepare)

    def second():
        local_second = inside(1, x_far, b, c, step, cum, cum_t)
        up_near = (
            ADAPTER_SCALE * dot(output_cotangent, adapter_up, ((1,), (1,))).astype(BF16)
        ).astype(BF16)
        near = [columns(stage) for stage in stages]
        return (
            local_second,
            carried(local_first[3], cum, 0, forward),
            in_order(up_near, swapped(up_near)),
            [(part, swapped(part)) for part in near],
            swapped(half(gate_values, 1 - core)),
        )

    local_second, incoming_first, up_twice, cots, z_far = gather.step(2, second)
    local = [local_first, local_second]

    def norm(group, incoming):
        scores, ssd, state, total = local[group]
        return norm_part(
            group, groups, heads, which, c, incoming, state, cum, pattern, ssd, gate_values, z_far, gain,
            adapter_down, up_twice,
        )

    def products(index, earlier):
        return [
            product_part(which, *cots[index], earlier[group], staged(index, group), width)
            for group in range(groups)
        ]

    def third():
        incoming = carried(local[1][3], cum, 1, forward)
        return [norm(0, incoming_first), norm(1, incoming)]

    normed = gather.step(3, third) if gather.steps > 3 else third()
    nothing = [None] * groups

    def lora_down():
        product = functools.reduce(jnp.add, [part[2] for part in normed])
        arrived = swapped(half(product, 1 - core, 0))
        down_product = (half(product, core, 0) + arrived).astype(BF16)
        part_b = ADAPTER_SCALE * dot(down_product, output_cotangent, ((0,), (0,)))
        far_b = swapped(half(part_b, 1 - core).astype(BF16))
        return Sums([part[3] for part in normed], half(part_b, core), far_b)

    def fourth():
        return lora_down(), products(0, nothing)

    sums, earlier = fourth()
    sums.mine, sums.sent, earlier = (
        gather.step(4, lambda: (sums.mine, sums.sent, earlier))
        if gather.steps > 4
        else (sums.mine, sums.sent, earlier)
    )

    def fifth():
        sums.over_x()
        return sums.mine, sums.sent, products(1, earlier) if len(stages) > 2 else earlier

    sums.mine, sums.sent, earlier = gather.step(5, fifth) if gather.steps > 5 else fifth()
    for index in range(6, gather.steps):
        gather.step(index, lambda: ())
    total, squares = sums.over_dp()

    entries = jnp.asarray([sums.width_a, total.shape[1] - sums.width_a], F32)
    entries = entries * (total.shape[0] * ring * across * 2)
    squares = everywhere(squares[:1])[0, :2]
    scale = 1.0 / jnp.maximum(1.0, jnp.sqrt(squares / entries + CLIP_EPSILON))
    count = ring * across
    homes = [
        (chip * 2 + number, number * count + chip) for chip in range(count) for number in range(2)
    ]
    total = lax.ppermute(total, AXES, homes)
    gradient_a = total[:, : sums.width_a] * scale[0]
    gradient_b = total[:, sums.width_a :] * scale[1]

    near, far = [], []
    for group in range(groups):
        hat, slope = normed[group][:2]
        grad, block_grad, grad_total = grad_part(
            group, groups, heads, which, *cots[-1], earlier[group], up_twice, adapter_down, gain, hat, slope,
            cum, pattern, c, staged(len(stages) - 1, group),
        )
        outgoing = carried(grad_total, cum, group, backward)
        base = back_part(group, groups, heads, which, local[group][0], grad, step, pattern, skip)
        own, others = cross_part(
            group, heads, which, b, outgoing, block_grad, step, cum, pattern, base
        )
        far.append(swapped(others))
        near.append(own)
    input_gradient = in_order(
        jnp.concatenate(near, axis=1), jnp.concatenate(far, axis=1), axis=1
    )
    return input_gradient, gradient_a, gradient_b


def solution(mesh):
    ring, ctx = mesh.shape["dp"], mesh.shape["ctx"]
    split = Mesh(mesh.devices.reshape(ring, ctx // 2, 2), AXES)
    rows = P(AXES, None)
    placed = (rows,) * 5 + (P(),) * 6 + (rows,) * 2
    return jax.shard_map(
        on_device,
        mesh=split,
        in_specs=placed,
        out_specs=(rows, P(None, AXES), P(None, AXES)),
        check_vma=False,
    )
```

```python
import functools

import jax
import jax.numpy as jnp
import numpy as np
from jax import lax
from jax.experimental import pallas as pl
from jax.experimental.pallas import tpu as pltpu
from jax.sharding import Mesh
from jax.sharding import PartitionSpec as P

P_SIZE = 64
N = 128
G = 4
Q = 256
EPS_NORM = 1e-05
CLIP_EPSILON = 1e-06
ADAPTER_SCALE = 2.0
VMEM_BYTES = 18 * 1024 * 1024

F32 = jnp.float32
BF16 = jnp.bfloat16
AXES = ("dp", "x", "core")


def dot(a, b, dims=((1,), (0,))):
    return lax.dot_general(a, b, (dims, ((), ())), preferred_element_type=F32)


def spread(values, pattern):
    high = values.astype(BF16).astype(F32)
    rest = values - high
    mid = rest.astype(BF16).astype(F32)
    return dot(jnp.concatenate([high, mid, rest - mid], axis=1).astype(BF16), pattern)


def spread_pattern(heads):
    return np.tile(np.repeat(np.eye(heads), P_SIZE, axis=1), (3, 1)).astype(BF16)


def of_core(ref, rows, core, first, heads):
    half = ref.shape[1] // 2
    return jnp.where(
        core == 0, ref[rows, first : first + heads], ref[rows, half + first : half + first + heads]
    )


def pair_rows(pair):
    lane = lax.broadcasted_iota(jnp.int32, pair.shape, 1)
    zero = jnp.zeros_like(pair)
    return jnp.concatenate(
        [jnp.where(lane < P_SIZE, pair, zero), jnp.where(lane >= P_SIZE, pair, zero)], axis=0
    )


def whole(shape):
    return pl.BlockSpec(shape, lambda *_: (0,) * len(shape))


def cost(flops, slowdown):
    return pl.CostEstimate(flops=flops * slowdown, bytes_accessed=0, transcendentals=0)


def params(*semantics):
    return pltpu.CompilerParams(
        dimension_semantics=semantics or None, vmem_limit_bytes=VMEM_BYTES
    )


def step_kernel(blocks, core_ref, near_ref, far_ref, bias_ref, rate_ref, step_ref, cum_ref, cum_t_ref):
    lower = lax.broadcasted_iota(jnp.int32, (Q, Q), 0) >= lax.broadcasted_iota(
        jnp.int32, (Q, Q), 1
    )
    for block in range(blocks):
        rows = slice(block * Q, (block + 1) * Q)
        local = slice(block % (blocks // 2) * Q, (block % (blocks // 2) + 1) * Q)
        raw = jnp.where(
            core_ref[0] == block // (blocks // 2), near_ref[local, :], far_ref[local, :]
        )
        raw = raw + bias_ref[...]
        step = jnp.maximum(raw, 0.0) + jnp.log1p(jnp.exp(-jnp.abs(raw)))
        cum = lax.dot_general(
            lower.astype(F32),
            -jnp.exp(rate_ref[...]) * step,
            (((1,), (0,)), ((), ())),
            precision=lax.Precision.HIGHEST,
            preferred_element_type=F32,
        )
        step_ref[rows, :] = step
        cum_ref[rows, :] = cum
        cum_t_ref[block] = cum.T


def step_part(core, near, far, bias, rate):
    rows, heads = 2 * near.shape[0], near.shape[1]
    spec = pltpu.PrefetchScalarGridSpec(
        num_scalar_prefetch=1,
        grid=(1,),
        in_specs=[whole(near.shape), whole(far.shape), whole(bias.shape), whole(rate.shape)],
        out_specs=[whole((rows, heads)), whole((rows, heads)), whole((rows // Q, heads, Q))],
    )
    return pl.pallas_call(
        functools.partial(step_kernel, rows // Q),
        grid_spec=spec,
        out_shape=[
            jax.ShapeDtypeStruct((rows, heads), F32),
            jax.ShapeDtypeStruct((rows, heads), F32),
            jax.ShapeDtypeStruct((rows // Q, heads, Q), F32),
        ],
        compiler_params=params("arbitrary"),
        cost_estimate=cost(rows * heads * Q, 200),
        name="step_part",
    )(core, near, far, bias, rate)


def local_kernel(
    first, heads, core_ref, near_ref, far_ref, b_ref, c_ref, step_ref, cum_ref, cum_t_ref, skip_ref,
    pattern_ref, scores_ref, ssd_ref, state_ref, total_ref, x_ref,
):
    block = pl.program_id(0)
    core = core_ref[0]
    x_ref[...] = jnp.where(
        block // (pl.num_programs(0) // 2) == core, near_ref[...], far_ref[...]
    )
    pattern = pattern_ref[...]
    step = of_core(step_ref, slice(None), core, first, heads)
    cum = of_core(cum_ref, slice(None), core, first, heads)
    start = pl.multiple_of(core * (cum_t_ref.shape[1] // 2) + first, 8)
    cum_t = cum_t_ref[0, pl.ds(start, heads), :]
    last = cum[Q - 1 : Q, :]
    step_wide = spread(step, pattern)
    weight = spread(step * jnp.exp(last - cum), pattern)
    decay = spread(jnp.broadcast_to(jnp.exp(last), (8, heads)), pattern)[:1, :]
    x = x_ref[...].astype(F32)
    xdt = (x * step_wide).astype(BF16)
    state = dot(b_ref[...], (x * weight).astype(BF16), ((0,), (0,)))
    state_ref[...] = state

    @pl.when(block == 0)
    def _():
        total_ref[...] = state

    @pl.when(block > 0)
    def _():
        total_ref[...] = total_ref[...] * decay + state

    inner = dot(b_ref[...], c_ref[...], ((1,), (1,)))
    causal = lax.broadcasted_iota(jnp.int32, (Q, Q), 1) >= lax.broadcasted_iota(
        jnp.int32, (Q, Q), 0
    )
    masked = jnp.where(causal, inner, 0.0)
    for pair in range(heads // 2):
        parts = []
        for head in (2 * pair, 2 * pair + 1):
            gap = cum_t[head : head + 1, :] - cum[:, head : head + 1]
            part = (masked * jnp.exp(jnp.where(causal, gap, 0.0))).astype(BF16)
            scores_ref[:, head * Q : (head + 1) * Q] = part
            parts.append(part)
        lanes = slice(pair * 2 * P_SIZE, (pair + 1) * 2 * P_SIZE)
        intra = dot(jnp.concatenate(parts, axis=0), pair_rows(xdt[:, lanes]), ((0,), (0,)))
        ssd_ref[:, lanes] = (
            intra + skip_ref[:, lanes] * x_ref[:, lanes].astype(F32)
        ).astype(ssd_ref.dtype)


def local_part(group, groups, heads, core, near, far, b, c, step, cum, cum_t, skip, pattern):
    rows = 2 * near.shape[0]
    blocks = rows // Q
    width = heads * P_SIZE
    row_block = pl.BlockSpec((Q, width), lambda i, s: (i, 0))
    spec = pltpu.PrefetchScalarGridSpec(
        num_scalar_prefetch=1,
        grid=(blocks,),
        in_specs=[
            pl.BlockSpec((Q, width), lambda i, s: (i % (blocks // 2), s[0] * groups + group)),
            pl.BlockSpec((Q, width), lambda i, s: (i % (blocks // 2), group)),
            pl.BlockSpec((Q, N), lambda i, s: (i, group)),
            pl.BlockSpec((Q, N), lambda i, s: (i, group)),
            pl.BlockSpec((Q, step.shape[1]), lambda i, s: (i, 0)),
            pl.BlockSpec((Q, step.shape[1]), lambda i, s: (i, 0)),
            pl.BlockSpec((1,) + cum_t.shape[1:], lambda i, s: (i, 0, 0)),
            pl.BlockSpec((1, width), lambda i, s: (0, s[0] * groups + group)),
            whole(pattern.shape),
        ],
        out_specs=[
            pl.BlockSpec((Q, heads * Q), lambda i, s: (i, 0)),
            row_block,
            pl.BlockSpec((N, width), lambda i, s: (i, 0)),
            pl.BlockSpec((N, width), lambda i, s: (0, 0)),
        ],
        scratch_shapes=[pltpu.VMEM((Q, width), BF16)],
    )
    return pl.pallas_call(
        functools.partial(local_kernel, group * heads, heads),
        grid_spec=spec,
        out_shape=[
            pltpu.HBM((rows, heads * Q), BF16),
            jax.ShapeDtypeStruct((rows, width), BF16),
            jax.ShapeDtypeStruct((blocks * N, width), F32),
            jax.ShapeDtypeStruct((N, width), F32),
        ],
        compiler_params=params("arbitrary"),
        cost_estimate=cost(rows * width * Q * 4, 18),
        name="local_part",
    )(core, near, far, b, c, step, cum, cum_t, skip, pattern)


def norm_kernel(
    blocks, first, heads, core_ref, c_ref, incoming_ref, state_ref, cum_ref, pattern_ref, ssd_ref, near_ref,
    far_ref, gain_ref, down_ref, up_ref, hat_ref, slope_ref, product_ref, sum_ref,
):
    gain = gain_ref[...]
    run = incoming_ref[...].astype(F32)
    total = None
    for block in range(blocks):
        rows = slice(block * Q, (block + 1) * Q)
        inter = dot(c_ref[rows, :], run.astype(BF16))
        growth = spread(jnp.exp(of_core(cum_ref, rows, core_ref[0], first, heads)), pattern_ref[...])
        ssd = ssd_ref[rows, :].astype(F32) + growth * inter
        local = slice(block % (blocks // 2) * Q, (block % (blocks // 2) + 1) * Q)
        z = jnp.where(
            core_ref[0] == block // (blocks // 2), near_ref[local, :], far_ref[local, :]
        ).astype(F32)
        silu = z / (1.0 + jnp.exp(-z))
        gated = ssd * silu
        rstd = lax.rsqrt(jnp.mean(gated * gated, axis=1, keepdims=True) + EPS_NORM)
        hat = gated * rstd
        normed = (hat * gain).astype(BF16)
        hat_ref[rows, :] = hat.astype(hat_ref.dtype)
        slope_ref[rows, :] = (rstd * silu).astype(slope_ref.dtype)
        product_ref[rows, :] = dot(normed, down_ref[...], ((1,), (1,)))
        part = dot(up_ref[rows, :], normed, ((0,), (0,)))
        total = part if total is None else total + part
        if block + 1 < blocks:
            states = slice(block * N, (block + 1) * N)
            run = run * growth[Q - 1 :, :] + state_ref[states, :]
    sum_ref[...] = total


def norm_part(
    group, groups, heads, core, c, incoming, state, cum, pattern, ssd, near, far, gain, down, up_twice
):
    rows, width = ssd.shape
    rank = down.shape[0]
    blocks = rows // Q
    spec = pltpu.PrefetchScalarGridSpec(
        num_scalar_prefetch=1,
        grid=(1,),
        in_specs=[
            pl.BlockSpec((rows, N), lambda i, s: (0, group)),
            pl.BlockSpec((N, width), lambda i, s: (group, 0)),
            whole(state.shape),
            whole(cum.shape),
            whole(pattern.shape),
            whole(ssd.shape),
            pl.BlockSpec((rows // 2, width), lambda i, s: (0, s[0] * groups + group)),
            pl.BlockSpec((rows // 2, width), lambda i, s: (0, group)),
            pl.BlockSpec((1, width), lambda i, s: (0, s[0] * groups + group)),
            pl.BlockSpec((rank, width), lambda i, s: (0, s[0] * groups + group)),
            whole(up_twice.shape),
        ],
        out_specs=[
            whole((rows, width)), whole((rows, width)), whole((rows, rank)), whole((rank, width)),
        ],
    )
    return pl.pallas_call(
        functools.partial(norm_kernel, blocks, group * heads, heads),
        grid_spec=spec,
        out_shape=[
            jax.ShapeDtypeStruct((rows, width), BF16),
            jax.ShapeDtypeStruct((rows, width), BF16),
            jax.ShapeDtypeStruct((rows, rank), F32),
            jax.ShapeDtypeStruct((rank, width), F32),
        ],
        compiler_params=params("arbitrary"),
        cost_estimate=cost(rows * width * 512, 14),
        name="norm_part",
    )(core, c, incoming, state, cum, pattern, ssd, near, far, gain, down, up_twice)


def product_kernel(first, spans, started, core_ref, near_ref, far_ref, *rest):
    pieces, out_ref = rest[started:-1], rest[-1]
    weights = joined(pieces, spans)
    depth = slice(first, first + weights.shape[0])
    half = near_ref.shape[0]
    for part in range(2):
        rows = slice(part * half, (part + 1) * half)
        cot = jnp.where(core_ref[0] == part, near_ref[:, depth], far_ref[:, depth])
        product = dot(cot, weights)
        out_ref[rows, :] = product + rest[0][rows, :] if started else product


def joined(pieces, spans):
    return jnp.concatenate(
        [piece[start : start + rows, :] for piece, (start, rows) in zip(pieces, spans)], axis=0
    )


def product_part(core, near, far, cut, first, earlier, pieces, width):
    rows = 2 * near.shape[0]
    held = [] if earlier is None else [earlier]
    columns = pl.BlockSpec((near.shape[0], cut), lambda i, s: (0, near.shape[1] // cut - 1))
    spec = pltpu.PrefetchScalarGridSpec(
        num_scalar_prefetch=1,
        grid=(1,),
        in_specs=[columns, columns]
        + [whole(array.shape) for array in held]
        + [whole(piece[0].shape) for piece in pieces],
        out_specs=whole((rows, width)),
    )
    return pl.pallas_call(
        functools.partial(product_kernel, first, tuple(piece[1:] for piece in pieces), len(held)),
        grid_spec=spec,
        out_shape=jax.ShapeDtypeStruct((rows, width), F32),
        compiler_params=params("arbitrary"),
        cost_estimate=cost(2 * rows * width * Q, 4),
        name="product_part",
    )(core, near, far, *held, *[piece[0] for piece in pieces])


def grad_kernel(
    blocks, first, heads, start, spans, core_ref, near_ref, far_ref, earlier_ref, up_ref, down_ref, gain_ref, hat_ref,
    slope_ref, cum_ref, pattern_ref, c_ref, *rest,
):
    pieces, (grad_ref, block_grad_ref, total_ref) = rest[:-3], rest[-3:]
    weights = joined(pieces, spans)
    depth = slice(start, start + weights.shape[0])
    gain = gain_ref[...]
    later = None
    for block in reversed(range(blocks)):
        rows = slice(block * Q, (block + 1) * Q)
        local = slice(block % (blocks // 2) * Q, (block % (blocks // 2) + 1) * Q)
        cot = jnp.where(
            core_ref[0] == block // (blocks // 2), near_ref[local, depth], far_ref[local, depth]
        )
        product = dot(cot, weights) + dot(up_ref[rows, :], down_ref[...]) + earlier_ref[rows, :]
        weighted = product * gain
        hat = hat_ref[rows, :].astype(F32)
        mean = jnp.mean(hat * weighted, axis=1, keepdims=True)
        grad = slope_ref[rows, :].astype(F32) * (weighted - hat * mean)
        grad_ref[rows, :] = grad.astype(grad_ref.dtype)
        growth = spread(jnp.exp(of_core(cum_ref, rows, core_ref[0], first, heads)), pattern_ref[...])
        fresh = dot(c_ref[rows, :], (growth * grad).astype(BF16), ((0,), (0,)))
        block_grad_ref[block * N : (block + 1) * N, :] = fresh
        later = (
            fresh
            if later is None
            else later * growth[Q - 1 :, :] + fresh
        )
    total_ref[...] = later.astype(BF16)


def grad_part(
    group, groups, heads, core, near, far, cut, start, earlier, up_twice, down, gain, hat, slope, cum, pattern, c, pieces
):
    rows, width = hat.shape
    rank = down.shape[0]
    blocks = rows // Q
    columns = pl.BlockSpec((near.shape[0], cut), lambda i, s: (0, near.shape[1] // cut - 1))
    spec = pltpu.PrefetchScalarGridSpec(
        num_scalar_prefetch=1,
        grid=(1,),
        in_specs=[
            columns,
            columns,
            whole(earlier.shape),
            whole(up_twice.shape),
            pl.BlockSpec((rank, width), lambda i, s: (0, s[0] * groups + group)),
            pl.BlockSpec((1, width), lambda i, s: (0, s[0] * groups + group)),
            whole(hat.shape),
            whole(slope.shape),
            whole(cum.shape),
            whole(pattern.shape),
            pl.BlockSpec((rows, N), lambda i, s: (0, group)),
        ]
        + [whole(piece[0].shape) for piece in pieces],
        out_specs=[whole((rows, width)), whole((blocks * N, width)), whole((N, width))],
    )
    return pl.pallas_call(
        functools.partial(
            grad_kernel, blocks, group * heads, heads, start, tuple(piece[1:] for piece in pieces)
        ),
        grid_spec=spec,
        out_shape=[
            jax.ShapeDtypeStruct((rows, width), BF16),
            jax.ShapeDtypeStruct((blocks * N, width), F32),
            jax.ShapeDtypeStruct((N, width), BF16),
        ],
        compiler_params=params("arbitrary"),
        cost_estimate=cost(2 * rows * width * Q, 8),
        name="grad_part",
    )(
        core, near, far, earlier, up_twice, down, gain, hat, slope, cum, pattern, c,
        *[piece[0] for piece in pieces],
    )


def back_kernel(first, heads, core_ref, scores_ref, grad_ref, step_ref, pattern_ref, skip_ref, out_ref):
    step = of_core(step_ref, slice(None), core_ref[0], first, heads)
    out_ref[...] = spread(step, pattern_ref[...])
    for pair in range(heads // 2):
        lanes = slice(pair * 2 * P_SIZE, (pair + 1) * 2 * P_SIZE)
        grad = grad_ref[:, lanes]
        back = dot(
            scores_ref[:, 2 * pair * Q : 2 * (pair + 1) * Q], pair_rows(grad)
        )
        out_ref[:, lanes] = out_ref[:, lanes] * back + skip_ref[:, lanes] * grad.astype(F32)


def back_part(group, groups, heads, core, scores, grad, step, pattern, skip):
    rows, width = grad.shape
    row_block = pl.BlockSpec((Q, width), lambda i, s: (i, 0))
    spec = pltpu.PrefetchScalarGridSpec(
        num_scalar_prefetch=1,
        grid=(rows // Q,),
        in_specs=[
            pl.BlockSpec((Q, heads * Q), lambda i, s: (i, 0)),
            row_block,
            pl.BlockSpec((Q, step.shape[1]), lambda i, s: (i, 0)),
            whole(pattern.shape),
            pl.BlockSpec((1, width), lambda i, s: (0, s[0] * groups + group)),
        ],
        out_specs=row_block,
    )
    return pl.pallas_call(
        functools.partial(back_kernel, group * heads, heads),
        grid_spec=spec,
        out_shape=jax.ShapeDtypeStruct((rows, width), F32),
        compiler_params=params("arbitrary"),
        cost_estimate=cost(rows * width * Q * 2, 8),
        name="back_part",
    )(core, scores, grad, step, pattern, skip)


def cross_kernel(
    blocks, first, heads, core_ref, b_ref, outgoing_ref, block_grad_ref, step_ref, cum_ref, pattern_ref,
    base_ref, near_ref, far_ref,
):
    run = outgoing_ref[...].astype(F32)
    for block in reversed(range(blocks)):
        rows = slice(block * Q, (block + 1) * Q)
        local = slice(block % (blocks // 2) * Q, (block % (blocks // 2) + 1) * Q)
        cross = dot(b_ref[rows, :], run.astype(BF16))
        cum = of_core(cum_ref, rows, core_ref[0], first, heads)
        last = cum[Q - 1 :, :]
        step = of_core(step_ref, rows, core_ref[0], first, heads)
        weight = spread(step * jnp.exp(last - cum), pattern_ref[...])
        value = (base_ref[rows, :] + weight * cross).astype(near_ref.dtype)
        own = core_ref[0] == block // (blocks // 2)

        @pl.when(own)
        def _():
            near_ref[local, :] = value

        @pl.when(jnp.logical_not(own))
        def _():
            far_ref[local, :] = value

        if block > 0:
            states = slice(block * N, (block + 1) * N)
            decay = spread(jnp.broadcast_to(jnp.exp(last), (8, heads)), pattern_ref[...])[:1, :]
            run = run * decay + block_grad_ref[states, :]


def cross_part(group, heads, core, b, outgoing, block_grad, step, cum, pattern, base):
    rows, width = base.shape
    blocks = rows // Q
    spec = pltpu.PrefetchScalarGridSpec(
        num_scalar_prefetch=1,
        grid=(1,),
        in_specs=[
            pl.BlockSpec((rows, N), lambda i, s: (0, group)),
            whole(outgoing.shape),
            whole(block_grad.shape),
            whole(step.shape),
            whole(cum.shape),
            whole(pattern.shape),
            whole(base.shape),
        ],
        out_specs=[whole((rows // 2, width))] * 2,
    )
    return pl.pallas_call(
        functools.partial(cross_kernel, blocks, group * heads, heads),
        grid_spec=spec,
        out_shape=[jax.ShapeDtypeStruct((rows // 2, width), BF16)] * 2,
        compiler_params=params("arbitrary"),
        cost_estimate=cost(rows * width * N * 2, 6),
        name="cross_part",
    )(core, b, outgoing, block_grad, step, cum, pattern, base)


def ring_order(count):
    return list(range(0, count, 2)) + list(range(count - 1 - count % 2, 0, -2))


def rotations(count):
    return [[(i, (i + k) % count) for i in range(count)] for k in range(count)]


def chip_order():
    ring, across = lax.axis_size("dp"), lax.axis_size("x")
    offsets = [0]
    for distance in range(1, (ring - 1) // 2 + 1):
        offsets += [-distance, distance]
    if ring % 2 == 0:
        offsets.append(ring // 2)
    me, x = lax.axis_index("dp"), lax.axis_index("x")
    seat = jnp.where(me % 2 == 0, me // 2, ring - (me + 1) // 2)

    def member(place):
        return jnp.where(place < (ring + 1) // 2, 2 * place, 2 * (ring - place) - 1)

    return [
        [member((seat + offset + ring) % ring) * across + (x - k + across) % across for k in range(across)]
        for offset in offsets
    ]


def ring_perms():
    ring = lax.axis_size("dp")
    order = ring_order(ring)
    ahead = [(order[i], order[(i + 1) % ring]) for i in range(ring)]
    return ahead, [(b, a) for a, b in ahead]


def cut_kernel(plans, count, *refs):
    arrays, outs = refs[:count], refs[count:]
    for out, plan in zip(outs, plans):
        row = 0
        for index, start, rows, column in plan:
            out[row : row + rows, :] = arrays[index][
                start : start + rows, column : column + out.shape[1]
            ]
            row += rows


def cut(arrays, plans, width):
    return small_call(
        functools.partial(cut_kernel, plans, len(arrays)),
        [],
        arrays,
        [
            jax.ShapeDtypeStruct((sum(part[2] for part in plan), width), arrays[0].dtype)
            for plan in plans
        ],
        "cut_rows",
    )


class Gather:
    def __init__(self, shard):
        self.ring = lax.axis_size("dp")
        self.across = lax.axis_size("x")
        self.turns = rotations(self.across)[1:]
        self.perms = ring_perms()
        self.shard = shard
        self.size = shard.shape[0]
        self.width = shard.shape[1] // 2
        late = shard[:, self.width :]
        self.late = [(late, 0, self.size)] * 2
        self.moving = [late, late]
        self.crossing = shard
        self.pieces = {}
        self.steps = self.ring // 2 + 2

    def sizes(self, index):
        early = 0 if index == 1 else self.across * self.size
        late = self.size
        if 2 * index == self.ring:
            late //= 2
        elif 2 * index > self.ring:
            early, late = early // 2, 0
        return early, late

    def step(self, index, beside):
        ring, size, width = self.ring, self.size, self.width
        early_size, late_size = self.sizes(index)
        got = tuple(lax.ppermute(array, "dp", perm) for array, perm in zip(self.moving, self.perms))
        crossed = tuple(lax.ppermute(self.crossing, "x", turn) for turn in self.turns)
        values = beside()
        got, crossed, values = lax.optimization_barrier((got, crossed, values))
        late = [(got[0], early_size, late_size), (got[1], 0, late_size)]
        early = [(got[0], 0, early_size), (got[1], late_size, early_size)]
        after_early, after_late = self.sizes(index + 1)
        more = index + 1 < self.steps
        if index == 1:
            first = [(0, 0, size, 0)] + [(1 + k, 0, size, 0) for k in range(len(crossed))]
            base = 1 + len(crossed)
            self.first, *rest = cut(
                [self.shard, *crossed, *got],
                [
                    first,
                    first + [(base, 0, after_late, 0)],
                    [(base + 1, size - after_late, after_late, 0)] + first,
                    [(base, 0, size, 0), (base + 1, 0, size, 0)],
                ],
                width,
            )
            self.moving, self.crossing = rest[:2], rest[2]
            met = [array[:, width:] for array in crossed]
            self.pieces[0] = [
                [(self.first, 0, self.first.shape[0])],
                [self.late[0]] + [(array, 0, size) for array in met],
            ]
        else:
            distance = index - 1
            if 2 * distance < ring:
                for side in range(2):
                    self.pieces[2 * distance - 1 + side] = [
                        [early[side]],
                        [self.late[side]] + [(array, side * size, size) for array in crossed],
                    ]
            else:
                self.pieces[2 * distance - 1] = [
                    early, self.late + [(array, 0, size) for array in crossed]
                ]
            if more:
                plans = [[(0, early_size, late_size, 0), (1, 0, late_size, 0)]]
                whole_array = (after_early, after_late) == (early_size, late_size)
                if not whole_array:
                    plans += [
                        [(0, 0, after_early, 0), (0, early_size, after_late, 0)],
                        [
                            (1, late_size - after_late, after_late, 0),
                            (1, late_size + early_size - after_early, after_early, 0),
                        ],
                    ]
                plans = [[part for part in plan if part[2]] for plan in plans]
                self.crossing, *moving = cut(list(got), plans, width)
                self.moving = moving or list(got)
        self.late = late
        return values


def down_kernel(core_ref, product_ref, arrived_ref, cot_ref, own_ref, sent_ref):
    down = (product_ref[...] + arrived_ref[...]).astype(BF16)
    half = own_ref.shape[1]
    parts = [
        ADAPTER_SCALE * dot(down, cot_ref[:, part * half : (part + 1) * half], ((0,), (0,)))
        for part in range(2)
    ]
    own_ref[...] = jnp.where(core_ref[0] == 0, parts[0], parts[1])
    sent_ref[...] = jnp.where(core_ref[0] == 0, parts[1], parts[0]).astype(sent_ref.dtype)


def down_part(core, product, arrived, cot):
    shape = (product.shape[1], cot.shape[1] // 2)
    return small_call(
        down_kernel,
        [core],
        [product, arrived, cot],
        [jax.ShapeDtypeStruct(shape, F32), jax.ShapeDtypeStruct(shape, BF16)],
        "down_part",
    )


def pack_kernel(ring, across, place_ref, first_ref, second_ref, own_ref, far_ref, mine_ref, *sent_refs):
    sums = (first_ref[...], second_ref[...])
    wide = sums[0].shape[1]
    other = own_ref[...] + far_ref[...].astype(F32)
    width_a = 2 * wide // (ring * across)
    width_b = other.shape[1] // (ring * across)
    for member in range(ring):
        blocks = []
        for x in range(across):
            chip = member * across + x
            start = chip * width_a % wide
            part = sums[chip * width_a // wide][:, start : start + width_a]
            blocks.append((part, other[:, chip * width_b : (chip + 1) * width_b]))
        for turn in range(across):
            target = (place_ref[1] + turn) % across
            chosen = blocks[0]
            for x in range(1, across):
                chosen = [jnp.where(target == x, new, old) for new, old in zip(blocks[x], chosen)]
            out = mine_ref if turn == 0 else sent_refs[turn - 1]
            out[member, :, :width_a] = chosen[0].astype(out.dtype)
            out[member, :, width_a:] = chosen[1].astype(out.dtype)


def halve_kernel(bit_ref, mine_ref, *refs):
    arrived, (kept_ref, sent_ref) = refs[:-2], refs[-2:]
    half = kept_ref.shape[0]
    for out, start in ((kept_ref, bit_ref[0] * half), (sent_ref, (1 - bit_ref[0]) * half)):
        total = mine_ref[pl.ds(start, half)]
        for ref in arrived:
            total = total + ref[pl.ds(start, half)].astype(F32)
        out[...] = total.astype(out.dtype)


def add_kernel(mine_ref, arrived_ref, total_ref, sent_ref):
    total = mine_ref[...] + arrived_ref[...].astype(F32)
    total_ref[...] = total
    sent_ref[...] = total.astype(sent_ref.dtype)


def total_kernel(width_a, place_ref, mine_ref, arrived_ref, total_ref, square_ref):
    total = mine_ref[...] + arrived_ref[...].astype(F32)
    squares = total * total
    lane = lax.broadcasted_iota(jnp.int32, squares.shape, 2)
    first = jnp.sum(jnp.where(lane < width_a, squares, 0.0))
    second = jnp.sum(jnp.where(lane >= width_a, squares, 0.0))
    column = lax.broadcasted_iota(jnp.int32, square_ref.shape, 1)
    square_ref[...] = jnp.where(column == 0, first, jnp.where(column == 1, second, 0.0))
    own = place_ref[0] % mine_ref.shape[0]
    total_ref[...] = mine_ref[own] + arrived_ref[own].astype(F32)


def small_call(kernel, scalars, arrays, outs, name):
    spec = pltpu.PrefetchScalarGridSpec(
        num_scalar_prefetch=len(scalars),
        grid=(1,),
        in_specs=[whole(array.shape) for array in arrays],
        out_specs=[whole(out.shape) for out in outs],
    )
    return pl.pallas_call(
        kernel,
        grid_spec=spec,
        out_shape=outs,
        compiler_params=params("arbitrary"),
        cost_estimate=cost(10**9, 1),
        name=name,
    )(*scalars, *arrays)


def packed(sums_a, own_b, far_b):
    ring, across = lax.axis_size("dp"), lax.axis_size("x")
    place = jnp.stack([lax.axis_index("dp"), lax.axis_index("x")]).astype(jnp.int32)
    count = ring * across
    shape = (ring, own_b.shape[0], (2 * sums_a[0].shape[1] + own_b.shape[1]) // count)
    mine, *sent = small_call(
        functools.partial(pack_kernel, ring, across),
        [place],
        [*sums_a, own_b, far_b],
        [jax.ShapeDtypeStruct(shape, F32)] + [jax.ShapeDtypeStruct(shape, BF16)] * (across - 1),
        "pack_sums",
    )
    return mine, sent


def halved(mine, arrived, distance):
    shape = (distance,) + mine.shape[1:]
    return small_call(
        halve_kernel,
        [((lax.axis_index("dp") // distance) % 2).astype(jnp.int32)[None]],
        [mine, *arrived],
        [jax.ShapeDtypeStruct(shape, F32), jax.ShapeDtypeStruct(shape, BF16)],
        "halve_sums",
    )


def over_x(sent):
    return [lax.ppermute(value, "x", turn) for value, turn in zip(sent, rotations(lax.axis_size("x"))[1:])]


def far_in_dp(value, distance):
    return lax.ppermute(value, "dp", [(i, i ^ distance) for i in range(lax.axis_size("dp"))])


def added(mine, arrived):
    return small_call(
        add_kernel,
        [],
        [mine, arrived],
        [jax.ShapeDtypeStruct(mine.shape, F32), jax.ShapeDtypeStruct(mine.shape, BF16)],
        "add_sums",
    )


def totals(mine, arrived, width_a):
    return small_call(
        functools.partial(total_kernel, width_a),
        [lax.axis_index("dp").astype(jnp.int32)[None]],
        [mine, arrived],
        [jax.ShapeDtypeStruct(mine.shape[1:], F32), jax.ShapeDtypeStruct((8, 128), F32)],
        "total_sums",
    )


def everywhere(value, distance):
    value = value + far_in_dp(value, distance)
    for axis in ("core", "x"):
        turns = rotations(lax.axis_size(axis))[1:]
        value = functools.reduce(jnp.add, [lax.ppermute(value, axis, turn) for turn in turns], value)
    return value


def on_device(
    state_input, gate_values, input_matrix, readout_matrix, step_unbiased, step_bias,
    decay_rate_log, skip_coefficients, norm_gain, adapter_down, adapter_up, projection_weight,
    output_cotangent,
):
    ring, across = lax.axis_size("dp"), lax.axis_size("x")
    core = lax.axis_index("core")
    swap = [(0, 1), (1, 0)]
    near_rows = state_input.shape[0]
    groups = G // 2
    heads = step_bias.shape[0] // G
    width = heads * P_SIZE

    def half(value, which, axis=-1):
        size = value.shape[axis] // 2
        return lax.dynamic_slice_in_dim(value, which * size, size, axis)

    def in_order(near, far, axis=0):
        return jnp.concatenate(
            [jnp.where(core == 0, near, far), jnp.where(core == 0, far, near)], axis=axis
        )

    def swapped(value):
        return lax.ppermute(value, "core", swap)

    sent_weight = half(projection_weight, 1 - core)
    sent_weight, state_input, step_unbiased, input_matrix, readout_matrix = lax.optimization_barrier(
        (sent_weight, state_input, step_unbiased, input_matrix, readout_matrix)
    )
    shard = in_order(half(projection_weight, core), swapped(sent_weight))
    raw_far = swapped(step_unbiased)
    x_far = swapped(
        jnp.concatenate(
            [half(value, 1 - core) for value in (state_input, input_matrix, readout_matrix)], axis=1
        )
    )
    shard, gate_values, output_cotangent = lax.optimization_barrier(
        (shard, gate_values, output_cotangent)
    )
    which = core.astype(jnp.int32)[None]
    chips = chip_order()
    chip_rows = shard.shape[0]
    slots = list(range(len(chips)))
    stages = [slots[:3], slots[3:5], slots[5:7], slots[7:]] if len(slots) > 7 else [slots[:1], slots[1:]]
    rows = 2 * near_rows
    blocks = rows // Q
    gather = Gather(shard)
    forward = [(i, i + 1) for i in range(across - 1)]
    backward = [(i + 1, i) for i in range(across - 1)]

    def staged(index, group):
        return [piece for slot in stages[index] for piece in gather.pieces[slot][group]]

    def depth(index):
        return sum(len(stage) for stage in stages[:index]) * across * chip_rows

    def carried(fresh, cum, perm, group=None):
        sent = fresh
        for lap in range(across - 1):
            arrived = lax.ppermute(sent, "x", perm)
            if lap + 2 < across:
                total = jnp.sum(cum.reshape(blocks, Q, -1)[:, Q - 1], axis=0)
                decay = jnp.repeat(jnp.exp(half(total, core)).reshape(groups, 1, heads), P_SIZE, axis=2)
                if group is not None:
                    decay = decay[group : group + 1]
                parts = [value.astype(F32).reshape(-1, N, width) for value in (arrived, fresh)]
                sent = (parts[0] * decay + parts[1]).astype(BF16).reshape(fresh.shape)
        return arrived

    skip = jnp.repeat(skip_coefficients, P_SIZE)[None, :]
    gain = norm_gain[None, :]
    pattern = spread_pattern(heads)

    def inside(group, x_far, b, c, step, cum, cum_t):
        return local_part(
            group, groups, heads, which, state_input, x_far, b, c, step, cum, cum_t, skip, pattern
        )

    def prepare():
        step, cum, cum_t = step_part(
            which, step_unbiased, raw_far, step_bias[None, :], decay_rate_log[None, :]
        )
        cut = groups * width
        b = in_order(half(input_matrix, core), x_far[:, cut : cut + groups * N])
        c = in_order(half(readout_matrix, core), x_far[:, cut + groups * N :])
        local = [inside(group, x_far, b, c, step, cum, cum_t) for group in range(groups)]
        return step, cum, cum_t, b, c, local

    step, cum, cum_t, b, c, local = gather.step(1, prepare)

    def second():
        fresh = jnp.concatenate([part[3].astype(BF16) for part in local], axis=0)
        incoming = carried(fresh, cum, forward)
        up_near = (
            ADAPTER_SCALE * dot(output_cotangent, adapter_up, ((1,), (1,))).astype(BF16)
        ).astype(BF16)
        parts = [
            lax.dynamic_slice_in_dim(output_cotangent, chip * chip_rows, chip_rows, 1)
            for offset in chips
            for chip in offset
        ]
        near = jnp.concatenate([half(gate_values, 1 - core)] + parts, axis=1)
        up_twice = in_order(up_near, swapped(up_near))
        far = swapped(near)
        normed = []
        for group in range(groups):
            scores, ssd, state, total = local[group]
            normed.append(
                norm_part(
                    group, groups, heads, which, c, incoming, state, cum, pattern, ssd, gate_values,
                    far, gain, adapter_down, up_twice,
                )
            )
        product = functools.reduce(jnp.add, [part[2] for part in normed])
        far_product = swapped(half(product, 1 - core, 0))
        return up_twice, near, far, normed, half(product, core, 0), far_product

    up_twice, cot_near, cot_far, normed, product, far_product = gather.step(2, second)
    cot_width = output_cotangent.shape[1]

    def during(index, beside):
        return gather.step(index, beside) if gather.steps > index else beside()

    distances = [ring >> k for k in range(1, ring.bit_length())]

    def third():
        own_b, sent_b = down_part(which, product, far_product, output_cotangent)
        mine, sent = packed([part[3] for part in normed], own_b, swapped(sent_b))
        return halved(mine, over_x(sent), distances[0])

    mine, sent = during(3, third)

    def products(indices, earlier):
        for index in indices:
            earlier = [
                product_part(
                    which, cot_near, cot_far, cot_width, depth(index), earlier[group], staged(index, group), width
                )
                for group in range(groups)
            ]
        return earlier

    def doubled(value, rounded, hops):
        for distance in hops:
            value, rounded = added(value, far_in_dp(rounded, distance))
        return value, rounded

    def fourth():
        held = list(range(len(stages) - 1))[:2]
        return doubled(mine, sent, distances[:-2]), products(held, [None] * groups)

    (mine, sent), earlier = during(4, fourth)
    width_a = 2 * width // (ring * across)

    def fifth():
        held = list(range(len(stages) - 1))[2:]
        return doubled(mine, sent, distances[:-1][-1:]), products(held, earlier)

    (mine, sent), earlier = during(5, fifth)
    for index in range(6, gather.steps):
        gather.step(index, lambda: ())
    total, squares = totals(mine, far_in_dp(sent, distances[-1]), width_a)

    grads = [
        grad_part(
            group, groups, heads, which, cot_near, cot_far, cot_width, depth(len(stages) - 1), earlier[group],
            up_twice, adapter_down, gain, *normed[group][:2], cum, pattern, c, staged(len(stages) - 1, group),
        )
        for group in range(groups)
    ]
    outgoing = [carried(part[2], cum, backward, group) for group, part in enumerate(grads)]
    bases = [
        back_part(group, groups, heads, which, local[group][0], grads[group][0], step, pattern, skip)
        for group in range(groups)
    ]
    near, far = [], []
    for group in range(groups):
        own, others = cross_part(
            group, heads, which, b, outgoing[group], grads[group][1], step, cum, pattern, bases[group]
        )
        far.append(swapped(others))
        near.append(own)
    entries = jnp.asarray([width_a, total.shape[1] - width_a], F32)
    entries = entries * (total.shape[0] * ring * across * 2)
    count = ring * across
    homes = [
        (chip * 2 + number, number * count + chip) for chip in range(count) for number in range(2)
    ]
    total, near[-1] = lax.optimization_barrier((total, near[-1]))
    total = lax.ppermute(total, AXES, homes)
    squares = everywhere(squares, distances[0])[0, :2]
    scale = 1.0 / jnp.maximum(1.0, jnp.sqrt(squares / entries + CLIP_EPSILON))
    gradient_a = total[:, :width_a] * scale[0]
    gradient_b = total[:, width_a:] * scale[1]
    input_gradient = in_order(
        jnp.concatenate(near, axis=1), jnp.concatenate(far, axis=1), axis=1
    )
    return input_gradient, gradient_a, gradient_b


def solution(mesh):
    ring, ctx = mesh.shape["dp"], mesh.shape["ctx"]
    split = Mesh(mesh.devices.reshape(ring, ctx // 2, 2), AXES)
    rows = P(AXES, None)
    placed = (rows,) * 5 + (P(),) * 6 + (rows,) * 2
    return jax.shard_map(
        on_device,
        mesh=split,
        in_specs=placed,
        out_specs=(rows, P(None, AXES), P(None, AXES)),
        check_vma=False,
    )
```

```python
import functools

import jax
import jax.numpy as jnp
import numpy as np
from jax import lax
from jax.experimental import pallas as pl
from jax.experimental.pallas import tpu as pltpu
from jax.sharding import Mesh
from jax.sharding import PartitionSpec as P

P_SIZE = 64
N = 128
G = 4
Q = 256
EPS_NORM = 1e-05
CLIP_EPSILON = 1e-06
ADAPTER_SCALE = 2.0
VMEM_BYTES = 18 * 1024 * 1024

F32 = jnp.float32
BF16 = jnp.bfloat16
AXES = ("dp", "x", "core")


def dot(a, b, dims=((1,), (0,))):
    return lax.dot_general(a, b, (dims, ((), ())), preferred_element_type=F32)


def spread(values, pattern):
    high = values.astype(BF16).astype(F32)
    rest = values - high
    mid = rest.astype(BF16).astype(F32)
    return dot(jnp.concatenate([high, mid, rest - mid], axis=1).astype(BF16), pattern)


def spread_pattern(heads):
    return np.tile(np.repeat(np.eye(heads), P_SIZE, axis=1), (3, 1)).astype(BF16)


def of_core(ref, rows, core, first, heads):
    half = ref.shape[1] // 2
    return jnp.where(
        core == 0, ref[rows, first : first + heads], ref[rows, half + first : half + first + heads]
    )


def pair_rows(pair):
    lane = lax.broadcasted_iota(jnp.int32, pair.shape, 1)
    zero = jnp.zeros_like(pair)
    return jnp.concatenate(
        [jnp.where(lane < P_SIZE, pair, zero), jnp.where(lane >= P_SIZE, pair, zero)], axis=0
    )


def of_quarter(ref, rows, quarter, heads):
    value = ref[rows, :heads]
    for index in range(1, ref.shape[1] // heads):
        value = jnp.where(quarter == index, ref[rows, index * heads : (index + 1) * heads], value)
    return value


def whole(shape):
    return pl.BlockSpec(shape, lambda *_: (0,) * len(shape))


def cost(flops, slowdown):
    return pl.CostEstimate(flops=flops * slowdown, bytes_accessed=0, transcendentals=0)


def params(*semantics):
    return pltpu.CompilerParams(
        dimension_semantics=semantics or None, vmem_limit_bytes=VMEM_BYTES
    )


def step_kernel(blocks, core_ref, near_ref, far_ref, bias_ref, rate_ref, step_ref, cum_ref, cum_t_ref):
    lower = lax.broadcasted_iota(jnp.int32, (Q, Q), 0) >= lax.broadcasted_iota(
        jnp.int32, (Q, Q), 1
    )
    for block in range(blocks):
        rows = slice(block * Q, (block + 1) * Q)
        local = slice(block % (blocks // 2) * Q, (block % (blocks // 2) + 1) * Q)
        raw = jnp.where(
            core_ref[0] == block // (blocks // 2), near_ref[local, :], far_ref[local, :]
        )
        raw = raw + bias_ref[...]
        step = jnp.maximum(raw, 0.0) + jnp.log1p(jnp.exp(-jnp.abs(raw)))
        cum = lax.dot_general(
            lower.astype(F32),
            -jnp.exp(rate_ref[...]) * step,
            (((1,), (0,)), ((), ())),
            precision=lax.Precision.HIGHEST,
            preferred_element_type=F32,
        )
        step_ref[rows, :] = step
        cum_ref[rows, :] = cum
        cum_t_ref[block] = cum.T


def step_part(core, near, far, bias, rate):
    rows, heads = 2 * near.shape[0], near.shape[1]
    spec = pltpu.PrefetchScalarGridSpec(
        num_scalar_prefetch=1,
        grid=(1,),
        in_specs=[whole(near.shape), whole(far.shape), whole(bias.shape), whole(rate.shape)],
        out_specs=[whole((rows, heads)), whole((rows, heads)), whole((rows // Q, heads, Q))],
    )
    return pl.pallas_call(
        functools.partial(step_kernel, rows // Q),
        grid_spec=spec,
        out_shape=[
            jax.ShapeDtypeStruct((rows, heads), F32),
            jax.ShapeDtypeStruct((rows, heads), F32),
            jax.ShapeDtypeStruct((rows // Q, heads, Q), F32),
        ],
        compiler_params=params("arbitrary"),
        cost_estimate=cost(rows * heads * Q, 200),
        name="step_part",
    )(core, near, far, bias, rate)


def local_kernel(
    heads, core_ref, near_ref, far_ref, b_ref, c_ref, step_ref, cum_ref, cum_t_ref, skip_ref,
    pattern_ref, top_ref, low_ref, ssd_ref, state_ref, sent_ref, x_ref, total_ref,
):
    block = pl.program_id(1)
    core = core_ref[0]
    quarter = core * pl.num_programs(0) + pl.program_id(0)
    x_ref[...] = jnp.where(
        block // (pl.num_programs(1) // 2) == core, near_ref[...], far_ref[...]
    )
    pattern = pattern_ref[...]
    step = of_quarter(step_ref, slice(None), quarter, heads)
    cum = of_quarter(cum_ref, slice(None), quarter, heads)
    start = pl.multiple_of(quarter * heads, 8)
    cum_t = cum_t_ref[0, pl.ds(start, heads), :]
    last = cum[Q - 1 : Q, :]
    step_wide = spread(step, pattern)
    weight = spread(step * jnp.exp(last - cum), pattern)
    decay = spread(jnp.broadcast_to(jnp.exp(last), (8, heads)), pattern)[:1, :]
    x = x_ref[...].astype(F32)
    xdt = (x * step_wide).astype(BF16)
    state = dot(b_ref[...], (x * weight).astype(BF16), ((0,), (0,)))
    state_ref[...] = state

    @pl.when(block == 0)
    def _():
        total_ref[...] = state

    @pl.when(block > 0)
    def _():
        total_ref[...] = total_ref[...] * decay + state

    sent_ref[...] = total_ref[...].astype(sent_ref.dtype)

    half = Q // 2
    inner = dot(b_ref[...], c_ref[...], ((1,), (1,)))
    causal = lax.broadcasted_iota(jnp.int32, (half, half), 1) >= lax.broadcasted_iota(
        jnp.int32, (half, half), 0
    )
    corner = jnp.where(causal, inner[:half, :half], 0.0)
    right = inner[:half, half:]
    end = jnp.where(causal, inner[half:, half:], 0.0)
    for pair in range(heads // 2):
        corners, rights = [], []
        for head in (2 * pair, 2 * pair + 1):
            across, down = cum_t[head : head + 1, :], cum[:, head : head + 1]
            gap = across[:, :half] - down[:half, :]
            first = (corner * jnp.exp(jnp.where(causal, gap, 0.0))).astype(BF16)
            second = (right * jnp.exp(across[:, half:] - down[:half, :])).astype(BF16)
            gap = across[:, half:] - down[half:, :]
            third = (end * jnp.exp(jnp.where(causal, gap, 0.0))).astype(BF16)
            top_ref[:, head * Q : head * Q + half] = first
            top_ref[:, head * Q + half : (head + 1) * Q] = second
            low_ref[:, head * half : (head + 1) * half] = third
            corners.append(first)
            rights += [second, third]
        lanes = slice(pair * 2 * P_SIZE, (pair + 1) * 2 * P_SIZE)
        values = xdt[:, lanes]
        intra = (
            dot(jnp.concatenate(corners, axis=0), pair_rows(values[:half, :]), ((0,), (0,))),
            dot(jnp.concatenate(rights, axis=0), pair_rows(values), ((0,), (0,))),
        )
        for part, rows in zip(intra, (slice(0, half), slice(half, Q))):
            ssd_ref[rows, lanes] = (
                part + skip_ref[:, lanes] * x_ref[rows, lanes].astype(F32)
            ).astype(ssd_ref.dtype)


def local_part(groups, heads, core, near, far, b, c, step, cum, cum_t, skip, pattern):
    rows = 2 * near.shape[0]
    blocks = rows // Q
    width = heads * P_SIZE
    row_block = pl.BlockSpec((Q, width), lambda g, i, s: (g * blocks + i, 0))
    spec = pltpu.PrefetchScalarGridSpec(
        num_scalar_prefetch=1,
        grid=(groups, blocks),
        in_specs=[
            pl.BlockSpec((Q, width), lambda g, i, s: (i % (blocks // 2), s[0] * groups + g)),
            pl.BlockSpec((Q, width), lambda g, i, s: (i % (blocks // 2), g)),
            pl.BlockSpec((Q, N), lambda g, i, s: (i, g)),
            pl.BlockSpec((Q, N), lambda g, i, s: (i, g)),
            pl.BlockSpec((Q, step.shape[1]), lambda g, i, s: (i, 0)),
            pl.BlockSpec((Q, step.shape[1]), lambda g, i, s: (i, 0)),
            pl.BlockSpec((1,) + cum_t.shape[1:], lambda g, i, s: (i, 0, 0)),
            pl.BlockSpec((1, width), lambda g, i, s: (0, s[0] * groups + g)),
            whole(pattern.shape),
        ],
        out_specs=[
            pl.BlockSpec((Q // 2, heads * Q), lambda g, i, s: (g * blocks + i, 0)),
            pl.BlockSpec((Q // 2, heads * Q // 2), lambda g, i, s: (g * blocks + i, 0)),
            row_block,
            pl.BlockSpec((N, width), lambda g, i, s: (g * blocks + i, 0)),
            pl.BlockSpec((N, width), lambda g, i, s: (g, 0)),
        ],
        scratch_shapes=[pltpu.VMEM((Q, width), BF16), pltpu.VMEM((N, width), F32)],
    )
    return pl.pallas_call(
        functools.partial(local_kernel, heads),
        grid_spec=spec,
        out_shape=[
            pltpu.HBM((groups * rows // 2, heads * Q), BF16),
            pltpu.HBM((groups * rows // 2, heads * Q // 2), BF16),
            jax.ShapeDtypeStruct((groups * rows, width), BF16),
            jax.ShapeDtypeStruct((groups * blocks * N, width), F32),
            jax.ShapeDtypeStruct((groups * N, width), BF16),
        ],
        compiler_params=params("arbitrary", "arbitrary"),
        cost_estimate=cost(groups * rows * width * Q * 4, 16),
        name="local_part",
    )(core, near, far, b, c, step, cum, cum_t, skip, pattern)


def norm_kernel(
    blocks, heads, core_ref, c_ref, incoming_ref, state_ref, cum_ref, pattern_ref, ssd_ref, near_ref,
    far_ref, gain_ref, down_ref, up_ref, hat_ref, slope_ref, product_ref, sum_ref,
):
    gain = gain_ref[...]
    group = pl.program_id(0)
    quarter = core_ref[0] * pl.num_programs(0) + group
    run = incoming_ref[...].astype(F32)
    total = None
    for block in range(blocks):
        rows = slice(block * Q, (block + 1) * Q)
        inter = dot(c_ref[rows, :], run.astype(BF16))
        growth = spread(jnp.exp(of_quarter(cum_ref, rows, quarter, heads)), pattern_ref[...])
        ssd = ssd_ref[rows, :].astype(F32) + growth * inter
        local = slice(block % (blocks // 2) * Q, (block % (blocks // 2) + 1) * Q)
        z = jnp.where(
            core_ref[0] == block // (blocks // 2), near_ref[local, :], far_ref[local, :]
        ).astype(F32)
        silu = z / (1.0 + jnp.exp(-z))
        gated = ssd * silu
        rstd = lax.rsqrt(jnp.mean(gated * gated, axis=1, keepdims=True) + EPS_NORM)
        hat = gated * rstd
        normed = (hat * gain).astype(BF16)
        hat_ref[rows, :] = hat.astype(hat_ref.dtype)
        slope_ref[rows, :] = (rstd * silu).astype(slope_ref.dtype)
        product = dot(normed, down_ref[...], ((1,), (1,)))
        product_ref[rows, :] = jnp.where(group == 0, product, product_ref[rows, :] + product)
        part = dot(up_ref[rows, :], normed, ((0,), (0,)))
        total = part if total is None else total + part
        if block + 1 < blocks:
            states = slice(block * N, (block + 1) * N)
            run = run * growth[Q - 1 :, :] + state_ref[states, :]
    sum_ref[...] = total


def norm_part(groups, heads, core, c, incoming, state, cum, pattern, ssd, near, far, gain, down, up_twice):
    rows, width = 2 * near.shape[0], heads * P_SIZE
    rank = down.shape[0]
    blocks = rows // Q
    group_rows = pl.BlockSpec((rows, width), lambda g, s: (g, 0))
    spec = pltpu.PrefetchScalarGridSpec(
        num_scalar_prefetch=1,
        grid=(groups,),
        in_specs=[
            pl.BlockSpec((rows, N), lambda g, s: (0, g)),
            pl.BlockSpec((N, width), lambda g, s: (g, 0)),
            pl.BlockSpec((blocks * N, width), lambda g, s: (g, 0)),
            whole(cum.shape),
            whole(pattern.shape),
            group_rows,
            pl.BlockSpec((rows // 2, width), lambda g, s: (0, s[0] * groups + g)),
            pl.BlockSpec((rows // 2, width), lambda g, s: (0, g)),
            pl.BlockSpec((1, width), lambda g, s: (0, s[0] * groups + g)),
            pl.BlockSpec((rank, width), lambda g, s: (0, s[0] * groups + g)),
            whole(up_twice.shape),
        ],
        out_specs=[
            group_rows,
            group_rows,
            whole((rows, rank)),
            pl.BlockSpec((rank, width), lambda g, s: (0, g)),
        ],
    )
    return pl.pallas_call(
        functools.partial(norm_kernel, blocks, heads),
        grid_spec=spec,
        out_shape=[
            jax.ShapeDtypeStruct((groups * rows, width), BF16),
            jax.ShapeDtypeStruct((groups * rows, width), BF16),
            jax.ShapeDtypeStruct((rows, rank), F32),
            jax.ShapeDtypeStruct((rank, groups * width), F32),
        ],
        compiler_params=params("arbitrary"),
        cost_estimate=cost(groups * rows * width * 512, 12),
        name="norm_part",
    )(core, c, incoming, state, cum, pattern, ssd, near, far, gain, down, up_twice)


def product_kernel(first, spans, started, core_ref, near_ref, far_ref, *rest):
    pieces, out_ref = rest[started:-1], rest[-1]
    weights = joined(pieces, spans)
    depth = slice(first, first + weights.shape[0])
    half = near_ref.shape[0]
    for part in range(2):
        rows = slice(part * half, (part + 1) * half)
        cot = jnp.where(core_ref[0] == part, near_ref[:, depth], far_ref[:, depth])
        product = dot(cot, weights)
        out_ref[rows, :] = product + rest[0][rows, :] if started else product


def joined(pieces, spans):
    return jnp.concatenate(
        [piece[start : start + rows, :] for piece, (start, rows) in zip(pieces, spans)], axis=0
    )


def product_part(core, near, far, cut, first, earlier, pieces, width):
    rows = 2 * near.shape[0]
    held = [] if earlier is None else [earlier]
    columns = pl.BlockSpec((near.shape[0], cut), lambda i, s: (0, near.shape[1] // cut - 1))
    spec = pltpu.PrefetchScalarGridSpec(
        num_scalar_prefetch=1,
        grid=(1,),
        in_specs=[columns, columns]
        + [whole(array.shape) for array in held]
        + [whole(piece[0].shape) for piece in pieces],
        out_specs=whole((rows, width)),
    )
    return pl.pallas_call(
        functools.partial(product_kernel, first, tuple(piece[1:] for piece in pieces), len(held)),
        grid_spec=spec,
        out_shape=jax.ShapeDtypeStruct((rows, width), F32),
        input_output_aliases={3: 0} if held else {},
        compiler_params=params("arbitrary"),
        cost_estimate=cost(2 * rows * width * Q, 4),
        name="product_part",
    )(core, near, far, *held, *[piece[0] for piece in pieces])


def grad_kernel(
    blocks, first, heads, start, spans, core_ref, near_ref, far_ref, earlier_ref, up_ref, down_ref, gain_ref, hat_ref,
    slope_ref, cum_ref, pattern_ref, c_ref, *rest,
):
    pieces, (grad_ref, block_grad_ref, total_ref) = rest[:-3], rest[-3:]
    weights = joined(pieces, spans)
    depth = slice(start, start + weights.shape[0])
    gain = gain_ref[...]
    later = None
    for block in reversed(range(blocks)):
        rows = slice(block * Q, (block + 1) * Q)
        local = slice(block % (blocks // 2) * Q, (block % (blocks // 2) + 1) * Q)
        cot = jnp.where(
            core_ref[0] == block // (blocks // 2), near_ref[local, depth], far_ref[local, depth]
        )
        product = dot(cot, weights) + dot(up_ref[rows, :], down_ref[...]) + earlier_ref[rows, :]
        weighted = product * gain
        hat = hat_ref[rows, :].astype(F32)
        mean = jnp.mean(hat * weighted, axis=1, keepdims=True)
        grad = slope_ref[rows, :].astype(F32) * (weighted - hat * mean)
        grad_ref[rows, :] = grad.astype(grad_ref.dtype)
        growth = spread(jnp.exp(of_core(cum_ref, rows, core_ref[0], first, heads)), pattern_ref[...])
        fresh = dot(c_ref[rows, :], (growth * grad).astype(BF16), ((0,), (0,)))
        block_grad_ref[block * N : (block + 1) * N, :] = fresh
        later = (
            fresh
            if later is None
            else later * growth[Q - 1 :, :] + fresh
        )
    total_ref[...] = later.astype(BF16)


def grad_part(
    group, groups, heads, core, near, far, cut, start, earlier, up_twice, down, gain, hat, slope, cum, pattern, c, pieces
):
    rows, width = earlier.shape
    rank = down.shape[0]
    blocks = rows // Q
    columns = pl.BlockSpec((near.shape[0], cut), lambda i, s: (0, near.shape[1] // cut - 1))
    spec = pltpu.PrefetchScalarGridSpec(
        num_scalar_prefetch=1,
        grid=(1,),
        in_specs=[
            columns,
            columns,
            whole(earlier.shape),
            whole(up_twice.shape),
            pl.BlockSpec((rank, width), lambda i, s: (0, s[0] * groups + group)),
            pl.BlockSpec((1, width), lambda i, s: (0, s[0] * groups + group)),
            pl.BlockSpec((rows, width), lambda i, s: (group, 0)),
            pl.BlockSpec((rows, width), lambda i, s: (group, 0)),
            whole(cum.shape),
            whole(pattern.shape),
            pl.BlockSpec((rows, N), lambda i, s: (0, group)),
        ]
        + [whole(piece[0].shape) for piece in pieces],
        out_specs=[whole((rows, width)), whole((blocks * N, width)), whole((N, width))],
    )
    return pl.pallas_call(
        functools.partial(
            grad_kernel, blocks, group * heads, heads, start, tuple(piece[1:] for piece in pieces)
        ),
        grid_spec=spec,
        out_shape=[
            jax.ShapeDtypeStruct((rows, width), BF16),
            jax.ShapeDtypeStruct((blocks * N, width), F32),
            jax.ShapeDtypeStruct((N, width), BF16),
        ],
        compiler_params=params("arbitrary"),
        cost_estimate=cost(2 * rows * width * Q, 8),
        name="grad_part",
    )(
        core, near, far, earlier, up_twice, down, gain, hat, slope, cum, pattern, c,
        *[piece[0] for piece in pieces],
    )


def back_kernel(
    first, heads, core_ref, top_ref, low_ref, grad_ref, step_ref, pattern_ref, skip_ref, out_ref
):
    half = Q // 2
    step = of_core(step_ref, slice(None), core_ref[0], first, heads)
    out_ref[...] = spread(step, pattern_ref[...])
    for pair in range(heads // 2):
        lanes = slice(pair * 2 * P_SIZE, (pair + 1) * 2 * P_SIZE)
        grad = grad_ref[:, lanes]
        back = (
            dot(top_ref[:, 2 * pair * Q : 2 * (pair + 1) * Q], pair_rows(grad)),
            dot(low_ref[:, 2 * pair * half : 2 * (pair + 1) * half], pair_rows(grad[half:, :])),
        )
        for part, rows in zip(back, (slice(0, half), slice(half, Q))):
            out_ref[rows, lanes] = out_ref[rows, lanes] * part + skip_ref[:, lanes] * grad_ref[
                rows, lanes
            ].astype(F32)


def back_part(group, groups, heads, core, top, low, grad, step, pattern, skip):
    rows, width = grad.shape
    row_block = pl.BlockSpec((Q, width), lambda i, s: (i, 0))
    spec = pltpu.PrefetchScalarGridSpec(
        num_scalar_prefetch=1,
        grid=(rows // Q,),
        in_specs=[
            pl.BlockSpec((Q // 2, heads * Q), lambda i, s: (group * (rows // Q) + i, 0)),
            pl.BlockSpec((Q // 2, heads * Q // 2), lambda i, s: (group * (rows // Q) + i, 0)),
            row_block,
            pl.BlockSpec((Q, step.shape[1]), lambda i, s: (i, 0)),
            whole(pattern.shape),
            pl.BlockSpec((1, width), lambda i, s: (0, s[0] * groups + group)),
        ],
        out_specs=row_block,
    )
    return pl.pallas_call(
        functools.partial(back_kernel, group * heads, heads),
        grid_spec=spec,
        out_shape=jax.ShapeDtypeStruct((rows, width), F32),
        compiler_params=params("arbitrary"),
        cost_estimate=cost(rows * width * Q * 2, 8),
        name="back_part",
    )(core, top, low, grad, step, pattern, skip)


def cross_kernel(
    blocks, first, heads, core_ref, b_ref, outgoing_ref, block_grad_ref, step_ref, cum_ref, pattern_ref,
    base_ref, near_ref, far_ref,
):
    run = outgoing_ref[...].astype(F32)
    for block in reversed(range(blocks)):
        rows = slice(block * Q, (block + 1) * Q)
        local = slice(block % (blocks // 2) * Q, (block % (blocks // 2) + 1) * Q)
        cross = dot(b_ref[rows, :], run.astype(BF16))
        cum = of_core(cum_ref, rows, core_ref[0], first, heads)
        last = cum[Q - 1 :, :]
        step = of_core(step_ref, rows, core_ref[0], first, heads)
        weight = spread(step * jnp.exp(last - cum), pattern_ref[...])
        value = (base_ref[rows, :] + weight * cross).astype(near_ref.dtype)
        own = core_ref[0] == block // (blocks // 2)

        @pl.when(own)
        def _():
            near_ref[local, :] = value

        @pl.when(jnp.logical_not(own))
        def _():
            far_ref[local, :] = value

        if block > 0:
            states = slice(block * N, (block + 1) * N)
            decay = spread(jnp.broadcast_to(jnp.exp(last), (8, heads)), pattern_ref[...])[:1, :]
            run = run * decay + block_grad_ref[states, :]


def cross_part(group, heads, core, b, outgoing, block_grad, step, cum, pattern, base):
    rows, width = base.shape
    blocks = rows // Q
    spec = pltpu.PrefetchScalarGridSpec(
        num_scalar_prefetch=1,
        grid=(1,),
        in_specs=[
            pl.BlockSpec((rows, N), lambda i, s: (0, group)),
            whole(outgoing.shape),
            whole(block_grad.shape),
            whole(step.shape),
            whole(cum.shape),
            whole(pattern.shape),
            whole(base.shape),
        ],
        out_specs=[whole((rows // 2, width))] * 2,
    )
    return pl.pallas_call(
        functools.partial(cross_kernel, blocks, group * heads, heads),
        grid_spec=spec,
        out_shape=[jax.ShapeDtypeStruct((rows // 2, width), BF16)] * 2,
        compiler_params=params("arbitrary"),
        cost_estimate=cost(rows * width * N * 2, 6),
        name="cross_part",
    )(core, b, outgoing, block_grad, step, cum, pattern, base)


def ring_order(count):
    return list(range(0, count, 2)) + list(range(count - 1 - count % 2, 0, -2))


def rotations(count):
    return [[(i, (i + k) % count) for i in range(count)] for k in range(count)]


def chip_order():
    ring, across = lax.axis_size("dp"), lax.axis_size("x")
    offsets = [0]
    for distance in range(1, (ring - 1) // 2 + 1):
        offsets += [-distance, distance]
    if ring % 2 == 0:
        offsets.append(ring // 2)
    me, x = lax.axis_index("dp"), lax.axis_index("x")
    seat = jnp.where(me % 2 == 0, me // 2, ring - (me + 1) // 2)

    def member(place):
        return jnp.where(place < (ring + 1) // 2, 2 * place, 2 * (ring - place) - 1)

    return [
        [member((seat + offset + ring) % ring) * across + (x - k + across) % across for k in range(across)]
        for offset in offsets
    ]


def ring_perms():
    ring = lax.axis_size("dp")
    order = ring_order(ring)
    ahead = [(order[i], order[(i + 1) % ring]) for i in range(ring)]
    return ahead, [(b, a) for a, b in ahead]


def cut_kernel(plans, count, *refs):
    arrays, outs = refs[:count], refs[count:]
    for out, plan in zip(outs, plans):
        row = 0
        for index, start, rows, column in plan:
            out[row : row + rows, :] = arrays[index][
                start : start + rows, column : column + out.shape[1]
            ]
            row += rows


def cut(arrays, plans, width):
    return small_call(
        functools.partial(cut_kernel, plans, len(arrays)),
        [],
        arrays,
        [
            jax.ShapeDtypeStruct((sum(part[2] for part in plan), width), arrays[0].dtype)
            for plan in plans
        ],
        "cut_rows",
    )


class Gather:
    def __init__(self, shard):
        self.ring = lax.axis_size("dp")
        self.across = lax.axis_size("x")
        self.turns = rotations(self.across)[1:]
        self.perms = ring_perms()
        self.shard = shard
        self.size = shard.shape[0]
        self.width = shard.shape[1] // 2
        late = shard[:, self.width :]
        self.late = [(late, 0, self.size)] * 2
        self.moving = [late, late]
        self.crossing = shard
        self.pieces = {}
        self.steps = self.ring // 2 + 2

    def sizes(self, index):
        early = 0 if index == 1 else self.across * self.size
        late = self.size
        if 2 * index == self.ring:
            late //= 2
        elif 2 * index > self.ring:
            early, late = early // 2, 0
        return early, late

    def step(self, index, beside):
        ring, size, width = self.ring, self.size, self.width
        early_size, late_size = self.sizes(index)
        got = tuple(lax.ppermute(array, "dp", perm) for array, perm in zip(self.moving, self.perms))
        crossed = tuple(lax.ppermute(self.crossing, "x", turn) for turn in self.turns)
        values = beside()
        got, crossed, values = lax.optimization_barrier((got, crossed, values))
        late = [(got[0], early_size, late_size), (got[1], 0, late_size)]
        early = [(got[0], 0, early_size), (got[1], late_size, early_size)]
        after_early, after_late = self.sizes(index + 1)
        more = index + 1 < self.steps
        if index == 1:
            first = [(0, 0, size, 0)] + [(1 + k, 0, size, 0) for k in range(len(crossed))]
            base = 1 + len(crossed)
            self.first, *rest = cut(
                [self.shard, *crossed, *got],
                [
                    first,
                    first + [(base, 0, after_late, 0)],
                    [(base + 1, size - after_late, after_late, 0)] + first,
                    [(base, 0, size, 0), (base + 1, 0, size, 0)],
                ],
                width,
            )
            self.moving, self.crossing = rest[:2], rest[2]
            met = [array[:, width:] for array in crossed]
            self.pieces[0] = [
                [(self.first, 0, self.first.shape[0])],
                [self.late[0]] + [(array, 0, size) for array in met],
            ]
        else:
            distance = index - 1
            if 2 * distance < ring:
                for side in range(2):
                    self.pieces[2 * distance - 1 + side] = [
                        [early[side]],
                        [self.late[side]] + [(array, side * size, size) for array in crossed],
                    ]
            else:
                self.pieces[2 * distance - 1] = [
                    early, self.late + [(array, 0, size) for array in crossed]
                ]
            if more:
                plans = [[(0, early_size, late_size, 0), (1, 0, late_size, 0)]]
                whole_array = (after_early, after_late) == (early_size, late_size)
                if not whole_array:
                    plans += [
                        [(0, 0, after_early, 0), (0, early_size, after_late, 0)],
                        [
                            (1, late_size - after_late, after_late, 0),
                            (1, late_size + early_size - after_early, after_early, 0),
                        ],
                    ]
                plans = [[part for part in plan if part[2]] for plan in plans]
                self.crossing, *moving = cut(list(got), plans, width)
                self.moving = moving or list(got)
                self.crossing, self.moving = lax.optimization_barrier((self.crossing, self.moving))
        self.late = late
        return values


def down_kernel(core_ref, product_ref, arrived_ref, cot_ref, own_ref, sent_ref):
    down = (product_ref[...] + arrived_ref[...]).astype(BF16)
    half = own_ref.shape[1]
    parts = [
        ADAPTER_SCALE * dot(down, cot_ref[:, part * half : (part + 1) * half], ((0,), (0,)))
        for part in range(2)
    ]
    own_ref[...] = jnp.where(core_ref[0] == 0, parts[0], parts[1])
    sent_ref[...] = jnp.where(core_ref[0] == 0, parts[1], parts[0]).astype(sent_ref.dtype)


def down_part(core, product, arrived, cot):
    shape = (product.shape[1], cot.shape[1] // 2)
    return small_call(
        down_kernel,
        [core],
        [product, arrived, cot],
        [jax.ShapeDtypeStruct(shape, F32), jax.ShapeDtypeStruct(shape, BF16)],
        "down_part",
    )


def pack_kernel(ring, across, place_ref, sum_ref, own_ref, far_ref, mine_ref, *sent_refs):
    other = own_ref[...] + far_ref[...].astype(F32)
    width_a = sum_ref.shape[1] // (ring * across)
    width_b = other.shape[1] // (ring * across)
    for member in range(ring):
        blocks = []
        for x in range(across):
            chip = member * across + x
            part = sum_ref[:, chip * width_a : (chip + 1) * width_a]
            blocks.append((part, other[:, chip * width_b : (chip + 1) * width_b]))
        for turn in range(across):
            target = (place_ref[1] + turn) % across
            chosen = blocks[0]
            for x in range(1, across):
                chosen = [jnp.where(target == x, new, old) for new, old in zip(blocks[x], chosen)]
            out = mine_ref if turn == 0 else sent_refs[turn - 1]
            out[member, :, :width_a] = chosen[0].astype(out.dtype)
            out[member, :, width_a:] = chosen[1].astype(out.dtype)


def halve_kernel(bit_ref, mine_ref, *refs):
    arrived, (kept_ref, sent_ref) = refs[:-2], refs[-2:]
    half = kept_ref.shape[0]
    for out, start in ((kept_ref, bit_ref[0] * half), (sent_ref, (1 - bit_ref[0]) * half)):
        total = mine_ref[pl.ds(start, half)]
        for ref in arrived:
            total = total + ref[pl.ds(start, half)].astype(F32)
        out[...] = total.astype(out.dtype)


def add_kernel(mine_ref, arrived_ref, total_ref, sent_ref):
    total = mine_ref[...] + arrived_ref[...].astype(F32)
    total_ref[...] = total
    sent_ref[...] = total.astype(sent_ref.dtype)


def total_kernel(width_a, place_ref, mine_ref, arrived_ref, total_ref, square_ref):
    total = mine_ref[...] + arrived_ref[...].astype(F32)
    squares = total * total
    lane = lax.broadcasted_iota(jnp.int32, squares.shape, 2)
    first = jnp.sum(jnp.where(lane < width_a, squares, 0.0))
    second = jnp.sum(jnp.where(lane >= width_a, squares, 0.0))
    column = lax.broadcasted_iota(jnp.int32, square_ref.shape, 1)
    square_ref[...] = jnp.where(column == 0, first, jnp.where(column == 1, second, 0.0))
    own = place_ref[0] % mine_ref.shape[0]
    total_ref[...] = mine_ref[own] + arrived_ref[own].astype(F32)


def small_call(kernel, scalars, arrays, outs, name):
    spec = pltpu.PrefetchScalarGridSpec(
        num_scalar_prefetch=len(scalars),
        grid=(1,),
        in_specs=[whole(array.shape) for array in arrays],
        out_specs=[whole(out.shape) for out in outs],
    )
    return pl.pallas_call(
        kernel,
        grid_spec=spec,
        out_shape=outs,
        compiler_params=params("arbitrary"),
        cost_estimate=cost(10**9, 1),
        name=name,
    )(*scalars, *arrays)


def packed(sum_a, own_b, far_b):
    ring, across = lax.axis_size("dp"), lax.axis_size("x")
    place = jnp.stack([lax.axis_index("dp"), lax.axis_index("x")]).astype(jnp.int32)
    count = ring * across
    shape = (ring, own_b.shape[0], (sum_a.shape[1] + own_b.shape[1]) // count)
    mine, *sent = small_call(
        functools.partial(pack_kernel, ring, across),
        [place],
        [sum_a, own_b, far_b],
        [jax.ShapeDtypeStruct(shape, F32)] + [jax.ShapeDtypeStruct(shape, BF16)] * (across - 1),
        "pack_sums",
    )
    return mine, sent


def halved(mine, arrived, distance):
    shape = (distance,) + mine.shape[1:]
    return small_call(
        halve_kernel,
        [((lax.axis_index("dp") // distance) % 2).astype(jnp.int32)[None]],
        [mine, *arrived],
        [jax.ShapeDtypeStruct(shape, F32), jax.ShapeDtypeStruct(shape, BF16)],
        "halve_sums",
    )


def over_x(sent):
    return [lax.ppermute(value, "x", turn) for value, turn in zip(sent, rotations(lax.axis_size("x"))[1:])]


def far_in_dp(value, distance):
    return lax.ppermute(value, "dp", [(i, i ^ distance) for i in range(lax.axis_size("dp"))])


def added(mine, arrived):
    return small_call(
        add_kernel,
        [],
        [mine, arrived],
        [jax.ShapeDtypeStruct(mine.shape, F32), jax.ShapeDtypeStruct(mine.shape, BF16)],
        "add_sums",
    )


def totals(mine, arrived, width_a):
    return small_call(
        functools.partial(total_kernel, width_a),
        [lax.axis_index("dp").astype(jnp.int32)[None]],
        [mine, arrived],
        [jax.ShapeDtypeStruct(mine.shape[1:], F32), jax.ShapeDtypeStruct((8, 128), F32)],
        "total_sums",
    )


def finish_kernel(entries, total_ref, square_ref, first_ref, second_ref):
    width = first_ref.shape[1]
    for out, count, column, lanes in (
        (first_ref, entries[0], 0, slice(0, width)),
        (second_ref, entries[1], 1, slice(width, width + second_ref.shape[1])),
    ):
        mean = square_ref[0:1, column : column + 1] / count
        out[...] = total_ref[:, lanes] / jnp.maximum(1.0, jnp.sqrt(mean + CLIP_EPSILON))


def finished(total, squares, width_a):
    rank, width = total.shape
    devices = lax.axis_size(AXES)
    widths = (width_a, width - width_a)
    return small_call(
        functools.partial(finish_kernel, tuple(float(rank * part * devices) for part in widths)),
        [],
        [total, squares],
        [jax.ShapeDtypeStruct((rank, part), F32) for part in widths],
        "finish",
    )


def over_axis(value, axis):
    turns = rotations(lax.axis_size(axis))[1:]
    return functools.reduce(jnp.add, [lax.ppermute(value, axis, turn) for turn in turns], value)


def on_device(
    state_input, gate_values, input_matrix, readout_matrix, step_unbiased, step_bias,
    decay_rate_log, skip_coefficients, norm_gain, adapter_down, adapter_up, projection_weight,
    output_cotangent,
):
    ring, across = lax.axis_size("dp"), lax.axis_size("x")
    core = lax.axis_index("core")
    swap = [(0, 1), (1, 0)]
    near_rows = state_input.shape[0]
    groups = G // 2
    heads = step_bias.shape[0] // G
    width = heads * P_SIZE

    def half(value, which, axis=-1):
        size = value.shape[axis] // 2
        return lax.dynamic_slice_in_dim(value, which * size, size, axis)

    def in_order(near, far, axis=0):
        return jnp.concatenate(
            [jnp.where(core == 0, near, far), jnp.where(core == 0, far, near)], axis=axis
        )

    def swapped(value):
        return lax.ppermute(value, "core", swap)

    sent_weight = half(projection_weight, 1 - core)
    sent_weight, state_input, step_unbiased, input_matrix, readout_matrix = lax.optimization_barrier(
        (sent_weight, state_input, step_unbiased, input_matrix, readout_matrix)
    )
    shard = in_order(half(projection_weight, core), swapped(sent_weight))
    raw_far = swapped(step_unbiased)
    x_far = swapped(
        jnp.concatenate(
            [half(value, 1 - core) for value in (state_input, input_matrix, readout_matrix)], axis=1
        )
    )
    shard, gate_values, output_cotangent = lax.optimization_barrier(
        (shard, gate_values, output_cotangent)
    )
    which = core.astype(jnp.int32)[None]
    chips = chip_order()
    chip_rows = shard.shape[0]
    slots = list(range(len(chips)))
    stages = [slots[:3], slots[3:5], slots[5:7], slots[7:]] if len(slots) > 7 else [slots[:1], slots[1:]]
    rows = 2 * near_rows
    blocks = rows // Q
    gather = Gather(shard)
    forward = [(i, i + 1) for i in range(across - 1)]
    backward = [(i + 1, i) for i in range(across - 1)]

    def staged(index, group):
        return [piece for slot in stages[index] for piece in gather.pieces[slot][group]]

    def depth(index):
        return sum(len(stage) for stage in stages[:index]) * across * chip_rows

    def carried(fresh, cum, perm, group=None):
        sent = fresh
        for lap in range(across - 1):
            arrived = lax.ppermute(sent, "x", perm)
            if lap + 2 < across:
                total = jnp.sum(cum.reshape(blocks, Q, -1)[:, Q - 1], axis=0)
                decay = jnp.repeat(jnp.exp(half(total, core)).reshape(groups, 1, heads), P_SIZE, axis=2)
                if group is not None:
                    decay = decay[group : group + 1]
                parts = [value.astype(F32).reshape(-1, N, width) for value in (arrived, fresh)]
                sent = (parts[0] * decay + parts[1]).astype(BF16).reshape(fresh.shape)
        return arrived

    skip = jnp.repeat(skip_coefficients, P_SIZE)[None, :]
    gain = norm_gain[None, :]
    pattern = spread_pattern(heads)

    def prepare():
        step, cum, cum_t = step_part(
            which, step_unbiased, raw_far, step_bias[None, :], decay_rate_log[None, :]
        )
        cut = groups * width
        b = in_order(half(input_matrix, core), x_far[:, cut : cut + groups * N])
        c = in_order(half(readout_matrix, core), x_far[:, cut + groups * N :])
        local = local_part(
            groups, heads, which, state_input, x_far, b, c, step, cum, cum_t, skip, pattern
        )
        return step, cum, cum_t, b, c, local

    step, cum, cum_t, b, c, local = gather.step(1, prepare)

    def second():
        ssd, state, fresh = local[2:]
        up_near = (
            ADAPTER_SCALE * dot(output_cotangent, adapter_up, ((1,), (1,))).astype(BF16)
        ).astype(BF16)
        parts = [
            lax.dynamic_slice_in_dim(output_cotangent, chip * chip_rows, chip_rows, 1)
            for offset in chips
            for chip in offset
        ]
        near = jnp.concatenate([half(gate_values, 1 - core)] + parts, axis=1)
        up_near, fresh = lax.optimization_barrier((up_near, fresh))
        incoming = carried(fresh, cum, forward)
        up_twice = in_order(up_near, swapped(up_near))
        far = swapped(near)
        hat, slope, product, sum_a = norm_part(
            groups, heads, which, c, incoming, state, cum, pattern, ssd, gate_values, far, gain, adapter_down,
            up_twice,
        )
        far_product = swapped(half(product, 1 - core, 0))
        return up_twice, near, far, (hat, slope), sum_a, half(product, core, 0), far_product

    up_twice, cot_near, cot_far, normed, sum_a, product, far_product = gather.step(2, second)
    cot_width = output_cotangent.shape[1]

    def during(index, beside):
        return gather.step(index, beside) if gather.steps > index else beside()

    distances = [ring >> k for k in range(1, ring.bit_length())]

    def third():
        own_b, sent_b = down_part(which, product, far_product, output_cotangent)
        mine, sent = packed(sum_a, own_b, swapped(sent_b))
        return mine, over_x(sent)

    mine, sent = during(3, third)

    def products(indices, earlier):
        for index in indices:
            earlier = [
                product_part(
                    which, cot_near, cot_far, cot_width, depth(index), earlier[group], staged(index, group), width
                )
                for group in range(groups)
            ]
        return earlier

    def doubled(value, rounded, hops):
        for distance in hops:
            value, rounded = added(value, far_in_dp(rounded, distance))
        return value, rounded

    def fourth():
        held = list(range(len(stages) - 1))[:2]
        halves = halved(mine, sent, distances[0])
        return doubled(*halves, distances[:-2]), products(held, [None] * groups)

    (mine, sent), earlier = during(4, fourth)
    width_a = 2 * width // (ring * across)

    def fifth():
        held = list(range(len(stages) - 1))[2:]
        return doubled(mine, sent, distances[:-1][-1:]), products(held, earlier)

    (mine, sent), earlier = during(5, fifth)
    for index in range(6, gather.steps):
        gather.step(index, lambda: ())
    arrived = far_in_dp(sent, distances[-1])

    grads = [
        grad_part(
            group, groups, heads, which, cot_near, cot_far, cot_width, depth(len(stages) - 1), earlier[group],
            up_twice, adapter_down, gain, *normed, cum, pattern, c, staged(len(stages) - 1, group),
        )
        for group in range(groups)
    ]
    arrived, grads = lax.optimization_barrier((arrived, grads))
    outgoing = [carried(part[2], cum, backward, group) for group, part in enumerate(grads)]
    total, squares = totals(mine, arrived, width_a)

    def back(group):
        return back_part(
            group, groups, heads, which, *local[:2], grads[group][0], step, pattern, skip
        )

    count = ring * across
    homes = [
        (chip * 2 + number, number * count + chip) for chip in range(count) for number in range(2)
    ]
    squares = squares + far_in_dp(squares, distances[0])
    bases = [back(0)]
    squares, bases, grads = lax.optimization_barrier((squares, bases, grads))
    squares = over_axis(squares, "core")
    bases.append(back(1))
    squares, bases, total = lax.optimization_barrier((squares, bases, total))
    squares = over_axis(squares, "x")
    total = lax.ppermute(total, AXES, homes)
    near, far = [], []
    for group in range(groups):
        if group == groups - 1:
            squares, bases, total = lax.optimization_barrier((squares, bases, total))
        own, others = cross_part(
            group, heads, which, b, outgoing[group], grads[group][1], step, cum, pattern, bases[group]
        )
        far.append(swapped(others))
        near.append(own)
    gradient_a, gradient_b = finished(total, squares, width_a)
    input_gradient = in_order(
        jnp.concatenate(near, axis=1), jnp.concatenate(far, axis=1), axis=1
    )
    return input_gradient, gradient_a, gradient_b


def solution(mesh):
    ring, ctx = mesh.shape["dp"], mesh.shape["ctx"]
    split = Mesh(mesh.devices.reshape(ring, ctx // 2, 2), AXES)
    rows = P(AXES, None)
    placed = (rows,) * 5 + (P(),) * 6 + (rows,) * 2
    return jax.shard_map(
        on_device,
        mesh=split,
        in_specs=placed,
        out_specs=(rows, P(None, AXES), P(None, AXES)),
        check_vma=False,
    )
```

```python
import functools

import jax
import jax.numpy as jnp
import numpy as np
from jax import lax
from jax.experimental import pallas as pl
from jax.experimental.pallas import tpu as pltpu
from jax.sharding import Mesh
from jax.sharding import PartitionSpec as P

P_SIZE = 64
N = 128
G = 4
Q = 256
EPS_NORM = 1e-05
CLIP_EPSILON = 1e-06
ADAPTER_SCALE = 2.0
VMEM_BYTES = 18 * 1024 * 1024

F32 = jnp.float32
BF16 = jnp.bfloat16
AXES = ("dp", "x", "core")


def dot(a, b, dims=((1,), (0,))):
    return lax.dot_general(a, b, (dims, ((), ())), preferred_element_type=F32)


def spread(values, pattern):
    high = values.astype(BF16).astype(F32)
    rest = values - high
    mid = rest.astype(BF16).astype(F32)
    return dot(jnp.concatenate([high, mid, rest - mid], axis=1).astype(BF16), pattern)


def spread_pattern(heads):
    return np.tile(np.repeat(np.eye(heads), P_SIZE, axis=1), (3, 1)).astype(BF16)


def of_core(ref, rows, core, first, heads):
    half = ref.shape[1] // 2
    return jnp.where(
        core == 0, ref[rows, first : first + heads], ref[rows, half + first : half + first + heads]
    )


def pair_rows(pair):
    lane = lax.broadcasted_iota(jnp.int32, pair.shape, 1)
    zero = jnp.zeros_like(pair)
    return jnp.concatenate(
        [jnp.where(lane < P_SIZE, pair, zero), jnp.where(lane >= P_SIZE, pair, zero)], axis=0
    )


def of_quarter(ref, rows, quarter, heads):
    value = ref[rows, :heads]
    for index in range(1, ref.shape[1] // heads):
        value = jnp.where(quarter == index, ref[rows, index * heads : (index + 1) * heads], value)
    return value


def whole(shape):
    return pl.BlockSpec(shape, lambda *_: (0,) * len(shape))


def cost(flops, slowdown):
    return pl.CostEstimate(flops=flops * slowdown, bytes_accessed=0, transcendentals=0)


def params(*semantics):
    return pltpu.CompilerParams(
        dimension_semantics=semantics or None, vmem_limit_bytes=VMEM_BYTES
    )


def step_kernel(blocks, core_ref, near_ref, far_ref, bias_ref, rate_ref, step_ref, cum_ref, cum_t_ref):
    lower = lax.broadcasted_iota(jnp.int32, (Q, Q), 0) >= lax.broadcasted_iota(
        jnp.int32, (Q, Q), 1
    )
    for block in range(blocks):
        rows = slice(block * Q, (block + 1) * Q)
        local = slice(block % (blocks // 2) * Q, (block % (blocks // 2) + 1) * Q)
        raw = jnp.where(
            core_ref[0] == block // (blocks // 2), near_ref[local, :], far_ref[local, :]
        )
        raw = raw + bias_ref[...]
        step = jnp.maximum(raw, 0.0) + jnp.log1p(jnp.exp(-jnp.abs(raw)))
        cum = lax.dot_general(
            lower.astype(F32),
            -jnp.exp(rate_ref[...]) * step,
            (((1,), (0,)), ((), ())),
            precision=lax.Precision.HIGHEST,
            preferred_element_type=F32,
        )
        step_ref[rows, :] = step
        cum_ref[rows, :] = cum
        cum_t_ref[block] = cum.T


def step_part(core, near, far, bias, rate):
    rows, heads = 2 * near.shape[0], near.shape[1]
    spec = pltpu.PrefetchScalarGridSpec(
        num_scalar_prefetch=1,
        grid=(1,),
        in_specs=[whole(near.shape), whole(far.shape), whole(bias.shape), whole(rate.shape)],
        out_specs=[whole((rows, heads)), whole((rows, heads)), whole((rows // Q, heads, Q))],
    )
    return pl.pallas_call(
        functools.partial(step_kernel, rows // Q),
        grid_spec=spec,
        out_shape=[
            jax.ShapeDtypeStruct((rows, heads), F32),
            jax.ShapeDtypeStruct((rows, heads), F32),
            jax.ShapeDtypeStruct((rows // Q, heads, Q), F32),
        ],
        compiler_params=params("arbitrary"),
        cost_estimate=cost(rows * heads * Q, 200),
        name="step_part",
    )(core, near, far, bias, rate)


def local_kernel(
    heads, core_ref, near_ref, far_ref, b_ref, c_ref, step_ref, cum_ref, cum_t_ref, skip_ref,
    pattern_ref, top_ref, low_ref, ssd_ref, state_ref, sent_ref, x_ref, total_ref,
):
    block = pl.program_id(1)
    core = core_ref[0]
    quarter = core * pl.num_programs(0) + pl.program_id(0)
    x_ref[...] = jnp.where(
        block // (pl.num_programs(1) // 2) == core, near_ref[...], far_ref[...]
    )
    pattern = pattern_ref[...]
    step = of_quarter(step_ref, slice(None), quarter, heads)
    cum = of_quarter(cum_ref, slice(None), quarter, heads)
    start = pl.multiple_of(quarter * heads, 8)
    cum_t = cum_t_ref[0, pl.ds(start, heads), :]
    last = cum[Q - 1 : Q, :]
    step_wide = spread(step, pattern)
    weight = spread(step * jnp.exp(last - cum), pattern)
    decay = spread(jnp.broadcast_to(jnp.exp(last), (8, heads)), pattern)[:1, :]
    x = x_ref[...].astype(F32)
    xdt = (x * step_wide).astype(BF16)
    state = dot(b_ref[...], (x * weight).astype(BF16), ((0,), (0,)))
    state_ref[...] = state

    @pl.when(block == 0)
    def _():
        total_ref[...] = state

    @pl.when(block > 0)
    def _():
        total_ref[...] = total_ref[...] * decay + state

    sent_ref[...] = total_ref[...].astype(sent_ref.dtype)

    half = Q // 2
    inner = dot(b_ref[...], c_ref[...], ((1,), (1,)))
    causal = lax.broadcasted_iota(jnp.int32, (half, half), 1) >= lax.broadcasted_iota(
        jnp.int32, (half, half), 0
    )
    corner = jnp.where(causal, inner[:half, :half], 0.0)
    right = inner[:half, half:]
    end = jnp.where(causal, inner[half:, half:], 0.0)
    for pair in range(heads // 2):
        corners, rights = [], []
        for head in (2 * pair, 2 * pair + 1):
            across, down = cum_t[head : head + 1, :], cum[:, head : head + 1]
            gap = across[:, :half] - down[:half, :]
            first = (corner * jnp.exp(jnp.where(causal, gap, 0.0))).astype(BF16)
            second = (right * jnp.exp(across[:, half:] - down[:half, :])).astype(BF16)
            gap = across[:, half:] - down[half:, :]
            third = (end * jnp.exp(jnp.where(causal, gap, 0.0))).astype(BF16)
            top_ref[:, head * Q : head * Q + half] = first
            top_ref[:, head * Q + half : (head + 1) * Q] = second
            low_ref[:, head * half : (head + 1) * half] = third
            corners.append(first)
            rights += [second, third]
        lanes = slice(pair * 2 * P_SIZE, (pair + 1) * 2 * P_SIZE)
        values = xdt[:, lanes]
        intra = (
            dot(jnp.concatenate(corners, axis=0), pair_rows(values[:half, :]), ((0,), (0,))),
            dot(jnp.concatenate(rights, axis=0), pair_rows(values), ((0,), (0,))),
        )
        for part, rows in zip(intra, (slice(0, half), slice(half, Q))):
            ssd_ref[rows, lanes] = (
                part + skip_ref[:, lanes] * x_ref[rows, lanes].astype(F32)
            ).astype(ssd_ref.dtype)


def local_part(groups, heads, core, near, far, b, c, step, cum, cum_t, skip, pattern):
    rows = 2 * near.shape[0]
    blocks = rows // Q
    width = heads * P_SIZE
    row_block = pl.BlockSpec((Q, width), lambda g, i, s: (g * blocks + i, 0))
    spec = pltpu.PrefetchScalarGridSpec(
        num_scalar_prefetch=1,
        grid=(groups, blocks),
        in_specs=[
            pl.BlockSpec((Q, width), lambda g, i, s: (i % (blocks // 2), s[0] * groups + g)),
            pl.BlockSpec((Q, width), lambda g, i, s: (i % (blocks // 2), g)),
            pl.BlockSpec((Q, N), lambda g, i, s: (i, g)),
            pl.BlockSpec((Q, N), lambda g, i, s: (i, g)),
            pl.BlockSpec((Q, step.shape[1]), lambda g, i, s: (i, 0)),
            pl.BlockSpec((Q, step.shape[1]), lambda g, i, s: (i, 0)),
            pl.BlockSpec((1,) + cum_t.shape[1:], lambda g, i, s: (i, 0, 0)),
            pl.BlockSpec((1, width), lambda g, i, s: (0, s[0] * groups + g)),
            whole(pattern.shape),
        ],
        out_specs=[
            pl.BlockSpec((Q // 2, heads * Q), lambda g, i, s: (g * blocks + i, 0)),
            pl.BlockSpec((Q // 2, heads * Q // 2), lambda g, i, s: (g * blocks + i, 0)),
            row_block,
            pl.BlockSpec((N, width), lambda g, i, s: (g * blocks + i, 0)),
            pl.BlockSpec((N, width), lambda g, i, s: (g, 0)),
        ],
        scratch_shapes=[pltpu.VMEM((Q, width), BF16), pltpu.VMEM((N, width), F32)],
    )
    return pl.pallas_call(
        functools.partial(local_kernel, heads),
        grid_spec=spec,
        out_shape=[
            pltpu.HBM((groups * rows // 2, heads * Q), BF16),
            pltpu.HBM((groups * rows // 2, heads * Q // 2), BF16),
            jax.ShapeDtypeStruct((groups * rows, width), BF16),
            jax.ShapeDtypeStruct((groups * blocks * N, width), F32),
            jax.ShapeDtypeStruct((groups * N, width), BF16),
        ],
        compiler_params=params("arbitrary", "arbitrary"),
        cost_estimate=cost(groups * rows * width * Q * 4, 16),
        name="local_part",
    )(core, near, far, b, c, step, cum, cum_t, skip, pattern)


def norm_kernel(
    blocks, heads, core_ref, c_ref, incoming_ref, state_ref, cum_ref, pattern_ref, ssd_ref, near_ref,
    far_ref, gain_ref, down_ref, up_ref, hat_ref, slope_ref, product_ref, sum_ref,
):
    gain = gain_ref[...]
    group = pl.program_id(0)
    quarter = core_ref[0] * pl.num_programs(0) + group
    run = incoming_ref[...].astype(F32)
    total = None
    for block in range(blocks):
        rows = slice(block * Q, (block + 1) * Q)
        inter = dot(c_ref[rows, :], run.astype(BF16))
        growth = spread(jnp.exp(of_quarter(cum_ref, rows, quarter, heads)), pattern_ref[...])
        ssd = ssd_ref[rows, :].astype(F32) + growth * inter
        local = slice(block % (blocks // 2) * Q, (block % (blocks // 2) + 1) * Q)
        z = jnp.where(
            core_ref[0] == block // (blocks // 2), near_ref[local, :], far_ref[local, :]
        ).astype(F32)
        silu = z / (1.0 + jnp.exp(-z))
        gated = ssd * silu
        rstd = lax.rsqrt(jnp.mean(gated * gated, axis=1, keepdims=True) + EPS_NORM)
        hat = gated * rstd
        normed = (hat * gain).astype(BF16)
        hat_ref[rows, :] = hat.astype(hat_ref.dtype)
        slope_ref[rows, :] = (rstd * silu).astype(slope_ref.dtype)
        product = dot(normed, down_ref[...], ((1,), (1,)))
        product_ref[rows, :] = jnp.where(group == 0, product, product_ref[rows, :] + product)
        part = dot(up_ref[rows, :], normed, ((0,), (0,)))
        total = part if total is None else total + part
        if block + 1 < blocks:
            states = slice(block * N, (block + 1) * N)
            run = run * growth[Q - 1 :, :] + state_ref[states, :]
    sum_ref[...] = total


def norm_part(groups, heads, core, c, incoming, state, cum, pattern, ssd, near, far, gain, down, up_twice):
    rows, width = 2 * near.shape[0], heads * P_SIZE
    rank = down.shape[0]
    blocks = rows // Q
    group_rows = pl.BlockSpec((rows, width), lambda g, s: (g, 0))
    spec = pltpu.PrefetchScalarGridSpec(
        num_scalar_prefetch=1,
        grid=(groups,),
        in_specs=[
            pl.BlockSpec((rows, N), lambda g, s: (0, g)),
            pl.BlockSpec((N, width), lambda g, s: (g, 0)),
            pl.BlockSpec((blocks * N, width), lambda g, s: (g, 0)),
            whole(cum.shape),
            whole(pattern.shape),
            group_rows,
            pl.BlockSpec((rows // 2, width), lambda g, s: (0, s[0] * groups + g)),
            pl.BlockSpec((rows // 2, width), lambda g, s: (0, g)),
            pl.BlockSpec((1, width), lambda g, s: (0, s[0] * groups + g)),
            pl.BlockSpec((rank, width), lambda g, s: (0, s[0] * groups + g)),
            whole(up_twice.shape),
        ],
        out_specs=[
            group_rows,
            group_rows,
            whole((rows, rank)),
            pl.BlockSpec((rank, width), lambda g, s: (0, g)),
        ],
    )
    return pl.pallas_call(
        functools.partial(norm_kernel, blocks, heads),
        grid_spec=spec,
        out_shape=[
            jax.ShapeDtypeStruct((groups * rows, width), BF16),
            jax.ShapeDtypeStruct((groups * rows, width), BF16),
            jax.ShapeDtypeStruct((rows, rank), F32),
            jax.ShapeDtypeStruct((rank, groups * width), F32),
        ],
        compiler_params=params("arbitrary"),
        cost_estimate=cost(groups * rows * width * 512, 12),
        name="norm_part",
    )(core, c, incoming, state, cum, pattern, ssd, near, far, gain, down, up_twice)


def product_kernel(first, spans, started, core_ref, near_ref, far_ref, *rest):
    pieces, out_ref = rest[started:-1], rest[-1]
    weights = joined(pieces, spans)
    depth = slice(first, first + weights.shape[0])
    half = near_ref.shape[0]
    for part in range(2):
        rows = slice(part * half, (part + 1) * half)
        cot = jnp.where(core_ref[0] == part, near_ref[:, depth], far_ref[:, depth])
        product = dot(cot, weights)
        out_ref[rows, :] = product + rest[0][rows, :] if started else product


def joined(pieces, spans):
    return jnp.concatenate(
        [piece[start : start + rows, :] for piece, (start, rows) in zip(pieces, spans)], axis=0
    )


def product_part(core, near, far, cut, first, earlier, pieces, width):
    rows = 2 * near.shape[0]
    held = [] if earlier is None else [earlier]
    columns = pl.BlockSpec((near.shape[0], cut), lambda i, s: (0, near.shape[1] // cut - 1))
    spec = pltpu.PrefetchScalarGridSpec(
        num_scalar_prefetch=1,
        grid=(1,),
        in_specs=[columns, columns]
        + [whole(array.shape) for array in held]
        + [whole(piece[0].shape) for piece in pieces],
        out_specs=whole((rows, width)),
    )
    return pl.pallas_call(
        functools.partial(product_kernel, first, tuple(piece[1:] for piece in pieces), len(held)),
        grid_spec=spec,
        out_shape=jax.ShapeDtypeStruct((rows, width), F32),
        input_output_aliases={3: 0} if held else {},
        compiler_params=params("arbitrary"),
        cost_estimate=cost(2 * rows * width * Q, 4),
        name="product_part",
    )(core, near, far, *held, *[piece[0] for piece in pieces])


def grad_kernel(
    blocks, first, heads, start, spans, core_ref, near_ref, far_ref, earlier_ref, up_ref, down_ref, gain_ref, hat_ref,
    slope_ref, cum_ref, pattern_ref, c_ref, *rest,
):
    pieces, (grad_ref, block_grad_ref, total_ref) = rest[:-3], rest[-3:]
    weights = joined(pieces, spans)
    depth = slice(start, start + weights.shape[0])
    gain = gain_ref[...]
    later = None
    for block in reversed(range(blocks)):
        rows = slice(block * Q, (block + 1) * Q)
        local = slice(block % (blocks // 2) * Q, (block % (blocks // 2) + 1) * Q)
        cot = jnp.where(
            core_ref[0] == block // (blocks // 2), near_ref[local, depth], far_ref[local, depth]
        )
        product = dot(cot, weights) + dot(up_ref[rows, :], down_ref[...]) + earlier_ref[rows, :]
        weighted = product * gain
        hat = hat_ref[rows, :].astype(F32)
        mean = jnp.mean(hat * weighted, axis=1, keepdims=True)
        grad = slope_ref[rows, :].astype(F32) * (weighted - hat * mean)
        grad_ref[rows, :] = grad.astype(grad_ref.dtype)
        growth = spread(jnp.exp(of_core(cum_ref, rows, core_ref[0], first, heads)), pattern_ref[...])
        fresh = dot(c_ref[rows, :], (growth * grad).astype(BF16), ((0,), (0,)))
        block_grad_ref[block * N : (block + 1) * N, :] = fresh
        later = (
            fresh
            if later is None
            else later * growth[Q - 1 :, :] + fresh
        )
    total_ref[...] = later.astype(BF16)


def grad_part(
    group, groups, heads, core, near, far, cut, start, earlier, up_twice, down, gain, hat, slope, cum, pattern, c, pieces
):
    rows, width = earlier.shape
    rank = down.shape[0]
    blocks = rows // Q
    columns = pl.BlockSpec((near.shape[0], cut), lambda i, s: (0, near.shape[1] // cut - 1))
    spec = pltpu.PrefetchScalarGridSpec(
        num_scalar_prefetch=1,
        grid=(1,),
        in_specs=[
            columns,
            columns,
            whole(earlier.shape),
            whole(up_twice.shape),
            pl.BlockSpec((rank, width), lambda i, s: (0, s[0] * groups + group)),
            pl.BlockSpec((1, width), lambda i, s: (0, s[0] * groups + group)),
            pl.BlockSpec((rows, width), lambda i, s: (group, 0)),
            pl.BlockSpec((rows, width), lambda i, s: (group, 0)),
            whole(cum.shape),
            whole(pattern.shape),
            pl.BlockSpec((rows, N), lambda i, s: (0, group)),
        ]
        + [whole(piece[0].shape) for piece in pieces],
        out_specs=[whole((rows, width)), whole((blocks * N, width)), whole((N, width))],
    )
    return pl.pallas_call(
        functools.partial(
            grad_kernel, blocks, group * heads, heads, start, tuple(piece[1:] for piece in pieces)
        ),
        grid_spec=spec,
        out_shape=[
            jax.ShapeDtypeStruct((rows, width), BF16),
            jax.ShapeDtypeStruct((blocks * N, width), F32),
            jax.ShapeDtypeStruct((N, width), BF16),
        ],
        compiler_params=params("arbitrary"),
        cost_estimate=cost(2 * rows * width * Q, 8),
        name="grad_part",
    )(
        core, near, far, earlier, up_twice, down, gain, hat, slope, cum, pattern, c,
        *[piece[0] for piece in pieces],
    )


def back_kernel(
    first, heads, core_ref, top_ref, low_ref, grad_ref, step_ref, pattern_ref, skip_ref, out_ref
):
    half = Q // 2
    step = of_core(step_ref, slice(None), core_ref[0], first, heads)
    out_ref[...] = spread(step, pattern_ref[...])
    for pair in range(heads // 2):
        lanes = slice(pair * 2 * P_SIZE, (pair + 1) * 2 * P_SIZE)
        grad = grad_ref[:, lanes]
        back = (
            dot(top_ref[:, 2 * pair * Q : 2 * (pair + 1) * Q], pair_rows(grad)),
            dot(low_ref[:, 2 * pair * half : 2 * (pair + 1) * half], pair_rows(grad[half:, :])),
        )
        for part, rows in zip(back, (slice(0, half), slice(half, Q))):
            out_ref[rows, lanes] = out_ref[rows, lanes] * part + skip_ref[:, lanes] * grad_ref[
                rows, lanes
            ].astype(F32)


def back_part(group, groups, heads, core, top, low, grad, step, pattern, skip):
    rows, width = grad.shape
    row_block = pl.BlockSpec((Q, width), lambda i, s: (i, 0))
    spec = pltpu.PrefetchScalarGridSpec(
        num_scalar_prefetch=1,
        grid=(rows // Q,),
        in_specs=[
            pl.BlockSpec((Q // 2, heads * Q), lambda i, s: (group * (rows // Q) + i, 0)),
            pl.BlockSpec((Q // 2, heads * Q // 2), lambda i, s: (group * (rows // Q) + i, 0)),
            row_block,
            pl.BlockSpec((Q, step.shape[1]), lambda i, s: (i, 0)),
            whole(pattern.shape),
            pl.BlockSpec((1, width), lambda i, s: (0, s[0] * groups + group)),
        ],
        out_specs=row_block,
    )
    return pl.pallas_call(
        functools.partial(back_kernel, group * heads, heads),
        grid_spec=spec,
        out_shape=jax.ShapeDtypeStruct((rows, width), F32),
        compiler_params=params("arbitrary"),
        cost_estimate=cost(rows * width * Q * 2, 8),
        name="back_part",
    )(core, top, low, grad, step, pattern, skip)


def cross_kernel(
    blocks, first, heads, core_ref, b_ref, outgoing_ref, block_grad_ref, step_ref, cum_ref, pattern_ref,
    base_ref, near_ref, far_ref,
):
    run = outgoing_ref[...].astype(F32)
    for block in reversed(range(blocks)):
        rows = slice(block * Q, (block + 1) * Q)
        local = slice(block % (blocks // 2) * Q, (block % (blocks // 2) + 1) * Q)
        cross = dot(b_ref[rows, :], run.astype(BF16))
        cum = of_core(cum_ref, rows, core_ref[0], first, heads)
        last = cum[Q - 1 :, :]
        step = of_core(step_ref, rows, core_ref[0], first, heads)
        weight = spread(step * jnp.exp(last - cum), pattern_ref[...])
        value = (base_ref[rows, :] + weight * cross).astype(near_ref.dtype)
        own = core_ref[0] == block // (blocks // 2)

        @pl.when(own)
        def _():
            near_ref[local, :] = value

        @pl.when(jnp.logical_not(own))
        def _():
            far_ref[local, :] = value

        if block > 0:
            states = slice(block * N, (block + 1) * N)
            decay = spread(jnp.broadcast_to(jnp.exp(last), (8, heads)), pattern_ref[...])[:1, :]
            run = run * decay + block_grad_ref[states, :]


def cross_part(group, heads, core, b, outgoing, block_grad, step, cum, pattern, base):
    rows, width = base.shape
    blocks = rows // Q
    spec = pltpu.PrefetchScalarGridSpec(
        num_scalar_prefetch=1,
        grid=(1,),
        in_specs=[
            pl.BlockSpec((rows, N), lambda i, s: (0, group)),
            whole(outgoing.shape),
            whole(block_grad.shape),
            whole(step.shape),
            whole(cum.shape),
            whole(pattern.shape),
            whole(base.shape),
        ],
        out_specs=[whole((rows // 2, width))] * 2,
    )
    return pl.pallas_call(
        functools.partial(cross_kernel, blocks, group * heads, heads),
        grid_spec=spec,
        out_shape=[jax.ShapeDtypeStruct((rows // 2, width), BF16)] * 2,
        compiler_params=params("arbitrary"),
        cost_estimate=cost(rows * width * N * 2, 6),
        name="cross_part",
    )(core, b, outgoing, block_grad, step, cum, pattern, base)


def ring_order(count):
    return list(range(0, count, 2)) + list(range(count - 1 - count % 2, 0, -2))


def rotations(count):
    return [[(i, (i + k) % count) for i in range(count)] for k in range(count)]


def chip_order():
    ring, across = lax.axis_size("dp"), lax.axis_size("x")
    offsets = [0]
    for distance in range(1, (ring - 1) // 2 + 1):
        offsets += [-distance, distance]
    if ring % 2 == 0:
        offsets.append(ring // 2)
    me, x = lax.axis_index("dp"), lax.axis_index("x")
    seat = jnp.where(me % 2 == 0, me // 2, ring - (me + 1) // 2)

    def member(place):
        return jnp.where(place < (ring + 1) // 2, 2 * place, 2 * (ring - place) - 1)

    return [
        [member((seat + offset + ring) % ring) * across + (x - k + across) % across for k in range(across)]
        for offset in offsets
    ]


def ring_perms():
    ring = lax.axis_size("dp")
    order = ring_order(ring)
    ahead = [(order[i], order[(i + 1) % ring]) for i in range(ring)]
    return ahead, [(b, a) for a, b in ahead]


def cut_kernel(plans, count, *refs):
    arrays, outs = refs[:count], refs[count:]
    for out, plan in zip(outs, plans):
        row = 0
        for index, start, rows, column in plan:
            out[row : row + rows, :] = arrays[index][
                start : start + rows, column : column + out.shape[1]
            ]
            row += rows


def cut(arrays, plans, width):
    return small_call(
        functools.partial(cut_kernel, plans, len(arrays)),
        [],
        arrays,
        [
            jax.ShapeDtypeStruct((sum(part[2] for part in plan), width), arrays[0].dtype)
            for plan in plans
        ],
        "cut_rows",
    )


class Gather:
    def __init__(self, shard):
        self.ring = lax.axis_size("dp")
        self.across = lax.axis_size("x")
        self.turns = rotations(self.across)[1:]
        self.perms = ring_perms()
        self.shard = shard
        self.size = shard.shape[0]
        self.width = shard.shape[1] // 2
        late = shard[:, self.width :]
        self.late = [(late, 0, self.size)] * 2
        self.moving = [late, late]
        self.crossing = shard
        self.pieces = {}
        self.steps = self.ring // 2 + 2

    def sizes(self, index):
        early = 0 if index == 1 else self.across * self.size
        late = self.size
        if 2 * index == self.ring:
            late //= 2
        elif 2 * index > self.ring:
            early, late = early // 2, 0
        return early, late

    def step(self, index, beside):
        ring, size, width = self.ring, self.size, self.width
        early_size, late_size = self.sizes(index)
        got = tuple(lax.ppermute(array, "dp", perm) for array, perm in zip(self.moving, self.perms))
        crossed = tuple(lax.ppermute(self.crossing, "x", turn) for turn in self.turns)
        values = beside()
        got, crossed, values = lax.optimization_barrier((got, crossed, values))
        late = [(got[0], early_size, late_size), (got[1], 0, late_size)]
        early = [(got[0], 0, early_size), (got[1], late_size, early_size)]
        after_early, after_late = self.sizes(index + 1)
        more = index + 1 < self.steps
        if index == 1:
            first = [(0, 0, size, 0)] + [(1 + k, 0, size, 0) for k in range(len(crossed))]
            base = 1 + len(crossed)
            self.first, *rest = cut(
                [self.shard, *crossed, *got],
                [
                    first,
                    first + [(base, 0, after_late, 0)],
                    [(base + 1, size - after_late, after_late, 0)] + first,
                    [(base, 0, size, 0), (base + 1, 0, size, 0)],
                ],
                width,
            )
            self.moving, self.crossing = rest[:2], rest[2]
            met = [array[:, width:] for array in crossed]
            self.pieces[0] = [
                [(self.first, 0, self.first.shape[0])],
                [self.late[0]] + [(array, 0, size) for array in met],
            ]
        else:
            distance = index - 1
            if 2 * distance < ring:
                for side in range(2):
                    self.pieces[2 * distance - 1 + side] = [
                        [early[side]],
                        [self.late[side]] + [(array, side * size, size) for array in crossed],
                    ]
            else:
                self.pieces[2 * distance - 1] = [
                    early, self.late + [(array, 0, size) for array in crossed]
                ]
            if more:
                plans = [[(0, early_size, late_size, 0), (1, 0, late_size, 0)]]
                whole_array = (after_early, after_late) == (early_size, late_size)
                if not whole_array:
                    plans += [
                        [(0, 0, after_early, 0), (0, early_size, after_late, 0)],
                        [
                            (1, late_size - after_late, after_late, 0),
                            (1, late_size + early_size - after_early, after_early, 0),
                        ],
                    ]
                plans = [[part for part in plan if part[2]] for plan in plans]
                self.crossing, *moving = cut(list(got), plans, width)
                self.moving = moving or list(got)
                self.crossing, self.moving = lax.optimization_barrier((self.crossing, self.moving))
        self.late = late
        return values


def down_kernel(core_ref, product_ref, arrived_ref, cot_ref, own_ref, sent_ref):
    down = (product_ref[...] + arrived_ref[...]).astype(BF16)
    half = own_ref.shape[1]
    parts = [
        ADAPTER_SCALE * dot(down, cot_ref[:, part * half : (part + 1) * half], ((0,), (0,)))
        for part in range(2)
    ]
    own_ref[...] = jnp.where(core_ref[0] == 0, parts[0], parts[1])
    sent_ref[...] = jnp.where(core_ref[0] == 0, parts[1], parts[0]).astype(sent_ref.dtype)


def down_part(core, product, arrived, cot):
    shape = (product.shape[1], cot.shape[1] // 2)
    return small_call(
        down_kernel,
        [core],
        [product, arrived, cot],
        [jax.ShapeDtypeStruct(shape, F32), jax.ShapeDtypeStruct(shape, BF16)],
        "down_part",
    )


def pack_kernel(ring, across, place_ref, sum_ref, own_ref, far_ref, mine_ref, *sent_refs):
    other = own_ref[...] + far_ref[...].astype(F32)
    width_a = sum_ref.shape[1] // (ring * across)
    width_b = other.shape[1] // (ring * across)
    for member in range(ring):
        blocks = []
        for x in range(across):
            chip = member * across + x
            part = sum_ref[:, chip * width_a : (chip + 1) * width_a]
            blocks.append((part, other[:, chip * width_b : (chip + 1) * width_b]))
        for turn in range(across):
            target = (place_ref[1] + turn) % across
            chosen = blocks[0]
            for x in range(1, across):
                chosen = [jnp.where(target == x, new, old) for new, old in zip(blocks[x], chosen)]
            out = mine_ref if turn == 0 else sent_refs[turn - 1]
            out[member, :, :width_a] = chosen[0].astype(out.dtype)
            out[member, :, width_a:] = chosen[1].astype(out.dtype)


def halve_kernel(bit_ref, mine_ref, *refs):
    arrived, (kept_ref, sent_ref) = refs[:-2], refs[-2:]
    half = kept_ref.shape[0]
    for out, start in ((kept_ref, bit_ref[0] * half), (sent_ref, (1 - bit_ref[0]) * half)):
        total = mine_ref[pl.ds(start, half)]
        for ref in arrived:
            total = total + ref[pl.ds(start, half)].astype(F32)
        out[...] = total.astype(out.dtype)


def add_kernel(mine_ref, arrived_ref, total_ref, sent_ref):
    total = mine_ref[...] + arrived_ref[...].astype(F32)
    total_ref[...] = total
    sent_ref[...] = total.astype(sent_ref.dtype)


def total_kernel(width_a, place_ref, mine_ref, arrived_ref, total_ref, square_ref):
    total = mine_ref[...] + arrived_ref[...].astype(F32)
    squares = total * total
    lane = lax.broadcasted_iota(jnp.int32, squares.shape, 2)
    first = jnp.sum(jnp.where(lane < width_a, squares, 0.0))
    second = jnp.sum(jnp.where(lane >= width_a, squares, 0.0))
    column = lax.broadcasted_iota(jnp.int32, square_ref.shape, 1)
    square_ref[...] = jnp.where(column == 0, first, jnp.where(column == 1, second, 0.0))
    own = place_ref[0] % mine_ref.shape[0]
    total_ref[...] = mine_ref[own] + arrived_ref[own].astype(F32)


def small_call(kernel, scalars, arrays, outs, name):
    spec = pltpu.PrefetchScalarGridSpec(
        num_scalar_prefetch=len(scalars),
        grid=(1,),
        in_specs=[whole(array.shape) for array in arrays],
        out_specs=[whole(out.shape) for out in outs],
    )
    return pl.pallas_call(
        kernel,
        grid_spec=spec,
        out_shape=outs,
        compiler_params=params("arbitrary"),
        cost_estimate=cost(10**9, 1),
        name=name,
    )(*scalars, *arrays)


def packed(sum_a, own_b, far_b):
    ring, across = lax.axis_size("dp"), lax.axis_size("x")
    place = jnp.stack([lax.axis_index("dp"), lax.axis_index("x")]).astype(jnp.int32)
    count = ring * across
    shape = (ring, own_b.shape[0], (sum_a.shape[1] + own_b.shape[1]) // count)
    mine, *sent = small_call(
        functools.partial(pack_kernel, ring, across),
        [place],
        [sum_a, own_b, far_b],
        [jax.ShapeDtypeStruct(shape, F32)] + [jax.ShapeDtypeStruct(shape, BF16)] * (across - 1),
        "pack_sums",
    )
    return mine, sent


def halved(mine, arrived, distance):
    shape = (distance,) + mine.shape[1:]
    return small_call(
        halve_kernel,
        [((lax.axis_index("dp") // distance) % 2).astype(jnp.int32)[None]],
        [mine, *arrived],
        [jax.ShapeDtypeStruct(shape, F32), jax.ShapeDtypeStruct(shape, BF16)],
        "halve_sums",
    )


def over_x(sent):
    return [lax.ppermute(value, "x", turn) for value, turn in zip(sent, rotations(lax.axis_size("x"))[1:])]


def far_in_dp(value, distance):
    return lax.ppermute(value, "dp", [(i, i ^ distance) for i in range(lax.axis_size("dp"))])


def added(mine, arrived):
    return small_call(
        add_kernel,
        [],
        [mine, arrived],
        [jax.ShapeDtypeStruct(mine.shape, F32), jax.ShapeDtypeStruct(mine.shape, BF16)],
        "add_sums",
    )


def totals(mine, arrived, width_a):
    return small_call(
        functools.partial(total_kernel, width_a),
        [lax.axis_index("dp").astype(jnp.int32)[None]],
        [mine, arrived],
        [jax.ShapeDtypeStruct(mine.shape[1:], F32), jax.ShapeDtypeStruct((8, 128), F32)],
        "total_sums",
    )


def finish_kernel(entries, total_ref, square_ref, first_ref, second_ref):
    width = first_ref.shape[1]
    for out, count, column, lanes in (
        (first_ref, entries[0], 0, slice(0, width)),
        (second_ref, entries[1], 1, slice(width, width + second_ref.shape[1])),
    ):
        mean = square_ref[0:1, column : column + 1] / count
        out[...] = total_ref[:, lanes] / jnp.maximum(1.0, jnp.sqrt(mean + CLIP_EPSILON))


def finished(total, squares, width_a):
    rank, width = total.shape
    devices = lax.axis_size(AXES)
    widths = (width_a, width - width_a)
    return small_call(
        functools.partial(finish_kernel, tuple(float(rank * part * devices) for part in widths)),
        [],
        [total, squares],
        [jax.ShapeDtypeStruct((rank, part), F32) for part in widths],
        "finish",
    )


def over_axis(value, axis):
    turns = rotations(lax.axis_size(axis))[1:]
    return functools.reduce(jnp.add, [lax.ppermute(value, axis, turn) for turn in turns], value)


def on_device(
    state_input, gate_values, input_matrix, readout_matrix, step_unbiased, step_bias,
    decay_rate_log, skip_coefficients, norm_gain, adapter_down, adapter_up, projection_weight,
    output_cotangent,
):
    ring, across = lax.axis_size("dp"), lax.axis_size("x")
    core = lax.axis_index("core")
    swap = [(0, 1), (1, 0)]
    near_rows = state_input.shape[0]
    groups = G // 2
    heads = step_bias.shape[0] // G
    width = heads * P_SIZE

    def half(value, which, axis=-1):
        size = value.shape[axis] // 2
        return lax.dynamic_slice_in_dim(value, which * size, size, axis)

    def in_order(near, far, axis=0):
        return jnp.concatenate(
            [jnp.where(core == 0, near, far), jnp.where(core == 0, far, near)], axis=axis
        )

    def swapped(value):
        return lax.ppermute(value, "core", swap)

    sent_weight = half(projection_weight, 1 - core)
    sent_weight, state_input, step_unbiased, input_matrix, readout_matrix = lax.optimization_barrier(
        (sent_weight, state_input, step_unbiased, input_matrix, readout_matrix)
    )
    shard = in_order(half(projection_weight, core), swapped(sent_weight))
    raw_far = swapped(step_unbiased)
    x_far = swapped(
        jnp.concatenate(
            [half(value, 1 - core) for value in (state_input, input_matrix, readout_matrix)], axis=1
        )
    )
    shard, gate_values, output_cotangent = lax.optimization_barrier(
        (shard, gate_values, output_cotangent)
    )
    which = core.astype(jnp.int32)[None]
    chips = chip_order()
    chip_rows = shard.shape[0]
    slots = list(range(len(chips)))
    stages = [slots[:3], slots[3:5], slots[5:7], slots[7:]] if len(slots) > 7 else [slots[:1], slots[1:]]
    rows = 2 * near_rows
    blocks = rows // Q
    gather = Gather(shard)
    forward = [(i, i + 1) for i in range(across - 1)]
    backward = [(i + 1, i) for i in range(across - 1)]

    def staged(index, group):
        return [piece for slot in stages[index] for piece in gather.pieces[slot][group]]

    def depth(index):
        return sum(len(stage) for stage in stages[:index]) * across * chip_rows

    def carried(fresh, cum, perm, group=None):
        sent = fresh
        for lap in range(across - 1):
            arrived = lax.ppermute(sent, "x", perm)
            if lap + 2 < across:
                total = jnp.sum(cum.reshape(blocks, Q, -1)[:, Q - 1], axis=0)
                decay = jnp.repeat(jnp.exp(half(total, core)).reshape(groups, 1, heads), P_SIZE, axis=2)
                if group is not None:
                    decay = decay[group : group + 1]
                parts = [value.astype(F32).reshape(-1, N, width) for value in (arrived, fresh)]
                sent = (parts[0] * decay + parts[1]).astype(BF16).reshape(fresh.shape)
        return arrived

    skip = jnp.repeat(skip_coefficients, P_SIZE)[None, :]
    gain = norm_gain[None, :]
    pattern = spread_pattern(heads)

    def prepare():
        step, cum, cum_t = step_part(
            which, step_unbiased, raw_far, step_bias[None, :], decay_rate_log[None, :]
        )
        cut = groups * width
        b = in_order(half(input_matrix, core), x_far[:, cut : cut + groups * N])
        c = in_order(half(readout_matrix, core), x_far[:, cut + groups * N :])
        local = local_part(
            groups, heads, which, state_input, x_far, b, c, step, cum, cum_t, skip, pattern
        )
        return step, cum, cum_t, b, c, local

    step, cum, cum_t, b, c, local = gather.step(1, prepare)

    def second():
        ssd, state, fresh = local[2:]
        up_near = (
            ADAPTER_SCALE * dot(output_cotangent, adapter_up, ((1,), (1,))).astype(BF16)
        ).astype(BF16)
        parts = [
            lax.dynamic_slice_in_dim(output_cotangent, chip * chip_rows, chip_rows, 1)
            for offset in chips
            for chip in offset
        ]
        near = jnp.concatenate([half(gate_values, 1 - core)] + parts, axis=1)
        up_near, fresh = lax.optimization_barrier((up_near, fresh))
        incoming = carried(fresh, cum, forward)
        up_twice = in_order(up_near, swapped(up_near))
        far = swapped(near)
        hat, slope, product, sum_a = norm_part(
            groups, heads, which, c, incoming, state, cum, pattern, ssd, gate_values, far, gain, adapter_down,
            up_twice,
        )
        far_product = swapped(half(product, 1 - core, 0))
        return up_twice, near, far, (hat, slope), sum_a, half(product, core, 0), far_product

    up_twice, cot_near, cot_far, normed, sum_a, product, far_product = gather.step(2, second)
    cot_width = output_cotangent.shape[1]

    def during(index, beside):
        return gather.step(index, beside) if gather.steps > index else beside()

    distances = [ring >> k for k in range(1, ring.bit_length())]

    def third():
        own_b, sent_b = down_part(which, product, far_product, output_cotangent)
        mine, sent = packed(sum_a, own_b, swapped(sent_b))
        return mine, over_x(sent)

    mine, sent = during(3, third)

    def products(indices, earlier):
        for index in indices:
            earlier = [
                product_part(
                    which, cot_near, cot_far, cot_width, depth(index), earlier[group], staged(index, group), width
                )
                for group in range(groups)
            ]
        return earlier

    def doubled(value, rounded, hops):
        for distance in hops:
            value, rounded = added(value, far_in_dp(rounded, distance))
        return value, rounded

    def fourth():
        held = list(range(len(stages) - 1))[:2]
        halves = halved(mine, sent, distances[0])
        return doubled(*halves, distances[:-2]), products(held, [None] * groups)

    (mine, sent), earlier = during(4, fourth)
    width_a = 2 * width // (ring * across)

    def fifth():
        held = list(range(len(stages) - 1))[2:]
        return doubled(mine, sent, distances[:-1][-1:]), products(held, earlier)

    (mine, sent), earlier = during(5, fifth)
    for index in range(6, gather.steps):
        gather.step(index, lambda: ())
    arrived = far_in_dp(sent, distances[-1])

    grads = [
        grad_part(
            group, groups, heads, which, cot_near, cot_far, cot_width, depth(len(stages) - 1), earlier[group],
            up_twice, adapter_down, gain, *normed, cum, pattern, c, staged(len(stages) - 1, group),
        )
        for group in range(groups)
    ]
    arrived, grads = lax.optimization_barrier((arrived, grads))
    outgoing = [carried(part[2], cum, backward, group) for group, part in enumerate(grads)]
    total, squares = totals(mine, arrived, width_a)

    def back(group):
        return back_part(
            group, groups, heads, which, *local[:2], grads[group][0], step, pattern, skip
        )

    count = ring * across
    homes = [
        (chip * 2 + number, number * count + chip) for chip in range(count) for number in range(2)
    ]
    squares = squares + far_in_dp(squares, distances[0])
    bases = [back(0)]
    squares, bases, grads = lax.optimization_barrier((squares, bases, grads))
    squares = over_axis(squares, "core")
    total = lax.ppermute(total, AXES, homes)
    bases.append(back(1))
    squares, bases, total = lax.optimization_barrier((squares, bases, total))
    squares = over_axis(squares, "x")
    near, far = [], []
    for group in range(groups):
        if group == groups - 1:
            squares, bases, total = lax.optimization_barrier((squares, bases, total))
        own, others = cross_part(
            group, heads, which, b, outgoing[group], grads[group][1], step, cum, pattern, bases[group]
        )
        far.append(swapped(others))
        near.append(own)
    gradient_a, gradient_b = finished(total, squares, width_a)
    input_gradient = in_order(
        jnp.concatenate(near, axis=1), jnp.concatenate(far, axis=1), axis=1
    )
    return input_gradient, gradient_a, gradient_b


def solution(mesh):
    ring, ctx = mesh.shape["dp"], mesh.shape["ctx"]
    split = Mesh(mesh.devices.reshape(ring, ctx // 2, 2), AXES)
    rows = P(AXES, None)
    placed = (rows,) * 5 + (P(),) * 6 + (rows,) * 2
    return jax.shard_map(
        on_device,
        mesh=split,
        in_specs=placed,
        out_specs=(rows, P(None, AXES), P(None, AXES)),
        check_vma=False,
    )
```
